32 devices in a mesh: expert: 8 (over z, x), shard: 4 (over y, core).
Axes of the slice: x: 2, y: 2, z: 4, core: 2. Of those that a mesh axis runs over, the one named last changes fastest.
Arguments:
- hidden_in: bfloat16 [8192, 1536], P(('expert', 'shard')), may hold values from -6 to 6
- segment_ids: int32 [8192], P('expert'), may hold values from 0 to 4, as said below
- routes: int32 [8192, 4], P(('expert', 'shard')), may hold values from 0 to 7, all different within a row; in each aligned block of 256 rows (0 to 255, 256 to 511, ...) at most 256 rows name the same one
- attn_gain: bfloat16 [1536], P('shard'), may hold values from 0.099609375 to 1.8984375
- moe_gain: bfloat16 [1536], P('shard'), may hold values from 0.099609375 to 1.8984375
- w_query: bfloat16 [1536, 1536], P('shard'), may hold values from -0.15625 to 0.15625
- w_key: bfloat16 [1536, 256], P('shard'), may hold values from -0.15625 to 0.15625
- w_value: bfloat16 [1536, 256], P('shard'), may hold values from -0.15625 to 0.15625
- w_out: bfloat16 [1536, 1536], P('shard'), may hold values from -1.25 to 1.25
- w_router: bfloat16 [1536, 8], P('shard'), may hold values from -0.078125 to 0.078125
- expert_gate: bfloat16 [8, 1536, 768], P('expert'), may hold values from -0.15625 to 0.15625
- expert_up: bfloat16 [8, 1536, 768], P('expert'), may hold values from -0.15625 to 0.15625
- expert_down: bfloat16 [8, 768, 1536], P('expert'), may hold values from -0.4375 to 0.4375
- out_grad: bfloat16 [8192, 1536], P(('expert', 'shard')), may hold values from -6 to 6
Outputs:
- layer_out: bfloat16 [8192, 1536], P(('expert', 'shard'))
- input_grad: float32 [8192, 1536], P(('expert', 'shard'))
- attn_gain_grad: float32 [1536], P('shard')
- moe_gain_grad: float32 [1536], P('shard')
- w_query_grad: float32 [1536, 1536], P('shard')
- w_key_grad: float32 [1536, 256], P('shard')
- w_value_grad: float32 [1536, 256], P('shard')
- w_out_grad: float32 [1536, 1536], P('shard')
- w_router_grad: float32 [1536, 8], P('shard')
- expert_gate_grad: float32 [8, 1536, 768], P('expert')
- expert_up_grad: float32 [8, 1536, 768], P('expert')
- expert_down_grad: float32 [8, 768, 1536], P('expert')
The draws below stay inside these ranges and needn't reach their ends.
Inputs may be any that keep to these rules, and one draw needn't show every extreme that they name: `segment_ids`: within each sequence of 1024 tokens the document numbers start at 0, never fall and step by one; every document has 64 tokens or more. `routes`: A token's 4 experts differ; among the tokens of one device no expert is named more than 256 times.
All inputs are finite; a program needn't handle non-finite values.
Results may differ from the reference program's by a relative error of at most 0.017.
Values may be sent and summed in bfloat16 or wider, within the bound.
No kernel may reach another device: no remote copies, remote signals or barrier semaphores. Data moves between devices by JAX's collectives and lax.ppermute only.
A program may use at most 192 MiB of HBM per device.

```python
import math
from functools import partial
import jax
import jax.numpy as jnp
import numpy as np
from jax import lax

D = 1536
HQ = 12
KVH = 2
HEAD = 128
F = 768
TOP = 4
TOK_DEV = 256
EXPERTS = 8
SEQ = 1024
TOKENS = 8192
QW = 1536
KW = 256
CAP = 256


def draw_segment_ids(key, part):
    key = jax.random.fold_in(key, 7)
    seq_count = TOKENS // SEQ
    streams = jax.random.split(key, 6)
    doc_unit = SEQ // 16
    head_len = jax.random.randint(streams[0], (seq_count,), 2 * doc_unit, 4 * doc_unit)
    tail_len = jax.random.randint(streams[1], (seq_count,), 2 * doc_unit, 4 * doc_unit)
    first_row = (jnp.arange(seq_count) == 0).astype(jnp.int32)
    head_split = jnp.maximum(jax.random.randint(streams[2], (seq_count,), 0, 2), first_row)
    tail_split = jnp.maximum(jax.random.randint(streams[3], (seq_count,), 0, 2), first_row)
    head_cut = jax.random.randint(streams[4], (seq_count,), doc_unit, head_len - doc_unit + 1)
    tail_cut = jax.random.randint(streams[5], (seq_count,), doc_unit, tail_len - doc_unit + 1)
    positions = jnp.arange(SEQ, dtype=jnp.int32)[None, :]
    tail_start = SEQ - tail_len
    numbers = (positions >= head_len[:, None]).astype(jnp.int32)
    numbers = numbers + (positions >= tail_start[:, None]).astype(jnp.int32)
    numbers = numbers + head_split[:, None] * (positions >= head_cut[:, None]).astype(jnp.int32)
    numbers = numbers + tail_split[:, None] * (positions >= (tail_start + tail_cut)[:, None]).astype(jnp.int32)
    return numbers.reshape(TOKENS).astype(jnp.int32)


def level_of(key, extent, shards, least, top_value):
    def one(dim, shards_of):
        draws = jax.random.uniform(jax.random.fold_in(jax.random.fold_in(key, 6), dim), (shards_of,), jnp.float32, least / len(shards), top_value / len(shards))
        return jnp.repeat(jnp.exp(draws), extent[dim] // shards_of).reshape((-1,) + (1,) * (len(extent) - dim - 1))

    loudness = one(*shards[0])
    for cut in shards[1:]:
        loudness = loudness * one(*cut)
    return loudness


def shared_out(stream_key, own, number, rows, number_of, top, reach, lean):
    order = jax.random.permutation(stream_key, number_of)
    heavy_load, ordinary = portions_of(number_of, rows * top, reach, lean, True), portions_of(number_of, rows * top, reach, lean, False)
    places = jnp.arange(number_of)

    def named(lengths, turn):
        used = int((lengths > 0).sum())
        fixed = max(1, used // 4)
        passed = fixed + (places - fixed + turn * (used - fixed)) % max(1, number_of - fixed)
        return jnp.zeros((number_of,), jnp.int32).at[order[jnp.where(places < fixed, places, passed)]].set(jnp.asarray(lengths, jnp.int32))

    lengths = jnp.where(number % 4 == 0, named(heavy_load, number // 4), named(ordinary, number - number // 4 - 1))
    mixed = jax.random.permutation(jax.random.fold_in(own, 3), number_of)
    donor, taker = mixed[0:number_of // 2 * 2:2], mixed[1:number_of // 2 * 2:2]
    room = jnp.minimum(lengths[donor] - 1, reach - lengths[taker]) // 2
    room = jnp.where((donor == order[0]) | (taker == order[0]) | (lengths[taker] == 0), 0, jnp.maximum(room, 0))
    passed = jax.random.randint(jax.random.fold_in(own, 4), (number_of // 2,), 0, 1 << 20) % (room + 1)
    lengths = lengths.at[donor].add(-passed).at[taker].add(passed)
    labels = jnp.searchsorted(jnp.cumsum(lengths), jnp.arange(rows * top), side="right").astype(jnp.int32)
    listing = labels.reshape(top, rows).T
    listing = listing[jax.random.permutation(jax.random.fold_in(own, 1), rows)]
    turn = jax.random.randint(jax.random.fold_in(own, 2), (rows, 1), 0, top)
    return jnp.take_along_axis(listing, (jnp.arange(top)[None, :] + turn) % top, axis=1)


def portions_of(number_of, total, most, skew, full):
    portions = [(1 << 20) // math.isqrt(standing ** skew) + 1 for standing in range(1, number_of + 1)]
    largest = most if full else min(most, max(-(-total // number_of), total * portions[0] // sum(portions)))
    least = 1 if total - largest >= number_of - 1 else 0
    holding, spare = [largest] + [least] * (number_of - 1), total - largest - least * (number_of - 1)
    while spare > 0:
        free = [i for i in range(1, number_of) if holding[i] < largest] or [i for i in range(1, number_of) if holding[i] < most]
        whole, left = sum([portions[i] for i in free]), spare
        for i in free:
            extra = min(most - holding[i], max(1, left * portions[i] // whole), spare)
            holding[i] = holding[i] + extra
            spare = spare - extra
    return np.array(holding)


def noise(rng, extent, spread, limit, cuts=(), kind=jnp.bfloat16):
    drawn = spread * jax.random.normal(rng, extent, jnp.float32)
    if cuts:
        drawn = drawn * level_of(rng, extent, cuts, -0.22, 0.18)
    return jnp.clip(drawn, -limit, limit).astype(kind)


def setup_inputs(seed: int = 0) -> dict:
    splits = jax.random.split(jax.random.key(seed), 15)
    hidden_in = noise(splits[0], (TOKENS, D), 1.0, 6.0, ((0, 32),))
    segment_ids = draw_segment_ids(jax.random.fold_in(splits[14], 71), 0)
    routes_keys = jax.random.split(jax.random.fold_in(splits[2], 1), TOKENS // TOK_DEV)
    routes_turns = jax.random.permutation(jax.random.fold_in(splits[2], 3), TOKENS // TOK_DEV)
    routes = jax.vmap(lambda own, number: shared_out(jax.random.fold_in(splits[2], 2), own, number, TOK_DEV, EXPERTS, TOP, CAP, 2))(routes_keys, routes_turns).reshape((TOKENS, TOP))
    attn_gain = jnp.clip(1.0 + 0.18 * jax.random.normal(splits[3], (D,), jnp.float32), 0.099609375, 1.8984375).astype(jnp.bfloat16)
    moe_gain = jnp.clip(1.0 + 0.18 * jax.random.normal(splits[4], (D,), jnp.float32), 0.099609375, 1.8984375).astype(jnp.bfloat16)
    w_query = noise(splits[5], (D, QW), D ** -0.5, 0.15625, ((0, 4),))
    w_key = noise(splits[6], (D, KW), D ** -0.5, 0.15625, ((0, 4),))
    w_value = noise(splits[7], (D, KW), D ** -0.5, 0.15625, ((0, 4),))
    w_out = noise(splits[8], (QW, D), (QW // 64) ** -0.5, 1.25, ((0, 4),))
    w_router = noise(splits[9], (D, EXPERTS), (4 * D) ** -0.5, 0.078125, ((0, 4),))
    expert_gate = noise(splits[10], (EXPERTS, D, F), D ** -0.5, 0.15625, ((0, 8),))
    expert_up = noise(splits[11], (EXPERTS, D, F), D ** -0.5, 0.15625, ((0, 8),))
    expert_down = noise(splits[12], (EXPERTS, F, D), (F // 4) ** -0.5, 0.4375, ((0, 8),))
    out_grad = noise(splits[13], (TOKENS, D), 1.0, 6.0, ((0, 32),))
    return {"hidden_in": hidden_in, "segment_ids": segment_ids, "routes": routes, "attn_gain": attn_gain, "moe_gain": moe_gain, "w_query": w_query, "w_key": w_key, "w_value": w_value, "w_out": w_out, "w_router": w_router, "expert_gate": expert_gate, "expert_up": expert_up, "expert_down": expert_down, "out_grad": out_grad}


EPSILON = 1e-06
ROPE_BASE = 10000.0
MASKED_SCORE = -1e+30
HIGHEST = lax.Precision.HIGHEST

@jax.custom_vjp
def low(v):
    return lax.optimization_barrier(v.astype(jnp.bfloat16)).astype(jnp.float32)

@jax.custom_vjp
def low_back(v):
    return v

def low_keep(v):
    return (low(v), None)

def low_pass(kept, grad):
    return (grad,)

def back_keep(v):
    return (v, None)

def back_low(kept, grad):
    return (low(grad),)
low.defvjp(low_keep, low_pass)
low_back.defvjp(back_keep, back_low)

def product(left, right):
    return jnp.dot(left, right, precision=HIGHEST)

def rms_norm(values, gain):
    factor = lax.rsqrt(lax.optimization_barrier(jnp.mean(values * values, -1, keepdims=True)) + EPSILON)
    return values * factor * gain

def rope_tables(positions, head_size):
    half_size = head_size // 2
    frequency = ROPE_BASE ** (-(jnp.arange(half_size, dtype=jnp.float32) * 2.0 / head_size))
    angles = positions.astype(jnp.float32)[:, None] * frequency[None, :]
    return (jnp.cos(angles), jnp.sin(angles))

def rotate(values, cosine_table, sine_table, head_size):
    rows_count = values.shape[0]
    shaped = values.reshape(rows_count, -1, head_size)
    half_size = head_size // 2
    first_half = shaped[..., :half_size]
    second_half = shaped[..., half_size:]
    cosine_part = cosine_table[:, None, :]
    sine_part = sine_table[:, None, :]
    turned = jnp.concatenate([first_half * cosine_part - second_half * sine_part, second_half * cosine_part + first_half * sine_part], -1)
    return turned.reshape(rows_count, -1)

def attend(pieces):
    queries, key_rows, value_rows, seg_rows = pieces
    groups = HQ // KVH
    query_heads = queries.reshape(SEQ, KVH, groups, HEAD)
    key_heads = key_rows.reshape(SEQ, KVH, HEAD)
    value_heads = value_rows.reshape(SEQ, KVH, HEAD)
    raw_scores = jnp.einsum('tkgd,skd->kgts', query_heads, key_heads, precision=HIGHEST)
    positions = jnp.arange(SEQ, dtype=jnp.int32)
    visible = (positions[:, None] >= positions[None, :]) & (seg_rows[:, None] == seg_rows[None, :])
    score_values = jnp.where(visible, low_back(raw_scores) * HEAD ** (-0.5), MASKED_SCORE)
    score_values = score_values - lax.optimization_barrier(jnp.max(score_values, -1, keepdims=True))
    exponent = jnp.exp(score_values)
    probabilities = exponent / lax.optimization_barrier(jnp.sum(exponent, -1, keepdims=True))
    attended = jnp.einsum('kgts,skd->tkgd', low(probabilities), value_heads, precision=HIGHEST)
    return attended.reshape(SEQ, HQ * HEAD)

def expert_block(gate_weights, up_weights, down_weights, pieces):
    copy_rows, expert_ids = pieces
    onehot = (expert_ids[:, None] == jnp.arange(EXPERTS, dtype=jnp.int32)[None, :]).astype(jnp.int32)
    before = jnp.cumsum(onehot, 0, dtype=jnp.int32) - onehot
    slot_id = expert_ids * CAP + lax.optimization_barrier(jnp.sum(before * onehot, 1, dtype=jnp.int32))
    source = jnp.zeros((EXPERTS * CAP,), jnp.int32).at[slot_id].set(jnp.arange(expert_ids.shape[0], dtype=jnp.int32))
    filled = jnp.zeros((EXPERTS * CAP,), jnp.float32).at[slot_id].set(1.0)
    buffer = (copy_rows[source] * filled[:, None]).reshape(EXPERTS, CAP, D)
    gate_pre = low_back(jnp.einsum('ecd,edf->ecf', buffer, gate_weights, precision=HIGHEST))
    up_pre = low_back(jnp.einsum('ecd,edf->ecf', buffer, up_weights, precision=HIGHEST))
    activation = low(gate_pre * jax.nn.sigmoid(gate_pre) * up_pre)
    result = low(low_back(jnp.einsum('ecf,efd->ecd', activation, down_weights, precision=HIGHEST)))
    return result.reshape(EXPERTS * CAP, D)[slot_id]

def layer_forward(params, inputs, seg_rows, route_ids):
    gain_attn, gain_moe, query_w, key_w, value_w, out_w, router_w, gate_w, up_w, down_w = params
    rows_count = inputs.shape[0]
    normed = low(rms_norm(inputs, gain_attn))
    positions = jnp.arange(rows_count, dtype=jnp.int32) % SEQ
    cosine_table, sine_table = rope_tables(positions, HEAD)
    queries = low(rotate(low_back(product(normed, query_w)), cosine_table, sine_table, HEAD))
    key_rows = low(rotate(low_back(product(normed, key_w)), cosine_table, sine_table, HEAD))
    value_rows = low(low_back(product(normed, value_w)))
    seq_count = rows_count // SEQ
    attended = lax.map(jax.checkpoint(attend), (queries.reshape(seq_count, SEQ, -1), key_rows.reshape(seq_count, SEQ, -1), value_rows.reshape(seq_count, SEQ, -1), seg_rows.reshape(seq_count, SEQ)))
    attended = low(low_back(attended.reshape(rows_count, -1)))
    mid_state = inputs + low_back(product(attended, out_w))
    normed_moe = low(rms_norm(mid_state, gain_moe))
    logits = product(normed_moe, router_w)
    onehot = (route_ids[:, :, None] == jnp.arange(EXPERTS, dtype=jnp.int32)[None, None, :]).astype(jnp.float32)
    chosen = lax.optimization_barrier(jnp.sum(onehot * logits[:, None, :], -1))
    chosen = chosen - lax.optimization_barrier(jnp.max(chosen, -1, keepdims=True))
    weights = jnp.exp(chosen)
    gate = weights / lax.optimization_barrier(jnp.sum(weights, -1, keepdims=True))
    copies = low_back(jnp.broadcast_to(normed_moe[:, None, :], (rows_count, TOP, D)))
    blocks = rows_count // TOK_DEV
    returned = lax.map(jax.checkpoint(partial(expert_block, gate_w, up_w, down_w)), (copies.reshape(blocks, TOK_DEV * TOP, D), route_ids.reshape(blocks, TOK_DEV * TOP)))
    returned = returned.reshape(rows_count, TOP, D)
    return mid_state + lax.optimization_barrier(jnp.sum(gate[:, :, None] * returned, 1))

def reference(hidden_in, segment_ids, routes, attn_gain, moe_gain, w_query, w_key, w_value, w_out, w_router, expert_gate, expert_up, expert_down, out_grad):
    params = tuple((member.astype(jnp.float32) for member in (attn_gain, moe_gain, w_query, w_key, w_value, w_out, w_router, expert_gate, expert_up, expert_down)))
    group_seqs = 4 if TOKENS // SEQ % 4 == 0 else 1
    span = group_seqs * SEQ
    group_count = TOKENS // span

    def group_step(totals, pieces):
        inputs, seg_rows, route_ids, cotangent = pieces
        result, pullback = jax.vjp(lambda weights_in, rows_in: layer_forward(weights_in, rows_in, seg_rows, route_ids), params, inputs)
        param_grads, input_grads = pullback(cotangent)
        totals = tuple((total + grad for total, grad in zip(totals, param_grads)))
        return (totals, (result, input_grads))
    zeros_init = tuple((jnp.zeros_like(member) for member in params))
    pieces = (hidden_in.astype(jnp.float32).reshape(group_count, span, D), segment_ids.reshape(group_count, span), routes.reshape(group_count, span, TOP), out_grad.astype(jnp.float32).reshape(group_count, span, D))
    sums, (outputs, input_grads) = lax.scan(group_step, zeros_init, pieces)
    return (outputs.reshape(TOKENS, D).astype(jnp.bfloat16), input_grads.reshape(TOKENS, D), sums[0], sums[1], sums[2], sums[3], sums[4], sums[5], sums[6], sums[7], sums[8], sums[9])
```

```python
import functools

import jax
import jax.numpy as jnp
from jax import lax
from jax.experimental import pallas as pl
from jax.experimental.pallas import tpu as pltpu
from jax.sharding import PartitionSpec as P

HQ = 12
KVH = 2
HEAD = 128


EPSILON = 1e-06
ROPE_BASE = 10000.0
MASKED_SCORE = -1e30
HIGHEST = lax.Precision.HIGHEST


def rope_tables(positions, head_size):
    half_size = head_size // 2
    frequency = ROPE_BASE ** (-(jnp.arange(half_size, dtype=jnp.float32) * 2.0 / head_size))
    angles = positions.astype(jnp.float32)[:, None] * frequency[None, :]
    return (jnp.cos(angles), jnp.sin(angles))


def rotate(values, cosine_table, sine_table, head_size):
    rows_count = values.shape[0]
    shaped = values.reshape(rows_count, -1, head_size)
    half_size = head_size // 2
    first_half = shaped[..., :half_size]
    second_half = shaped[..., half_size:]
    cosine_part = cosine_table[:, None, :]
    sine_part = sine_table[:, None, :]
    turned = jnp.concatenate(
        [
            first_half * cosine_part - second_half * sine_part,
            second_half * cosine_part + first_half * sine_part,
        ],
        -1,
    )
    return turned.reshape(rows_count, -1)


def norm_forward(values, gain):
    factor = lax.rsqrt(jnp.mean(values * values, -1, keepdims=True) + EPSILON)
    unit_rows = values * factor
    return (unit_rows, factor, (unit_rows * gain).astype(jnp.bfloat16))


def norm_backward(grad_rows, unit_rows, factor, gain):
    gain_grad = jnp.sum(grad_rows * unit_rows, 0)
    scaled_grad = grad_rows * gain
    return (
        factor * (scaled_grad - unit_rows * jnp.mean(scaled_grad * unit_rows, -1, keepdims=True)),
        gain_grad,
    )


def score_block(query_heads, key_heads, visible, score_scale):
    raw_scores = jnp.einsum(
        "tkgd,skd->kgts", query_heads, key_heads, preferred_element_type=jnp.float32
    )
    return jnp.where(visible, raw_scores * score_scale, MASKED_SCORE)


def on_device_routed(
    hidden_in,
    segment_ids,
    routes,
    attn_gain,
    moe_gain,
    w_query,
    w_key,
    w_value,
    w_out,
    w_router,
    expert_gate,
    expert_up,
    expert_down,
    out_grad,
):
    tok_rows = hidden_in.shape[0]
    top_count = routes.shape[1]
    experts = w_router.shape[1]
    capacity = tok_rows * top_count * 2 // experts
    groups = HQ // KVH
    score_scale = HEAD ** (-0.5)
    shard_index = lax.axis_index("shard")
    n_expert = lax.axis_size("expert")
    local_experts = expert_gate.shape[0]
    gain_attn, gain_moe, query_w, key_w, value_w, out_w, router_w = (
        lax.all_gather(attn_gain, "shard", axis=0, tiled=True),
        lax.all_gather(moe_gain, "shard", axis=0, tiled=True),
        lax.all_gather(w_query, "shard", axis=0, tiled=True),
        lax.all_gather(w_key, "shard", axis=0, tiled=True),
        lax.all_gather(w_value, "shard", axis=0, tiled=True),
        lax.all_gather(w_out, "shard", axis=0, tiled=True),
        lax.all_gather(w_router, "shard", axis=0, tiled=True),
    )
    gain_attn = gain_attn.astype(jnp.float32)
    gain_moe = gain_moe.astype(jnp.float32)
    inputs = hidden_in.astype(jnp.float32)
    unit_attn, factor_attn, normed = norm_forward(inputs, gain_attn)
    q_pre = jnp.dot(normed, query_w, preferred_element_type=jnp.float32)
    k_pre = jnp.dot(normed, key_w, preferred_element_type=jnp.float32)
    value_rows = jnp.dot(normed, value_w, preferred_element_type=jnp.float32).astype(jnp.bfloat16)
    positions = shard_index * tok_rows + jnp.arange(tok_rows, dtype=jnp.int32)
    cosine_table, sine_table = rope_tables(positions, HEAD)
    queries = rotate(q_pre, cosine_table, sine_table, HEAD).astype(jnp.bfloat16)
    key_local = rotate(k_pre, cosine_table, sine_table, HEAD).astype(jnp.bfloat16)
    key_rows, value_all = (
        lax.all_gather(key_local, "shard", axis=0, tiled=True),
        lax.all_gather(value_rows, "shard", axis=0, tiled=True),
    )
    seq_len = key_rows.shape[0]
    query_heads = queries.reshape(tok_rows, KVH, groups, HEAD)
    key_heads = key_rows.reshape(seq_len, KVH, HEAD)
    value_heads = value_all.reshape(seq_len, KVH, HEAD)
    seg_local = lax.dynamic_slice_in_dim(segment_ids, shard_index * tok_rows, tok_rows)
    visible = (positions[:, None] >= jnp.arange(seq_len, dtype=jnp.int32)[None, :]) & (
        seg_local[:, None] == segment_ids[None, :]
    )
    score_values = score_block(query_heads, key_heads, visible, score_scale)
    top_score = jnp.max(score_values, -1, keepdims=True)
    exponent = jnp.exp(score_values - top_score)
    denominators = jnp.sum(exponent, -1, keepdims=True)
    probabilities = exponent / denominators
    log_total = top_score + jnp.log(denominators)
    attended = (
        jnp.einsum(
            "kgts,skd->tkgd",
            probabilities.astype(jnp.bfloat16),
            value_heads,
            preferred_element_type=jnp.float32,
        )
        .reshape(tok_rows, -1)
        .astype(jnp.bfloat16)
    )
    mid_state = inputs + jnp.dot(attended, out_w, preferred_element_type=jnp.float32)
    unit_moe, factor_moe, normed_moe = norm_forward(mid_state, gain_moe)
    logits = jnp.dot(normed_moe, router_w, preferred_element_type=jnp.float32)
    onehot = (routes[:, :, None] == jnp.arange(experts, dtype=jnp.int32)[None, None, :]).astype(
        jnp.float32
    )
    chosen = jnp.sum(onehot * logits[:, None, :], -1)
    chosen = chosen - jnp.max(chosen, -1, keepdims=True)
    weights = jnp.exp(chosen)
    gate = weights / jnp.sum(weights, -1, keepdims=True)
    flat_routes = routes.reshape(-1)
    route_hot = (flat_routes[:, None] == jnp.arange(experts, dtype=jnp.int32)[None, :]).astype(
        jnp.int32
    )
    before = jnp.cumsum(route_hot, 0, dtype=jnp.int32) - route_hot
    slot_id = flat_routes * capacity + jnp.sum(before * route_hot, 1, dtype=jnp.int32)
    source = (
        jnp.zeros((experts * capacity,), jnp.int32)
        .at[slot_id]
        .set(jnp.arange(tok_rows * top_count, dtype=jnp.int32))
    )
    filled = jnp.zeros((experts * capacity,), jnp.bool_).at[slot_id].set(True)
    outgoing = jnp.where(filled[:, None], jnp.take(normed_moe, source // top_count, axis=0), 0)
    outgoing = outgoing.reshape(experts, capacity, -1)
    arrived = lax.all_to_all(outgoing, "expert", split_axis=0, concat_axis=0, tiled=True)
    item_count = arrived.shape[1]
    shaped = arrived.reshape(n_expert, local_experts, item_count, -1)
    gate_pre = jnp.einsum("nlcd,ldf->nlcf", shaped, expert_gate, preferred_element_type=jnp.float32)
    up_pre = jnp.einsum("nlcd,ldf->nlcf", shaped, expert_up, preferred_element_type=jnp.float32)
    hidden_rows = (gate_pre * jax.nn.sigmoid(gate_pre) * up_pre).astype(jnp.bfloat16)
    result = jnp.einsum(
        "nlcf,lfd->nlcd", hidden_rows, expert_down, preferred_element_type=jnp.float32
    )
    result = result.astype(jnp.bfloat16).reshape(arrived.shape)
    returned = lax.all_to_all(result, "expert", split_axis=0, concat_axis=0, tiled=True)
    outcome = (
        returned,
        arrived,
        gate_pre.reshape(n_expert * local_experts, item_count, -1),
        up_pre.reshape(n_expert * local_experts, item_count, -1),
        hidden_rows.reshape(n_expert * local_experts, item_count, -1),
    )
    returned_rows = jnp.take(outcome[0].reshape(experts * capacity, -1), slot_id, axis=0).reshape(
        tok_rows, top_count, -1
    )
    mixed = mid_state + jnp.sum(gate[:, :, None] * returned_rows, 1)
    layer_out = mixed.astype(jnp.bfloat16)
    grad_out = out_grad.astype(jnp.float32)
    gate_grad = jnp.sum(returned_rows * grad_out[:, None, :], -1)
    gate_slots = jnp.take(gate.reshape(-1), source, axis=0)
    d_send = jnp.where(
        filled[:, None], jnp.take(grad_out, source // top_count, axis=0) * gate_slots[:, None], 0.0
    )
    d_send = d_send.astype(jnp.bfloat16).reshape(experts, capacity, -1)
    d_arrived = lax.all_to_all(d_send, "expert", split_axis=0, concat_axis=0, tiled=True)
    d_shaped = d_arrived.reshape(n_expert, local_experts, capacity, -1)
    arrived_rows = outcome[1].reshape(n_expert, local_experts, capacity, -1)
    gate_pre = outcome[2].reshape(n_expert, local_experts, capacity, -1)
    up_pre = outcome[3].reshape(n_expert, local_experts, capacity, -1)
    hidden_rows = outcome[4].reshape(n_expert, local_experts, capacity, -1)
    sigmoid_gate = jax.nn.sigmoid(gate_pre)
    d_hidden = jnp.einsum(
        "nlcd,lfd->nlcf", d_shaped, expert_down, preferred_element_type=jnp.float32
    )
    down_grad = jnp.einsum(
        "nlcf,nlcd->lfd", hidden_rows, d_shaped, preferred_element_type=jnp.float32
    )
    d_gate = (d_hidden * up_pre * sigmoid_gate * (1.0 + gate_pre * (1.0 - sigmoid_gate))).astype(
        jnp.bfloat16
    )
    d_up = (d_hidden * gate_pre * sigmoid_gate).astype(jnp.bfloat16)
    gate_w_grad = jnp.einsum(
        "nlcd,nlcf->ldf", arrived_rows, d_gate, preferred_element_type=jnp.float32
    )
    up_w_grad = jnp.einsum("nlcd,nlcf->ldf", arrived_rows, d_up, preferred_element_type=jnp.float32)
    d_rows = jnp.einsum("nlcf,ldf->nlcd", d_gate, expert_gate, preferred_element_type=jnp.float32)
    d_rows = d_rows + jnp.einsum(
        "nlcf,ldf->nlcd", d_up, expert_up, preferred_element_type=jnp.float32
    )
    d_rows = d_rows.astype(jnp.bfloat16).reshape(experts, capacity, -1)
    d_returned = lax.all_to_all(d_rows, "expert", split_axis=0, concat_axis=0, tiled=True)
    expert_sums = (
        lax.psum(gate_w_grad.astype(jnp.bfloat16), "shard").astype(jnp.float32),
        lax.psum(up_w_grad.astype(jnp.bfloat16), "shard").astype(jnp.float32),
        lax.psum(down_grad.astype(jnp.bfloat16), "shard").astype(jnp.float32),
    )
    d_copies = jnp.take(d_returned.reshape(experts * capacity, -1), slot_id, axis=0).reshape(
        tok_rows, top_count, -1
    )
    d_normed_moe = jnp.sum(d_copies, 1, dtype=jnp.float32)
    d_chosen = gate * (gate_grad - jnp.sum(gate * gate_grad, -1, keepdims=True))
    d_logits = jnp.sum(onehot * d_chosen[:, :, None], 1)
    router_f32 = router_w.astype(jnp.float32)
    d_normed_moe = d_normed_moe + jnp.dot(d_logits, router_f32.T, precision=HIGHEST)
    router_grad = jnp.dot(normed_moe.astype(jnp.float32).T, d_logits, precision=HIGHEST)
    d_mid_norm, gain_moe_grad = norm_backward(d_normed_moe, unit_moe, factor_moe, gain_moe)
    d_mid = grad_out + d_mid_norm
    d_branch = d_mid.astype(jnp.bfloat16)
    out_w_grad = jnp.dot(attended.T, d_branch, preferred_element_type=jnp.float32)
    d_attended = jnp.dot(d_branch, out_w.T, preferred_element_type=jnp.float32).astype(jnp.bfloat16)
    d_attended = d_attended.reshape(tok_rows, KVH, groups, HEAD)
    score_again = score_block(query_heads, key_heads, visible, score_scale)
    prob_again = jnp.exp(score_again - log_total)
    d_probs = jnp.einsum(
        "tkgd,skd->kgts", d_attended, value_heads, preferred_element_type=jnp.float32
    )
    d_scores = (
        prob_again * (d_probs - jnp.sum(prob_again * d_probs, -1, keepdims=True)) * score_scale
    )
    d_scores = d_scores.astype(jnp.bfloat16)
    d_query = jnp.einsum(
        "kgts,skd->tkgd", d_scores, key_heads, preferred_element_type=jnp.float32
    ).reshape(tok_rows, -1)
    d_key_part = jnp.einsum(
        "kgts,tkgd->skd", d_scores, query_heads, preferred_element_type=jnp.float32
    ).reshape(seq_len, -1)
    d_value_part = jnp.einsum(
        "kgts,tkgd->skd",
        prob_again.astype(jnp.bfloat16),
        d_attended,
        preferred_element_type=jnp.float32,
    ).reshape(seq_len, -1)
    d_keys, d_values = (
        lax.psum_scatter(
            d_key_part.astype(jnp.bfloat16), "shard", scatter_dimension=0, tiled=True
        ).astype(jnp.float32),
        lax.psum_scatter(
            d_value_part.astype(jnp.bfloat16), "shard", scatter_dimension=0, tiled=True
        ).astype(jnp.float32),
    )
    d_q_pre = rotate(d_query, cosine_table, -sine_table, HEAD).astype(jnp.bfloat16)
    d_k_pre = rotate(d_keys, cosine_table, -sine_table, HEAD).astype(jnp.bfloat16)
    d_v_pre = d_values.astype(jnp.bfloat16)
    query_grad = jnp.dot(normed.T, d_q_pre, preferred_element_type=jnp.float32)
    key_grad = jnp.dot(normed.T, d_k_pre, preferred_element_type=jnp.float32)
    value_grad = jnp.dot(normed.T, d_v_pre, preferred_element_type=jnp.float32)
    d_normed = jnp.dot(d_q_pre, query_w.T, preferred_element_type=jnp.float32)
    d_normed = d_normed + jnp.dot(d_k_pre, key_w.T, preferred_element_type=jnp.float32)
    d_normed = d_normed + jnp.dot(d_v_pre, value_w.T, preferred_element_type=jnp.float32)
    d_input_norm, gain_attn_grad = norm_backward(d_normed, unit_attn, factor_attn, gain_attn)
    input_grad = d_mid + d_input_norm
    partial_sums = (
        gain_attn_grad,
        gain_moe_grad,
        query_grad,
        key_grad,
        value_grad,
        out_w_grad,
        router_grad,
    )
    summed = lax.psum(
        (
            partial_sums[0],
            partial_sums[1],
            partial_sums[2],
            partial_sums[3],
            partial_sums[4],
            partial_sums[5],
            partial_sums[6],
        ),
        ("expert", "shard"),
    )
    n_shard = lax.axis_size("shard")
    owned_grads = tuple(
        (
            lax.dynamic_slice_in_dim(
                member, shard_index * (member.shape[0] // n_shard), member.shape[0] // n_shard, 0
            )
            for member in summed
        )
    )
    return (
        layer_out,
        input_grad,
        owned_grads[0],
        owned_grads[1],
        owned_grads[2],
        owned_grads[3],
        owned_grads[4],
        owned_grads[5],
        owned_grads[6],
        expert_sums[0],
        expert_sums[1],
        expert_sums[2],
    )


AXES = ("expert", "shard")
N_EXPERT = 8
N_SHARD = 4
LANES = 128
MEBIBYTE = 1 << 20
BF16 = jnp.bfloat16
F32 = jnp.float32


def swap(values, expert_bits, shard_bits):
    pairs = [
        (e * N_SHARD + s, (e ^ expert_bits) * N_SHARD + (s ^ shard_bits))
        for e in range(N_EXPERT)
        for s in range(N_SHARD)
    ]
    return lax.ppermute(values, AXES, pairs)


def next_plane(values):
    pairs = [
        (e * N_SHARD + s, ((e + 2) % N_EXPERT) * N_SHARD + s)
        for e in range(N_EXPERT)
        for s in range(N_SHARD)
    ]
    return lax.ppermute(values, AXES, pairs)


def gather_shards(values):
    other_core = swap(values, 0, 1)
    other_y = swap(values, 0, 2)
    return [values, other_core, other_y, swap(other_y, 0, 1)]


def xor_blocks(blocks, index):
    odd = (index & 1) == 1
    high = (index & 2) == 2
    once = [jnp.where(odd, blocks[j ^ 1], blocks[j]) for j in range(4)]
    return [jnp.where(high, once[j ^ 2], once[j]) for j in range(4)]


def rejoin(mine, partner, low_first):
    return jnp.where(
        low_first,
        jnp.concatenate([mine, partner], 0),
        jnp.concatenate([partner, mine], 0),
    )


def dot_nn(left, right):
    return lax.dot_general(left, right, (((1,), (0,)), ((), ())), preferred_element_type=F32)


def dot_nt(left, right):
    return lax.dot_general(left, right, (((1,), (1,)), ((), ())), preferred_element_type=F32)


def dot_tn(left, right):
    return lax.dot_general(left, right, (((0,), (0,)), ((), ())), preferred_element_type=F32)


def turn(values, cosine, sine):
    return values * cosine + pltpu.roll(values, HEAD // 2, 1) * sine


def attention_forward_body(
    where_ref, h1_ref, w0, w1, w2, w3, key_ref, value_ref, cos_ref, sin_ref, segq_ref, segk_ref,
    query_out, prob_out, attended_out, bias_ref,
):
    rows, seq_len = bias_ref.shape

    @pl.when(pl.program_id(0) == 0)
    def _():
        base = where_ref[0] * rows
        query_pos = base + lax.broadcasted_iota(jnp.int32, (rows, seq_len), 0)
        key_pos = lax.broadcasted_iota(jnp.int32, (rows, seq_len), 1)
        visible = (query_pos >= key_pos) & (segq_ref[...] == segk_ref[...])
        bias_ref[...] = jnp.where(visible, 0.0, MASKED_SCORE)

    depth = w0.shape[0]
    pre = dot_nn(h1_ref[:, :depth], w0[...])
    for j, weight in enumerate((w1, w2, w3)):
        pre = pre + dot_nn(h1_ref[:, (j + 1) * depth : (j + 2) * depth], weight[...])
    for h in range(pre.shape[1] // HEAD):
        cols = slice(h * HEAD, (h + 1) * HEAD)
        query = turn(pre[:, cols], cos_ref[...], sin_ref[...]).astype(BF16)
        query_out[:, cols] = query
        scores = dot_nt(query, key_ref[...]) * HEAD ** (-0.5) + bias_ref[...]
        exponent = jnp.exp(scores - jnp.max(scores, -1, keepdims=True))
        total = jnp.sum(exponent, -1, keepdims=True)
        probs = (exponent * (1.0 / total)).astype(BF16)
        prob_out[h] = probs
        attended_out[:, cols] = dot_nn(probs, value_ref[...]).astype(BF16)


def attention_forward(where, h1_rel, w_query, keys_values, cosine, sine, seg_query, seg_key):
    rows, width = h1_rel.shape
    seq_len = keys_values.shape[0]
    cols = width // N_SHARD
    heads = cols // HEAD

    def whole(shape):
        return pl.BlockSpec(shape, lambda j, w: (0,) * len(shape))

    weight = pl.BlockSpec((cols, cols), lambda j, w: (0, w[0] ^ j))
    part = pl.BlockSpec((rows, cols), lambda j, w: (0, j))
    return pl.pallas_call(
        attention_forward_body,
        grid_spec=pltpu.PrefetchScalarGridSpec(
            num_scalar_prefetch=1,
            grid=(N_SHARD,),
            in_specs=[
                whole((rows, width)), weight, weight, weight, weight,
                pl.BlockSpec((seq_len, HEAD), lambda j, w: (0, (w[0] ^ j) // 2)),
                pl.BlockSpec((seq_len, HEAD), lambda j, w: (0, KVH + (w[0] ^ j) // 2)),
                whole((rows, HEAD)), whole((rows, HEAD)), whole((rows, 1)), whole((1, seq_len)),
            ],
            out_specs=[part, pl.BlockSpec((heads, rows, seq_len), lambda j, w: (j, 0, 0)), part],
            scratch_shapes=[pltpu.VMEM((rows, seq_len), F32)],
        ),
        out_shape=[
            jax.ShapeDtypeStruct((rows, width), BF16),
            jax.ShapeDtypeStruct((HQ, rows, seq_len), BF16),
            jax.ShapeDtypeStruct((rows, width), BF16),
        ],
        compiler_params=pltpu.CompilerParams(vmem_limit_bytes=40 * MEBIBYTE),
        cost_estimate=pl.CostEstimate(flops=5 * 10**9, bytes_accessed=2 * 10**7, transcendentals=3 * 10**6),
        name="attention_forward",
    )(where, h1_rel, *w_query, keys_values, keys_values, cosine, sine, seg_query, seg_key)


def attention_backward_body(
    where_ref, branch_ref, out0, out1, out2, out3, attended_ref, query_ref, prob_ref, key_ref, value_ref,
    w0, w1, w2, w3, cos_ref, sin_ref,
    dq_out, dk_out, dv_out, dh_out, dh_acc, dk_acc, dv_acc, da_ref, stack_ref,
):
    step = pl.program_id(0)
    depth = w0.shape[0]
    rows = branch_ref.shape[0]

    for j, weight in enumerate((out0, out1, out2, out3)):

        @pl.when(step == j)
        def _(weight=weight):
            da_ref[...] = dot_nt(branch_ref[...], weight[...]).astype(BF16)

    @pl.when(step % 2 == 0)
    def _():
        dk_acc[...] = jnp.zeros_like(dk_acc)
        dv_acc[...] = jnp.zeros_like(dv_acc)

    @pl.when(step == 0)
    def _():
        dh_acc[...] = jnp.zeros_like(dh_acc)

    d_pre = []
    for h in range(depth // HEAD):
        cols = slice(h * HEAD, (h + 1) * HEAD)
        d_att = da_ref[:, cols]
        probs = prob_ref[h]
        delta = jnp.sum(d_att.astype(F32) * attended_ref[:, cols].astype(F32), -1, keepdims=True)
        d_probs = dot_nt(d_att, value_ref[...])
        d_scores = (probs.astype(F32) * ((d_probs - delta) * HEAD ** (-0.5))).astype(BF16)
        stack_ref[h * rows : (h + 1) * rows, :] = d_scores
        d_query = dot_nn(d_scores, key_ref[...])
        d_pre.append(turn(d_query, cos_ref[...], -sin_ref[...]).astype(BF16))
        dk_acc[...] += dot_tn(query_ref[:, cols], d_scores)
        dv_acc[...] += dot_tn(d_att, probs)
    d_pre = jnp.concatenate(d_pre, 1)
    dq_out[...] = d_pre
    for j, weight in enumerate((w0, w1, w2, w3)):
        dh_acc[:, j * depth : (j + 1) * depth] += dot_nt(d_pre, weight[...])

    @pl.when(step % 2 == 1)
    def _():
        dk_out[...] = dk_acc[...].T.astype(BF16)
        dv_out[...] = dv_acc[...].T.astype(BF16)

    @pl.when(step == N_SHARD - 1)
    def _():
        dh_out[...] = dh_acc[...]


def attention_backward(where, branch, w_out, attended, queries, probs, keys_values, w_query, cosine, sine):
    rows, width = branch.shape
    seq_len = keys_values.shape[0]
    cols = width // N_SHARD
    heads = cols // HEAD

    def whole(shape):
        return pl.BlockSpec(shape, lambda j, w: (0,) * len(shape))

    weight = pl.BlockSpec((cols, cols), lambda j, w: (0, w[0] ^ j))
    part = pl.BlockSpec((rows, cols), lambda j, w: (0, j))
    head_part = pl.BlockSpec((seq_len, HEAD), lambda j, w: (0, (w[0] ^ j) // 2))
    return pl.pallas_call(
        attention_backward_body,
        grid_spec=pltpu.PrefetchScalarGridSpec(
            num_scalar_prefetch=1,
            grid=(N_SHARD,),
            in_specs=[whole((rows, width))] + [whole((cols, width))] * 4 + [
                part, part, pl.BlockSpec((heads, rows, seq_len), lambda j, w: (j, 0, 0)),
                head_part,
                pl.BlockSpec((seq_len, HEAD), lambda j, w: (0, KVH + (w[0] ^ j) // 2)),
                weight, weight, weight, weight, whole((rows, HEAD)), whole((rows, HEAD)),
            ],
            out_specs=[
                pl.BlockSpec((rows, cols), lambda j, w: (0, w[0] ^ j)),
                head_part, head_part, whole((rows, width)),
            ],
            scratch_shapes=[
                pltpu.VMEM((rows, width), F32),
                pltpu.VMEM((HEAD, seq_len), F32),
                pltpu.VMEM((HEAD, seq_len), F32),
                pltpu.VMEM((rows, cols), BF16),
                pltpu.VMEM((heads * rows, seq_len), BF16),
            ],
        ),
        out_shape=[
            jax.ShapeDtypeStruct((rows, width), BF16),
            jax.ShapeDtypeStruct((seq_len, KVH * HEAD), BF16),
            jax.ShapeDtypeStruct((seq_len, KVH * HEAD), BF16),
            jax.ShapeDtypeStruct((rows, width), F32),
        ],
        compiler_params=pltpu.CompilerParams(vmem_limit_bytes=48 * MEBIBYTE),
        cost_estimate=pl.CostEstimate(flops=8 * 10**9, bytes_accessed=3 * 10**7, transcendentals=0),
        name="attention_backward",
    )(where, branch, *w_out, attended, queries, probs, keys_values, keys_values, *w_query, cosine, sine)


def expert_body(
    where_ref, h2_ref, dy_ref, router_ref, gate_own, up_own, down_own, gate_far, up_far, down_far,
    message_out, mixed_out, da_out, db_out, act_out, gates_ref, dh_acc, y_acc, gg_acc,
):
    e = pl.program_id(0)
    f = pl.program_id(1)
    rows, width = h2_ref.shape
    lane = lax.broadcasted_iota(jnp.int32, (rows, LANES), 1)

    @pl.when((e == 0) & (f == 0))
    def _():
        named = dy_ref[:, width:].astype(F32) > 0.5
        logits = jnp.where(named, dot_nn(h2_ref[...], router_ref[...]), MASKED_SCORE)
        top = jnp.max(logits, -1, keepdims=True)
        weights = jnp.where(named, jnp.exp(logits - top), 0.0)
        gates_ref[...] = weights / jnp.sum(weights, -1, keepdims=True)
        dh_acc[...] = jnp.zeros_like(dh_acc)
        y_acc[...] = jnp.zeros_like(y_acc)
        gg_acc[...] = jnp.zeros_like(gg_acc)

    here = lane == (where_ref[0] ^ e)

    def work(gate_ref, up_ref, down_ref):
        gate = jnp.sum(jnp.where(here, gates_ref[...], 0.0), -1, keepdims=True)
        h2 = h2_ref[...]
        a = dot_nn(h2, gate_ref[...])
        b = dot_nn(h2, up_ref[...])
        d_plain = dot_nt(dy_ref[:, :width], down_ref[...])
        sigmoid = 1.0 / (1.0 + jnp.exp(-a))
        silu = a * sigmoid
        act = silu * b
        gate_grad = jnp.sum(act * d_plain, -1, keepdims=True)
        gg_acc[...] += jnp.where(here, gate_grad, 0.0)
        d_act = d_plain * gate
        d_a = (d_act * b * (sigmoid + silu * (1.0 - sigmoid))).astype(BF16)
        d_b = (d_act * silu).astype(BF16)
        scaled = (act * gate).astype(BF16)
        da_out[...] = d_a
        db_out[...] = d_b
        act_out[...] = scaled
        dh_acc[...] += dot_nt(d_a, gate_ref[...]) + dot_nt(d_b, up_ref[...])
        y_acc[...] += dot_nn(scaled, down_ref[...])

    @pl.when(e == 0)
    def _():
        work(gate_own, up_own, down_own)

    @pl.when(e == 1)
    def _():
        work(gate_far, up_far, down_far)

    @pl.when((e == pl.num_programs(0) - 1) & (f == pl.num_programs(1) - 1))
    def _():
        message_out[:, :width] = dh_acc[...].astype(BF16)
        high = gg_acc[...].astype(BF16).astype(F32)
        low = pltpu.roll(gg_acc[...] - high, N_EXPERT, 1)
        message_out[:, width:] = (high + low).astype(BF16)
        mixed_out[...] = y_acc[...].astype(BF16)


def expert_block(where, h2, dy_routes, router, own, far):
    rows, width = h2.shape
    hidden = own[0].shape[1]
    chunk = 256
    chunks = hidden // chunk

    def whole(shape):
        return pl.BlockSpec(shape, lambda e, f, w: (0,) * len(shape))

    own_step = lambda e, f: jnp.where(e == 0, f, chunks - 1)
    far_step = lambda e, f: jnp.where(e == 0, 0, f)
    own_in = pl.BlockSpec((width, chunk), lambda e, f, w: (0, own_step(e, f)))
    own_down = pl.BlockSpec((chunk, width), lambda e, f, w: (own_step(e, f), 0))
    far_in = pl.BlockSpec((width, chunk), lambda e, f, w: (0, far_step(e, f)))
    far_down = pl.BlockSpec((chunk, width), lambda e, f, w: (far_step(e, f), 0))
    part = pl.BlockSpec((rows, chunk), lambda e, f, w: (0, e * chunks + f))
    return pl.pallas_call(
        expert_body,
        grid_spec=pltpu.PrefetchScalarGridSpec(
            num_scalar_prefetch=1,
            grid=(2, chunks),
            in_specs=[
                whole((rows, width)), whole(dy_routes.shape), whole(router.shape),
                own_in, own_in, own_down, far_in, far_in, far_down,
            ],
            out_specs=[whole((rows, width + LANES)), whole((rows, width)), part, part, part],
            scratch_shapes=[
                pltpu.VMEM((rows, LANES), F32),
                pltpu.VMEM((rows, width), F32),
                pltpu.VMEM((rows, width), F32),
                pltpu.VMEM((rows, LANES), F32),
            ],
        ),
        out_shape=[
            jax.ShapeDtypeStruct((rows, width + LANES), BF16),
            jax.ShapeDtypeStruct((rows, width), BF16),
            jax.ShapeDtypeStruct((rows, 2 * hidden), BF16),
            jax.ShapeDtypeStruct((rows, 2 * hidden), BF16),
            jax.ShapeDtypeStruct((rows, 2 * hidden), BF16),
        ],
        compiler_params=pltpu.CompilerParams(vmem_limit_bytes=40 * MEBIBYTE),
        cost_estimate=pl.CostEstimate(flops=8 * 10**9, bytes_accessed=2 * 10**7, transcendentals=4 * 10**5),
        name="expert_block",
    )(where, h2, dy_routes, router, *own, *far)


def summed_products_body(where_ref, *refs, parts, sets):
    lefts = refs[:parts]
    rights = refs[parts : parts * (1 + sets)]
    outs = refs[parts * (1 + sets) :]
    for k in range(sets):
        total = dot_tn(lefts[0][...], rights[k * parts][...])
        for j in range(1, parts):
            total = total + dot_tn(lefts[j][...], rights[k * parts + j][...])
        out = outs[k]
        if len(out.shape) == 3:
            pieces = out.shape[0]
            deep = out.shape[1]
            for piece in range(pieces):
                out[where_ref[0] ^ piece] = total[piece * deep : (piece + 1) * deep].astype(out.dtype)
        else:
            out[...] = total.astype(out.dtype)


def summed_products(where, lefts, right_sets, grid, left_spec, right_spec, out_spec, out_shape, name):
    parts = len(lefts)
    sets = len(right_sets)
    return pl.pallas_call(
        functools.partial(summed_products_body, parts=parts, sets=sets),
        grid_spec=pltpu.PrefetchScalarGridSpec(
            num_scalar_prefetch=1,
            grid=grid,
            in_specs=[left_spec] * parts + [right_spec] * (parts * sets),
            out_specs=[out_spec] * sets,
        ),
        out_shape=[jax.ShapeDtypeStruct(out_shape, BF16)] * sets,
        compiler_params=pltpu.CompilerParams(vmem_limit_bytes=48 * MEBIBYTE),
        cost_estimate=pl.CostEstimate(flops=3 * 10**9, bytes_accessed=10**7, transcendentals=0),
        name=name,
    )(where, *lefts, *[member for members in right_sets for member in members])


def sum_over_planes(pieces):
    shape = pieces.shape[1:]
    low = pieces.reshape((4, 2) + shape)
    kept = low[:, 0].astype(F32) + swap(low[:, 1], 1, 0).astype(F32)
    kept = kept.astype(BF16).reshape((2, 2) + shape)
    kept = kept[:, 0].astype(F32) + swap(kept[:, 1], 2, 0).astype(F32)
    kept = kept.astype(BF16)
    own = (kept[0].astype(F32) + swap(kept[1], 4, 0).astype(F32)).astype(BF16)
    two = jnp.stack([own, swap(own, 4, 0)])
    four = jnp.stack([two, swap(two, 2, 0)], 1).reshape((4,) + shape)
    return four, swap(four, 1, 0)


def reorder_body(where_ref, even_ref, odd_ref, out_ref):
    place = where_ref[0] ^ pl.program_id(0)

    @pl.when(place % 2 == 0)
    def _():
        out_ref[...] = even_ref[...].astype(F32)

    @pl.when(place % 2 == 1)
    def _():
        out_ref[...] = odd_ref[...].astype(F32)


def reorder(where, even, odd):
    shape = even.shape[1:]
    spec = pl.BlockSpec((1,) + shape, lambda b, w: ((w[0] ^ b) // 2, 0, 0))
    return pl.pallas_call(
        reorder_body,
        grid_spec=pltpu.PrefetchScalarGridSpec(
            num_scalar_prefetch=1,
            grid=(N_EXPERT,),
            in_specs=[spec, spec],
            out_specs=pl.BlockSpec((1,) + shape, lambda b, w: (b, 0, 0)),
        ),
        out_shape=jax.ShapeDtypeStruct((N_EXPERT,) + shape, F32),
        name="reorder",
    )(where, even, odd).reshape(N_EXPERT * shape[0], shape[1])


def fetch_far(mine, core):
    half = mine.shape[0] // 2
    part = swap(lax.dynamic_slice_in_dim(mine, core * half, half, 0), 1, 0)
    return rejoin(part, swap(part, 0, 1), core == 0)


def expert_weight_sums(send, keep, axis, core):
    received = swap(send, 0, 1)
    half = send.shape[axis] // 2
    cut = lambda a, i: lax.slice_in_dim(a, i * half, (i + 1) * half, axis=axis).astype(F32)
    for_far = (cut(keep, 1) + cut(received, 1)).astype(BF16)
    total = cut(keep, 0) + cut(received, 0) + swap(for_far, 1, 0).astype(F32)
    total = total.astype(BF16)
    total = (total.astype(F32) + swap(total, 0, 2).astype(F32)).astype(BF16)
    return rejoin(total, swap(total, 0, 1), core == 0).astype(F32)[None]


def on_device_rings(
    hidden_in, segment_ids, routes, attn_gain, moe_gain, w_query, w_key, w_value, w_out, w_router,
    expert_gate, expert_up, expert_down, out_grad,
):
    rows, width = hidden_in.shape
    experts = w_router.shape[1]
    shard = lax.axis_index("shard")
    expert = lax.axis_index("expert")
    core = shard % 2
    where_shard = shard.astype(jnp.int32)[None]
    where_expert = expert.astype(jnp.int32)[None]
    where_core = core.astype(jnp.int32)[None]
    where_far_core = 1 - where_core
    block = width // N_SHARD
    low = KVH * HEAD

    small = jnp.concatenate(
        [w_router, attn_gain[:, None], moe_gain[:, None], jnp.zeros((block, LANES - experts - 2), BF16)], 1
    )
    packed = gather_shards(jnp.concatenate([w_key, w_value, small], 1))
    query_w = gather_shards(w_query)
    out_w = gather_shards(w_out)
    mask = (routes[:, :, None] == jnp.arange(LANES, dtype=jnp.int32)[None, None, :]).any(1)
    dy_routes = [jnp.concatenate([out_grad, mask.astype(BF16)], 1)]
    for _ in range(3):
        dy_routes.append(next_plane(dy_routes[-1]))
    own = (expert_gate[0], expert_up[0], expert_down[0])
    far = tuple(fetch_far(member, core) for member in own)

    inputs = hidden_in.astype(F32)
    factor_attn = lax.rsqrt(jnp.mean(inputs * inputs, -1, keepdims=True) + EPSILON)
    unit_rel = jnp.concatenate(
        xor_blocks([inputs[:, j * block : (j + 1) * block] for j in range(4)], shard), 1
    ) * factor_attn
    gain_rel = jnp.concatenate([member[:, 2 * low + experts] for member in packed]).astype(F32)
    h1_rel = (unit_rel * gain_rel).astype(BF16)
    key_value_w = [member[:, : 2 * low] for member in packed]
    pre = sum(dot_nn(h1_rel[:, j * block : (j + 1) * block], key_value_w[j]) for j in range(4))
    positions = shard * rows + jnp.arange(rows, dtype=jnp.int32)
    cosine, sine = rope_tables(positions, HEAD)
    key_local = rotate(pre[:, :low], cosine, sine, HEAD)
    key_value = jnp.concatenate([key_local, pre[:, low:]], 1).astype(BF16)
    keys_values = jnp.concatenate(xor_blocks(gather_shards(key_value), shard), 0)
    cosine_row = jnp.concatenate([cosine, cosine], 1)
    sine_row = jnp.concatenate([-sine, sine], 1)
    seg_query = lax.dynamic_slice_in_dim(segment_ids, shard * rows, rows)[:, None]
    queries, probs, attended = attention_forward(
        where_shard, h1_rel, query_w, keys_values, cosine_row, sine_row, seg_query, segment_ids[None, :]
    )
    mid_state = inputs + sum(
        dot_nn(attended[:, j * block : (j + 1) * block], out_w[j]) for j in range(4)
    )
    factor_moe = lax.rsqrt(jnp.mean(mid_state * mid_state, -1, keepdims=True) + EPSILON)
    unit_moe = mid_state * factor_moe
    small_true = jnp.concatenate(xor_blocks([member[:, 2 * low :] for member in packed], shard), 0)
    gain_moe = small_true[:, experts + 1].astype(F32)
    router_pad = jnp.where(jnp.arange(LANES)[None, :] < experts, small_true, 0)
    router = small_true[:, :experts].astype(F32)
    h2 = [(unit_moe * gain_moe).astype(BF16)]

    h1_rows = [h1_rel[:, :block]] + [swap(h1_rel[:, j * block : (j + 1) * block], 0, j) for j in (1, 2, 3)]
    att_rows = [attended[:, :block]] + [
        swap(attended[:, j * block : (j + 1) * block], 0, j) for j in (1, 2, 3)
    ]

    for _ in range(3):
        h2.append(next_plane(h2[-1]))
    done = [None] * 4
    add = lambda a, b: (a.astype(F32) + b.astype(F32)).astype(BF16)
    done[0] = expert_block(where_expert, h2[0], dy_routes[0], router_pad, own, far)
    message = None
    mixed = None
    for j in (1, 2, 3):
        done[j] = expert_block(where_expert, h2[j], dy_routes[j], router_pad, own, far)
        message = next_plane(done[j][0] if j == 1 else add(done[j][0], message))
        mixed = next_plane(done[j][1] if j == 1 else add(done[j][1], mixed))
    total = done[0][0].astype(F32) + message.astype(F32)
    layer_out = (mid_state + done[0][1].astype(F32) + mixed.astype(F32)).astype(BF16)

    hidden = own[0].shape[1]
    deep = width // 2

    def in_grads(where):
        return summed_products(
            where, h2, [[done[j][2] for j in range(4)], [done[j][3] for j in range(4)]], (2,),
            pl.BlockSpec((rows, deep), lambda i, w: (0, w[0])),
            pl.BlockSpec((rows, hidden), lambda i, w: (0, i)),
            pl.BlockSpec((deep, hidden), lambda i, w: (0, i)),
            (deep, 2 * hidden), "expert_in_grads",
        )

    def down_grads(where):
        return summed_products(
            where, [done[j][4] for j in range(4)], [dy_routes], (2,),
            pl.BlockSpec((rows, hidden // 2), lambda i, w: (0, 2 * i + w[0])),
            pl.BlockSpec((rows, width), lambda i, w: (0, 0)),
            pl.BlockSpec((hidden // 2, width), lambda i, w: (i, 0)),
            (hidden, width), "expert_down_grads",
        )

    (down_send,) = down_grads(where_far_core)
    gate_send, up_send = in_grads(where_far_core)
    (down_keep,) = down_grads(where_core)
    gate_keep, up_keep = in_grads(where_core)
    down_sum = expert_weight_sums(down_send, down_keep, 0, core)
    gate_sum = expert_weight_sums(gate_send, gate_keep, 1, core)
    up_sum = expert_weight_sums(up_send, up_keep, 1, core)

    named = mask[:, :experts]
    logits = jnp.where(named, dot_nn(h2[0], router_pad[:, :experts]), MASKED_SCORE)
    weights = jnp.where(named, jnp.exp(logits - jnp.max(logits, -1, keepdims=True)), 0.0)
    gate = weights / jnp.sum(weights, -1, keepdims=True)
    gate_grad = total[:, width : width + experts] + total[:, width + experts : width + 2 * experts]
    d_logits = gate * (gate_grad - jnp.sum(gate * gate_grad, -1, keepdims=True))
    d_h2 = total[:, :width] + jnp.dot(d_logits, router.T, precision=HIGHEST)
    router_grad = jnp.dot(d_logits.T, h2[0].astype(F32), precision=HIGHEST)
    d_mid_norm, gain_moe_grad = norm_backward(d_h2, unit_moe, factor_moe, gain_moe)
    d_mid = out_grad.astype(F32) + d_mid_norm
    d_branch = d_mid.astype(BF16)
    branches = gather_shards(d_branch)

    def mixer_grads(lefts, rights, name):
        n = rights[0].shape[1]
        (pieces,) = summed_products(
            where_expert, lefts, [rights], (1,),
            pl.BlockSpec((rows, block), lambda i, w: (0, 0)),
            pl.BlockSpec((rows, n), lambda i, w: (0, 0)),
            pl.BlockSpec((N_EXPERT, block // N_EXPERT, n), lambda i, w: (0, 0, 0)),
            (N_EXPERT, block // N_EXPERT, n), name,
        )
        even, odd = sum_over_planes(pieces)
        return reorder(where_expert, even, odd)

    out_w_grad = mixer_grads(att_rows, branches, "w_out_grad")

    d_q_pre, d_key_part, d_value_part, d_normed = attention_backward(
        where_shard, d_branch, out_w, attended, queries, probs, keys_values, query_w, cosine_row, sine_row
    )
    d_parts = jnp.concatenate([d_key_part, d_value_part], 1).reshape(N_SHARD, rows, 2 * low)
    d_rel = xor_blocks([d_parts[j] for j in range(4)], shard)
    from_core = swap(jnp.stack([d_rel[1], d_rel[3]]), 0, 1)
    d_far = add(d_rel[2], from_core[1])
    d_key_value = d_rel[0].astype(F32) + from_core[0].astype(F32) + swap(d_far, 0, 2).astype(F32)
    d_k_pre = rotate(d_key_value[:, :low], cosine, -sine, HEAD)
    d_kv_pre = jnp.concatenate([d_k_pre, d_key_value[:, low:]], 1).astype(BF16)
    d_pre = gather_shards(jnp.concatenate([d_q_pre, d_kv_pre], 1))
    in_grad = mixer_grads(h1_rows, d_pre, "w_in_grads")
    d_normed = d_normed + jnp.concatenate([dot_nt(d_kv_pre, member) for member in key_value_w], 1)
    d_input_norm, gain_attn_grad = norm_backward(d_normed, unit_rel, factor_attn, gain_rel)
    d_input_norm = jnp.concatenate(
        xor_blocks([d_input_norm[:, j * block : (j + 1) * block] for j in range(4)], shard), 1
    )
    input_grad = d_mid + d_input_norm

    rest = jnp.concatenate([gain_moe_grad[None], router_grad, jnp.zeros((6, width), F32)], 0)
    rest = xor_blocks([rest[:, j * block : (j + 1) * block] for j in range(4)], shard)
    pieces = [
        jnp.concatenate([gain_attn_grad[None, j * block : (j + 1) * block], rest[j]], 0) for j in range(4)
    ]
    from_core = swap(jnp.stack([pieces[1], pieces[3]]), 0, 1)
    sums = pieces[0] + from_core[0] + swap(pieces[2] + from_core[1], 0, 2)
    for bit in (1, 2, 4):
        sums = sums + swap(sums, bit, 0)
    return (
        layer_out,
        input_grad,
        sums[0],
        sums[1],
        in_grad[:, :width],
        in_grad[:, width : width + low],
        in_grad[:, width + low :],
        out_w_grad,
        sums[2 : 2 + experts].T,
        gate_sum,
        up_sum,
        down_sum,
    )


def on_device(hidden_in, segment_ids, routes, *rest):
    rows = hidden_in.shape[0]
    experts = rest[6].shape[1]
    capacity = rows * routes.shape[1] * 2 // experts
    shape = (lax.axis_size("expert"), lax.axis_size("shard"))
    if shape == (N_EXPERT, N_SHARD) and experts == N_EXPERT and capacity == rows:
        return on_device_rings(hidden_in, segment_ids, routes, *rest)
    return on_device_routed(hidden_in, segment_ids, routes, *rest)


def solution(mesh):
    placed = (
        P(("expert", "shard"), None),
        P("expert"),
        P(("expert", "shard"), None),
        P("shard"),
        P("shard"),
        P("shard", None),
        P("shard", None),
        P("shard", None),
        P("shard", None),
        P("shard", None),
        P("expert", None, None),
        P("expert", None, None),
        P("expert", None, None),
        P(("expert", "shard"), None),
    )
    return jax.shard_map(
        on_device,
        mesh=mesh,
        in_specs=placed,
        out_specs=(
            P(("expert", "shard"), None),
            P(("expert", "shard"), None),
            P("shard"),
            P("shard"),
            P("shard", None),
            P("shard", None),
            P("shard", None),
            P("shard", None),
            P("shard", None),
            P("expert", None, None),
            P("expert", None, None),
            P("expert", None, None),
        ),
        check_vma=False,
    )
```

```python
import functools

import jax
import jax.numpy as jnp
from jax import lax
from jax.experimental import pallas as pl
from jax.experimental.pallas import tpu as pltpu
from jax.sharding import PartitionSpec as P

HQ = 12
KVH = 2
HEAD = 128


EPSILON = 1e-06
ROPE_BASE = 10000.0
MASKED_SCORE = -1e30
HIGHEST = lax.Precision.HIGHEST


def rope_tables(positions, head_size):
    half_size = head_size // 2
    frequency = ROPE_BASE ** (-(jnp.arange(half_size, dtype=jnp.float32) * 2.0 / head_size))
    angles = positions.astype(jnp.float32)[:, None] * frequency[None, :]
    return (jnp.cos(angles), jnp.sin(angles))


def rotate(values, cosine_table, sine_table, head_size):
    rows_count = values.shape[0]
    shaped = values.reshape(rows_count, -1, head_size)
    half_size = head_size // 2
    first_half = shaped[..., :half_size]
    second_half = shaped[..., half_size:]
    cosine_part = cosine_table[:, None, :]
    sine_part = sine_table[:, None, :]
    turned = jnp.concatenate(
        [
            first_half * cosine_part - second_half * sine_part,
            second_half * cosine_part + first_half * sine_part,
        ],
        -1,
    )
    return turned.reshape(rows_count, -1)


def norm_forward(values, gain):
    factor = lax.rsqrt(jnp.mean(values * values, -1, keepdims=True) + EPSILON)
    unit_rows = values * factor
    return (unit_rows, factor, (unit_rows * gain).astype(jnp.bfloat16))


def norm_backward(grad_rows, unit_rows, factor, gain):
    gain_grad = jnp.sum(grad_rows * unit_rows, 0)
    scaled_grad = grad_rows * gain
    return (
        factor * (scaled_grad - unit_rows * jnp.mean(scaled_grad * unit_rows, -1, keepdims=True)),
        gain_grad,
    )


def score_block(query_heads, key_heads, visible, score_scale):
    raw_scores = jnp.einsum(
        "tkgd,skd->kgts", query_heads, key_heads, preferred_element_type=jnp.float32
    )
    return jnp.where(visible, raw_scores * score_scale, MASKED_SCORE)


def on_device_routed(
    hidden_in,
    segment_ids,
    routes,
    attn_gain,
    moe_gain,
    w_query,
    w_key,
    w_value,
    w_out,
    w_router,
    expert_gate,
    expert_up,
    expert_down,
    out_grad,
):
    tok_rows = hidden_in.shape[0]
    top_count = routes.shape[1]
    experts = w_router.shape[1]
    capacity = tok_rows * top_count * 2 // experts
    groups = HQ // KVH
    score_scale = HEAD ** (-0.5)
    shard_index = lax.axis_index("shard")
    n_expert = lax.axis_size("expert")
    local_experts = expert_gate.shape[0]
    gain_attn, gain_moe, query_w, key_w, value_w, out_w, router_w = (
        lax.all_gather(attn_gain, "shard", axis=0, tiled=True),
        lax.all_gather(moe_gain, "shard", axis=0, tiled=True),
        lax.all_gather(w_query, "shard", axis=0, tiled=True),
        lax.all_gather(w_key, "shard", axis=0, tiled=True),
        lax.all_gather(w_value, "shard", axis=0, tiled=True),
        lax.all_gather(w_out, "shard", axis=0, tiled=True),
        lax.all_gather(w_router, "shard", axis=0, tiled=True),
    )
    gain_attn = gain_attn.astype(jnp.float32)
    gain_moe = gain_moe.astype(jnp.float32)
    inputs = hidden_in.astype(jnp.float32)
    unit_attn, factor_attn, normed = norm_forward(inputs, gain_attn)
    q_pre = jnp.dot(normed, query_w, preferred_element_type=jnp.float32)
    k_pre = jnp.dot(normed, key_w, preferred_element_type=jnp.float32)
    value_rows = jnp.dot(normed, value_w, preferred_element_type=jnp.float32).astype(jnp.bfloat16)
    positions = shard_index * tok_rows + jnp.arange(tok_rows, dtype=jnp.int32)
    cosine_table, sine_table = rope_tables(positions, HEAD)
    queries = rotate(q_pre, cosine_table, sine_table, HEAD).astype(jnp.bfloat16)
    key_local = rotate(k_pre, cosine_table, sine_table, HEAD).astype(jnp.bfloat16)
    key_rows, value_all = (
        lax.all_gather(key_local, "shard", axis=0, tiled=True),
        lax.all_gather(value_rows, "shard", axis=0, tiled=True),
    )
    seq_len = key_rows.shape[0]
    query_heads = queries.reshape(tok_rows, KVH, groups, HEAD)
    key_heads = key_rows.reshape(seq_len, KVH, HEAD)
    value_heads = value_all.reshape(seq_len, KVH, HEAD)
    seg_local = lax.dynamic_slice_in_dim(segment_ids, shard_index * tok_rows, tok_rows)
    visible = (positions[:, None] >= jnp.arange(seq_len, dtype=jnp.int32)[None, :]) & (
        seg_local[:, None] == segment_ids[None, :]
    )
    score_values = score_block(query_heads, key_heads, visible, score_scale)
    top_score = jnp.max(score_values, -1, keepdims=True)
    exponent = jnp.exp(score_values - top_score)
    denominators = jnp.sum(exponent, -1, keepdims=True)
    probabilities = exponent / denominators
    log_total = top_score + jnp.log(denominators)
    attended = (
        jnp.einsum(
            "kgts,skd->tkgd",
            probabilities.astype(jnp.bfloat16),
            value_heads,
            preferred_element_type=jnp.float32,
        )
        .reshape(tok_rows, -1)
        .astype(jnp.bfloat16)
    )
    mid_state = inputs + jnp.dot(attended, out_w, preferred_element_type=jnp.float32)
    unit_moe, factor_moe, normed_moe = norm_forward(mid_state, gain_moe)
    logits = jnp.dot(normed_moe, router_w, preferred_element_type=jnp.float32)
    onehot = (routes[:, :, None] == jnp.arange(experts, dtype=jnp.int32)[None, None, :]).astype(
        jnp.float32
    )
    chosen = jnp.sum(onehot * logits[:, None, :], -1)
    chosen = chosen - jnp.max(chosen, -1, keepdims=True)
    weights = jnp.exp(chosen)
    gate = weights / jnp.sum(weights, -1, keepdims=True)
    flat_routes = routes.reshape(-1)
    route_hot = (flat_routes[:, None] == jnp.arange(experts, dtype=jnp.int32)[None, :]).astype(
        jnp.int32
    )
    before = jnp.cumsum(route_hot, 0, dtype=jnp.int32) - route_hot
    slot_id = flat_routes * capacity + jnp.sum(before * route_hot, 1, dtype=jnp.int32)
    source = (
        jnp.zeros((experts * capacity,), jnp.int32)
        .at[slot_id]
        .set(jnp.arange(tok_rows * top_count, dtype=jnp.int32))
    )
    filled = jnp.zeros((experts * capacity,), jnp.bool_).at[slot_id].set(True)
    outgoing = jnp.where(filled[:, None], jnp.take(normed_moe, source // top_count, axis=0), 0)
    outgoing = outgoing.reshape(experts, capacity, -1)
    arrived = lax.all_to_all(outgoing, "expert", split_axis=0, concat_axis=0, tiled=True)
    item_count = arrived.shape[1]
    shaped = arrived.reshape(n_expert, local_experts, item_count, -1)
    gate_pre = jnp.einsum("nlcd,ldf->nlcf", shaped, expert_gate, preferred_element_type=jnp.float32)
    up_pre = jnp.einsum("nlcd,ldf->nlcf", shaped, expert_up, preferred_element_type=jnp.float32)
    hidden_rows = (gate_pre * jax.nn.sigmoid(gate_pre) * up_pre).astype(jnp.bfloat16)
    result = jnp.einsum(
        "nlcf,lfd->nlcd", hidden_rows, expert_down, preferred_element_type=jnp.float32
    )
    result = result.astype(jnp.bfloat16).reshape(arrived.shape)
    returned = lax.all_to_all(result, "expert", split_axis=0, concat_axis=0, tiled=True)
    outcome = (
        returned,
        arrived,
        gate_pre.reshape(n_expert * local_experts, item_count, -1),
        up_pre.reshape(n_expert * local_experts, item_count, -1),
        hidden_rows.reshape(n_expert * local_experts, item_count, -1),
    )
    returned_rows = jnp.take(outcome[0].reshape(experts * capacity, -1), slot_id, axis=0).reshape(
        tok_rows, top_count, -1
    )
    mixed = mid_state + jnp.sum(gate[:, :, None] * returned_rows, 1)
    layer_out = mixed.astype(jnp.bfloat16)
    grad_out = out_grad.astype(jnp.float32)
    gate_grad = jnp.sum(returned_rows * grad_out[:, None, :], -1)
    gate_slots = jnp.take(gate.reshape(-1), source, axis=0)
    d_send = jnp.where(
        filled[:, None], jnp.take(grad_out, source // top_count, axis=0) * gate_slots[:, None], 0.0
    )
    d_send = d_send.astype(jnp.bfloat16).reshape(experts, capacity, -1)
    d_arrived = lax.all_to_all(d_send, "expert", split_axis=0, concat_axis=0, tiled=True)
    d_shaped = d_arrived.reshape(n_expert, local_experts, capacity, -1)
    arrived_rows = outcome[1].reshape(n_expert, local_experts, capacity, -1)
    gate_pre = outcome[2].reshape(n_expert, local_experts, capacity, -1)
    up_pre = outcome[3].reshape(n_expert, local_experts, capacity, -1)
    hidden_rows = outcome[4].reshape(n_expert, local_experts, capacity, -1)
    sigmoid_gate = jax.nn.sigmoid(gate_pre)
    d_hidden = jnp.einsum(
        "nlcd,lfd->nlcf", d_shaped, expert_down, preferred_element_type=jnp.float32
    )
    down_grad = jnp.einsum(
        "nlcf,nlcd->lfd", hidden_rows, d_shaped, preferred_element_type=jnp.float32
    )
    d_gate = (d_hidden * up_pre * sigmoid_gate * (1.0 + gate_pre * (1.0 - sigmoid_gate))).astype(
        jnp.bfloat16
    )
    d_up = (d_hidden * gate_pre * sigmoid_gate).astype(jnp.bfloat16)
    gate_w_grad = jnp.einsum(
        "nlcd,nlcf->ldf", arrived_rows, d_gate, preferred_element_type=jnp.float32
    )
    up_w_grad = jnp.einsum("nlcd,nlcf->ldf", arrived_rows, d_up, preferred_element_type=jnp.float32)
    d_rows = jnp.einsum("nlcf,ldf->nlcd", d_gate, expert_gate, preferred_element_type=jnp.float32)
    d_rows = d_rows + jnp.einsum(
        "nlcf,ldf->nlcd", d_up, expert_up, preferred_element_type=jnp.float32
    )
    d_rows = d_rows.astype(jnp.bfloat16).reshape(experts, capacity, -1)
    d_returned = lax.all_to_all(d_rows, "expert", split_axis=0, concat_axis=0, tiled=True)
    expert_sums = (
        lax.psum(gate_w_grad.astype(jnp.bfloat16), "shard").astype(jnp.float32),
        lax.psum(up_w_grad.astype(jnp.bfloat16), "shard").astype(jnp.float32),
        lax.psum(down_grad.astype(jnp.bfloat16), "shard").astype(jnp.float32),
    )
    d_copies = jnp.take(d_returned.reshape(experts * capacity, -1), slot_id, axis=0).reshape(
        tok_rows, top_count, -1
    )
    d_normed_moe = jnp.sum(d_copies, 1, dtype=jnp.float32)
    d_chosen = gate * (gate_grad - jnp.sum(gate * gate_grad, -1, keepdims=True))
    d_logits = jnp.sum(onehot * d_chosen[:, :, None], 1)
    router_f32 = router_w.astype(jnp.float32)
    d_normed_moe = d_normed_moe + jnp.dot(d_logits, router_f32.T, precision=HIGHEST)
    router_grad = jnp.dot(normed_moe.astype(jnp.float32).T, d_logits, precision=HIGHEST)
    d_mid_norm, gain_moe_grad = norm_backward(d_normed_moe, unit_moe, factor_moe, gain_moe)
    d_mid = grad_out + d_mid_norm
    d_branch = d_mid.astype(jnp.bfloat16)
    out_w_grad = jnp.dot(attended.T, d_branch, preferred_element_type=jnp.float32)
    d_attended = jnp.dot(d_branch, out_w.T, preferred_element_type=jnp.float32).astype(jnp.bfloat16)
    d_attended = d_attended.reshape(tok_rows, KVH, groups, HEAD)
    score_again = score_block(query_heads, key_heads, visible, score_scale)
    prob_again = jnp.exp(score_again - log_total)
    d_probs = jnp.einsum(
        "tkgd,skd->kgts", d_attended, value_heads, preferred_element_type=jnp.float32
    )
    d_scores = (
        prob_again * (d_probs - jnp.sum(prob_again * d_probs, -1, keepdims=True)) * score_scale
    )
    d_scores = d_scores.astype(jnp.bfloat16)
    d_query = jnp.einsum(
        "kgts,skd->tkgd", d_scores, key_heads, preferred_element_type=jnp.float32
    ).reshape(tok_rows, -1)
    d_key_part = jnp.einsum(
        "kgts,tkgd->skd", d_scores, query_heads, preferred_element_type=jnp.float32
    ).reshape(seq_len, -1)
    d_value_part = jnp.einsum(
        "kgts,tkgd->skd",
        prob_again.astype(jnp.bfloat16),
        d_attended,
        preferred_element_type=jnp.float32,
    ).reshape(seq_len, -1)
    d_keys, d_values = (
        lax.psum_scatter(
            d_key_part.astype(jnp.bfloat16), "shard", scatter_dimension=0, tiled=True
        ).astype(jnp.float32),
        lax.psum_scatter(
            d_value_part.astype(jnp.bfloat16), "shard", scatter_dimension=0, tiled=True
        ).astype(jnp.float32),
    )
    d_q_pre = rotate(d_query, cosine_table, -sine_table, HEAD).astype(jnp.bfloat16)
    d_k_pre = rotate(d_keys, cosine_table, -sine_table, HEAD).astype(jnp.bfloat16)
    d_v_pre = d_values.astype(jnp.bfloat16)
    query_grad = jnp.dot(normed.T, d_q_pre, preferred_element_type=jnp.float32)
    key_grad = jnp.dot(normed.T, d_k_pre, preferred_element_type=jnp.float32)
    value_grad = jnp.dot(normed.T, d_v_pre, preferred_element_type=jnp.float32)
    d_normed = jnp.dot(d_q_pre, query_w.T, preferred_element_type=jnp.float32)
    d_normed = d_normed + jnp.dot(d_k_pre, key_w.T, preferred_element_type=jnp.float32)
    d_normed = d_normed + jnp.dot(d_v_pre, value_w.T, preferred_element_type=jnp.float32)
    d_input_norm, gain_attn_grad = norm_backward(d_normed, unit_attn, factor_attn, gain_attn)
    input_grad = d_mid + d_input_norm
    partial_sums = (
        gain_attn_grad,
        gain_moe_grad,
        query_grad,
        key_grad,
        value_grad,
        out_w_grad,
        router_grad,
    )
    summed = lax.psum(
        (
            partial_sums[0],
            partial_sums[1],
            partial_sums[2],
            partial_sums[3],
            partial_sums[4],
            partial_sums[5],
            partial_sums[6],
        ),
        ("expert", "shard"),
    )
    n_shard = lax.axis_size("shard")
    owned_grads = tuple(
        (
            lax.dynamic_slice_in_dim(
                member, shard_index * (member.shape[0] // n_shard), member.shape[0] // n_shard, 0
            )
            for member in summed
        )
    )
    return (
        layer_out,
        input_grad,
        owned_grads[0],
        owned_grads[1],
        owned_grads[2],
        owned_grads[3],
        owned_grads[4],
        owned_grads[5],
        owned_grads[6],
        expert_sums[0],
        expert_sums[1],
        expert_sums[2],
    )


AXES = ("expert", "shard")
N_EXPERT = 8
N_SHARD = 4
LANES = 128
MEBIBYTE = 1 << 20
BF16 = jnp.bfloat16
F32 = jnp.float32


def cost(microseconds):
    return pl.CostEstimate(flops=microseconds * 10**9, bytes_accessed=10**5, transcendentals=0)


def swap(values, expert_bits, shard_bits):
    pairs = [
        (e * N_SHARD + s, (e ^ expert_bits) * N_SHARD + (s ^ shard_bits))
        for e in range(N_EXPERT)
        for s in range(N_SHARD)
    ]
    return lax.ppermute(values, AXES, pairs)


def next_plane(values):
    pairs = [
        (e * N_SHARD + s, ((e + 2) % N_EXPERT) * N_SHARD + s)
        for e in range(N_EXPERT)
        for s in range(N_SHARD)
    ]
    return lax.ppermute(values, AXES, pairs)


def gather_shards(values):
    other_core = swap(values, 0, 1)
    other_y = swap(values, 0, 2)
    return [values, other_core, other_y, swap(other_y, 0, 1)]


def xor_blocks(blocks, index):
    odd = (index & 1) == 1
    high = (index & 2) == 2
    once = [jnp.where(odd, blocks[j ^ 1], blocks[j]) for j in range(4)]
    return [jnp.where(high, once[j ^ 2], once[j]) for j in range(4)]


def together(*values):
    return lax.optimization_barrier(values)


def after(value, *others):
    return lax.optimization_barrier((value,) + others)[0]


def rejoin(mine, partner, low_first):
    return jnp.where(
        low_first,
        jnp.concatenate([mine, partner], 0),
        jnp.concatenate([partner, mine], 0),
    )


def dot_nn(left, right):
    return lax.dot_general(left, right, (((1,), (0,)), ((), ())), preferred_element_type=F32)


def dot_nt(left, right):
    return lax.dot_general(left, right, (((1,), (1,)), ((), ())), preferred_element_type=F32)


def dot_tn(left, right):
    return lax.dot_general(left, right, (((0,), (0,)), ((), ())), preferred_element_type=F32)


def turn(values, cosine, sine):
    return values * cosine + pltpu.roll(values, HEAD // 2, 1) * sine


def attention_forward_body(
    where_ref, h1_ref, w0, w1, w2, w3, key_ref, value_ref, cos_ref, sin_ref, segq_ref, segk_ref,
    query_out, prob_out, attended_out, bias_ref,
):
    rows, seq_len = bias_ref.shape

    @pl.when(pl.program_id(0) == 0)
    def _():
        base = where_ref[0] * rows
        query_pos = base + lax.broadcasted_iota(jnp.int32, (rows, seq_len), 0)
        key_pos = lax.broadcasted_iota(jnp.int32, (rows, seq_len), 1)
        visible = (query_pos >= key_pos) & (segq_ref[...] == segk_ref[...])
        bias_ref[...] = jnp.where(visible, 0.0, MASKED_SCORE)

    depth = w0.shape[0]
    pre = dot_nn(h1_ref[:, :depth], w0[...])
    for j, weight in enumerate((w1, w2, w3)):
        pre = pre + dot_nn(h1_ref[:, (j + 1) * depth : (j + 2) * depth], weight[...])
    for h in range(pre.shape[1] // HEAD):
        cols = slice(h * HEAD, (h + 1) * HEAD)
        query = turn(pre[:, cols], cos_ref[...], sin_ref[...]).astype(BF16)
        query_out[:, cols] = query
        scores = dot_nt(query, key_ref[...]) * HEAD ** (-0.5) + bias_ref[...]
        exponent = jnp.exp(scores - jnp.max(scores, -1, keepdims=True))
        total = jnp.sum(exponent, -1, keepdims=True)
        probs = (exponent * (1.0 / total)).astype(BF16)
        prob_out[h] = probs
        attended_out[:, cols] = dot_nn(probs, value_ref[...]).astype(BF16)


def attention_forward(where, h1_rel, w_query, keys_values, cosine, sine, seg_query, seg_key):
    rows, width = h1_rel.shape
    seq_len = keys_values.shape[0]
    cols = width // N_SHARD
    heads = cols // HEAD

    def whole(shape):
        return pl.BlockSpec(shape, lambda j, w: (0,) * len(shape))

    weight = pl.BlockSpec((cols, cols), lambda j, w: (0, w[0] ^ j))
    part = pl.BlockSpec((rows, cols), lambda j, w: (0, j))
    return pl.pallas_call(
        attention_forward_body,
        grid_spec=pltpu.PrefetchScalarGridSpec(
            num_scalar_prefetch=1,
            grid=(N_SHARD,),
            in_specs=[
                whole((rows, width)), weight, weight, weight, weight,
                pl.BlockSpec((seq_len, HEAD), lambda j, w: (0, (w[0] ^ j) // 2)),
                pl.BlockSpec((seq_len, HEAD), lambda j, w: (0, KVH + (w[0] ^ j) // 2)),
                whole((rows, HEAD)), whole((rows, HEAD)), whole((rows, 1)), whole((1, seq_len)),
            ],
            out_specs=[part, pl.BlockSpec((heads, rows, seq_len), lambda j, w: (j, 0, 0)), part],
            scratch_shapes=[pltpu.VMEM((rows, seq_len), F32)],
        ),
        out_shape=[
            jax.ShapeDtypeStruct((rows, width), BF16),
            jax.ShapeDtypeStruct((HQ, rows, seq_len), BF16),
            jax.ShapeDtypeStruct((rows, width), BF16),
        ],
        compiler_params=pltpu.CompilerParams(vmem_limit_bytes=56 * MEBIBYTE),
        cost_estimate=cost(15),
        name="attention_forward",
    )(where, h1_rel, *w_query, keys_values, keys_values, cosine, sine, seg_query, seg_key)


def attention_backward_body(
    where_ref, branch_ref, out0, out1, out2, out3, attended_ref, query_ref, prob_ref, key_ref, value_ref,
    w0, w1, w2, w3, cos_ref, sin_ref,
    dq_out, dk_out, dv_out, dh_out, dh_acc, dk_acc, dv_acc, da_ref, stack_ref,
):
    step = pl.program_id(0)
    depth = w0.shape[0]
    rows = branch_ref.shape[0]

    for j, weight in enumerate((out0, out1, out2, out3)):

        @pl.when(step == j)
        def _(weight=weight):
            da_ref[...] = dot_nt(branch_ref[...], weight[...]).astype(BF16)

    @pl.when(step % 2 == 0)
    def _():
        dk_acc[...] = jnp.zeros_like(dk_acc)
        dv_acc[...] = jnp.zeros_like(dv_acc)

    @pl.when(step == 0)
    def _():
        dh_acc[...] = jnp.zeros_like(dh_acc)

    d_pre = []
    for h in range(depth // HEAD):
        cols = slice(h * HEAD, (h + 1) * HEAD)
        d_att = da_ref[:, cols]
        probs = prob_ref[h]
        delta = jnp.sum(d_att.astype(F32) * attended_ref[:, cols].astype(F32), -1, keepdims=True)
        d_probs = dot_nt(d_att, value_ref[...])
        d_scores = (probs.astype(F32) * ((d_probs - delta) * HEAD ** (-0.5))).astype(BF16)
        stack_ref[h * rows : (h + 1) * rows, :] = d_scores
        d_query = dot_nn(d_scores, key_ref[...])
        d_pre.append(turn(d_query, cos_ref[...], -sin_ref[...]).astype(BF16))
        dk_acc[...] += dot_tn(query_ref[:, cols], d_scores)
        dv_acc[...] += dot_tn(d_att, probs)
    d_pre = jnp.concatenate(d_pre, 1)
    dq_out[...] = d_pre
    for j, weight in enumerate((w0, w1, w2, w3)):
        dh_acc[:, j * depth : (j + 1) * depth] += dot_nt(d_pre, weight[...])

    @pl.when(step % 2 == 1)
    def _():
        dk_out[...] = dk_acc[...].T.astype(BF16)
        dv_out[...] = dv_acc[...].T.astype(BF16)

    @pl.when(step == N_SHARD - 1)
    def _():
        dh_out[...] = dh_acc[...]


def attention_backward(where, branch, w_out, attended, queries, probs, keys_values, w_query, cosine, sine):
    rows, width = branch.shape
    seq_len = keys_values.shape[0]
    cols = width // N_SHARD
    heads = cols // HEAD

    def whole(shape):
        return pl.BlockSpec(shape, lambda j, w: (0,) * len(shape))

    weight = pl.BlockSpec((cols, cols), lambda j, w: (0, w[0] ^ j))
    part = pl.BlockSpec((rows, cols), lambda j, w: (0, j))
    head_part = pl.BlockSpec((seq_len, HEAD), lambda j, w: (0, (w[0] ^ j) // 2))
    return pl.pallas_call(
        attention_backward_body,
        grid_spec=pltpu.PrefetchScalarGridSpec(
            num_scalar_prefetch=1,
            grid=(N_SHARD,),
            in_specs=[whole((rows, width))] + [whole((cols, width))] * 4 + [
                part, part, pl.BlockSpec((heads, rows, seq_len), lambda j, w: (j, 0, 0)),
                head_part,
                pl.BlockSpec((seq_len, HEAD), lambda j, w: (0, KVH + (w[0] ^ j) // 2)),
                weight, weight, weight, weight, whole((rows, HEAD)), whole((rows, HEAD)),
            ],
            out_specs=[
                pl.BlockSpec((rows, cols), lambda j, w: (0, w[0] ^ j)),
                head_part, head_part, whole((rows, width)),
            ],
            scratch_shapes=[
                pltpu.VMEM((rows, width), F32),
                pltpu.VMEM((HEAD, seq_len), F32),
                pltpu.VMEM((HEAD, seq_len), F32),
                pltpu.VMEM((rows, cols), BF16),
                pltpu.VMEM((heads * rows, seq_len), BF16),
            ],
        ),
        out_shape=[
            jax.ShapeDtypeStruct((rows, width), BF16),
            jax.ShapeDtypeStruct((seq_len, KVH * HEAD), BF16),
            jax.ShapeDtypeStruct((seq_len, KVH * HEAD), BF16),
            jax.ShapeDtypeStruct((rows, width), F32),
        ],
        compiler_params=pltpu.CompilerParams(vmem_limit_bytes=56 * MEBIBYTE),
        cost_estimate=cost(17),
        name="attention_backward",
    )(where, branch, *w_out, attended, queries, probs, keys_values, keys_values, *w_query, cosine, sine)


def expert_body(
    where_ref, h2_ref, dy_ref, router_ref, *refs,
):
    own, far = refs[:6], refs[6:12]
    message_out, mixed_out, da_out, db_out, act_out, gates_ref, dh_acc, y_acc, gg_acc = refs[12:]
    e = pl.program_id(0)
    f = pl.program_id(1)
    rows, width = h2_ref.shape
    half = width // 2
    lane = lax.broadcasted_iota(jnp.int32, (rows, LANES), 1)
    places = [pl.ds(pl.multiple_of((where_ref[1] ^ i) * half, LANES), half) for i in range(2)]

    @pl.when((e == 0) & (f == 0))
    def _():
        named = dy_ref[:, width:].astype(F32) > 0.5
        logits = dot_nt(h2_ref[...], router_ref[...])
        logits = jnp.concatenate([logits, jnp.zeros((rows, LANES - logits.shape[1]), F32)], 1)
        logits = jnp.where(named, logits, MASKED_SCORE)
        top = jnp.max(logits, -1, keepdims=True)
        weights = jnp.where(named, jnp.exp(logits - top), 0.0)
        gates_ref[...] = weights / jnp.sum(weights, -1, keepdims=True)
        dh_acc[...] = jnp.zeros_like(dh_acc)
        y_acc[...] = jnp.zeros_like(y_acc)
        gg_acc[...] = jnp.zeros_like(gg_acc)

    here = lane == (where_ref[0] ^ e)

    def work(members):
        gates, ups, downs = [[members[2 * k + i] for i in range(2)] for k in range(3)]
        gate = jnp.sum(jnp.where(here, gates_ref[...], 0.0), -1, keepdims=True)
        h2 = [h2_ref[:, place] for place in places]
        dy = [dy_ref[:, place] for place in places]
        load = lambda ref: ref[...].reshape(ref.shape[-2:])
        a = dot_nn(h2[0], load(gates[0])) + dot_nn(h2[1], load(gates[1]))
        b = dot_nn(h2[0], load(ups[0])) + dot_nn(h2[1], load(ups[1]))
        d_plain = dot_nt(dy[0], load(downs[0])) + dot_nt(dy[1], load(downs[1]))
        sigmoid = 1.0 / (1.0 + jnp.exp(-a))
        silu = a * sigmoid
        act = silu * b
        gate_grad = jnp.sum(act * d_plain, -1, keepdims=True)
        gg_acc[...] += jnp.where(here, gate_grad, 0.0)
        d_act = d_plain * gate
        d_a = (d_act * b * (sigmoid + silu * (1.0 - sigmoid))).astype(BF16)
        d_b = (d_act * silu).astype(BF16)
        scaled = (act * gate).astype(BF16)
        da_out[...] = d_a
        db_out[...] = d_b
        act_out[...] = scaled
        for i in range(2):
            dh_acc[i] += dot_nt(d_a, load(gates[i])) + dot_nt(d_b, load(ups[i]))
            y_acc[i] += dot_nn(scaled, load(downs[i]))

    @pl.when(e == 0)
    def _():
        work(own)

    @pl.when(e == 1)
    def _():
        work(far)

    @pl.when((e == pl.num_programs(0) - 1) & (f == pl.num_programs(1) - 1))
    def _():
        for i in range(2):
            message_out[:, places[i]] = dh_acc[i].astype(BF16)
            mixed_out[:, places[i]] = y_acc[i].astype(BF16)
        high = gg_acc[...].astype(BF16).astype(F32)
        low = pltpu.roll(gg_acc[...] - high, N_EXPERT, 1)
        message_out[:, width:] = (high + low).astype(BF16)


def expert_block(where, h2, dy_routes, router, own, far):
    rows, width = h2.shape
    hidden = own[0].shape[1]
    half = width // 2
    chunk = 256
    chunks = hidden // chunk

    def whole(shape):
        return pl.BlockSpec(shape, lambda e, f, w: (0,) * len(shape))

    own_step = lambda e, f: jnp.where(e == 0, f, chunks - 1)
    far_step = lambda e, f: jnp.where(e == 0, 0, f)
    own_in = [pl.BlockSpec((half, chunk), lambda e, f, w, i=i: (w[1] ^ i, own_step(e, f))) for i in range(2)]
    own_down = [pl.BlockSpec((chunk, half), lambda e, f, w, i=i: (own_step(e, f), w[1] ^ i)) for i in range(2)]
    far_in = [pl.BlockSpec((1, half, chunk), lambda e, f, w, k=k: (k, 0, far_step(e, f))) for k in range(2)]
    far_down = pl.BlockSpec((1, chunk, half), lambda e, f, w: (2, far_step(e, f), 0))
    part = pl.BlockSpec((rows, chunk), lambda e, f, w: (0, e * chunks + f))
    return pl.pallas_call(
        expert_body,
        grid_spec=pltpu.PrefetchScalarGridSpec(
            num_scalar_prefetch=1,
            grid=(2, chunks),
            in_specs=[whole((rows, width)), whole(dy_routes.shape), whole(router.shape)]
            + own_in + own_in + own_down
            + [far_in[0], far_in[0], far_in[1], far_in[1], far_down, far_down],
            out_specs=[whole((rows, width + LANES)), whole((rows, width)), part, part, part],
            scratch_shapes=[
                pltpu.VMEM((rows, LANES), F32),
                pltpu.VMEM((2, rows, half), F32),
                pltpu.VMEM((2, rows, half), F32),
                pltpu.VMEM((rows, LANES), F32),
            ],
        ),
        out_shape=[
            jax.ShapeDtypeStruct((rows, width + LANES), BF16),
            jax.ShapeDtypeStruct((rows, width), BF16),
            jax.ShapeDtypeStruct((rows, 2 * hidden), BF16),
            jax.ShapeDtypeStruct((rows, 2 * hidden), BF16),
            jax.ShapeDtypeStruct((rows, 2 * hidden), BF16),
        ],
        compiler_params=pltpu.CompilerParams(vmem_limit_bytes=28 * MEBIBYTE),
        cost_estimate=cost(20),
        name="expert_block",
    )(
        where, h2, dy_routes, router, own[0], own[0], own[1], own[1], own[2], own[2],
        far[0], far[1], far[0], far[1], far[0], far[1],
    )


def summed_products_body(where_ref, *refs, parts, sets):
    lefts = refs[:parts]
    rights = refs[parts : parts * (1 + sets)]
    outs = refs[parts * (1 + sets) :]
    for k in range(sets):
        total = dot_tn(lefts[0][...], rights[k * parts][...])
        for j in range(1, parts):
            total = total + dot_tn(lefts[j][...], rights[k * parts + j][...])
        out = outs[k]
        if len(out.shape) == 3:
            pieces = out.shape[0]
            deep = out.shape[1]
            for piece in range(pieces):
                out[where_ref[0] ^ piece] = total[piece * deep : (piece + 1) * deep].astype(out.dtype)
        else:
            out[...] = total.astype(out.dtype)


def summed_products(where, lefts, right_sets, grid, left_spec, right_spec, out_spec, out_shape, name):
    parts = len(lefts)
    sets = len(right_sets)
    return pl.pallas_call(
        functools.partial(summed_products_body, parts=parts, sets=sets),
        grid_spec=pltpu.PrefetchScalarGridSpec(
            num_scalar_prefetch=1,
            grid=grid,
            in_specs=[left_spec] * parts + [right_spec] * (parts * sets),
            out_specs=[out_spec] * sets,
        ),
        out_shape=[jax.ShapeDtypeStruct(out_shape, BF16)] * sets,
        compiler_params=pltpu.CompilerParams(vmem_limit_bytes=56 * MEBIBYTE),
        cost_estimate=cost(5),
        name=name,
    )(where, *lefts, *[member for members in right_sets for member in members])


def in_grads_body(where_ref, *refs):
    h2_refs, da_refs, db_refs = refs[:4], refs[4:8], refs[8:12]
    send_ref, keep_ref, turned_ref = refs[12:]
    rows = h2_refs[0].shape[0]
    half = turned_ref.shape[0] // 2

    @pl.when(pl.program_id(0) == 0)
    def _():
        for j in range(4):
            turned_ref[:, j * rows : (j + 1) * rows] = h2_refs[j][...].T

    for k, member in enumerate((da_refs, db_refs)):
        for out, place in ((send_ref, 1 - where_ref[0]), (keep_ref, where_ref[0])):
            here = pl.ds(pl.multiple_of(place * half, LANES), half)
            total = dot_nn(turned_ref[here, :rows], member[0][...])
            for j in range(1, 4):
                total = total + dot_nn(turned_ref[here, j * rows : (j + 1) * rows], member[j][...])
            out[k] = total.astype(BF16)


def expert_in_grads(where, h2, d_a, d_b):
    rows, width = h2[0].shape
    columns = d_a[0].shape[1]
    chunk = 256
    half = width // 2
    part = pl.BlockSpec((rows, chunk), lambda i, w: (0, i))
    out = pl.BlockSpec((2, half, chunk), lambda i, w: (0, 0, i))
    return pl.pallas_call(
        in_grads_body,
        grid_spec=pltpu.PrefetchScalarGridSpec(
            num_scalar_prefetch=1,
            grid=(columns // chunk,),
            in_specs=[pl.BlockSpec((rows, width), lambda i, w: (0, 0))] * 4 + [part] * 8,
            out_specs=[out] * 2,
            scratch_shapes=[pltpu.VMEM((width, 4 * rows), BF16)],
        ),
        out_shape=[jax.ShapeDtypeStruct((2, half, columns), BF16)] * 2,
        compiler_params=pltpu.CompilerParams(vmem_limit_bytes=30 * MEBIBYTE),
        cost_estimate=cost(1),
        name="expert_in_grads",
    )(where, *h2, *d_a, *d_b)


def down_grads_body(where_ref, *refs):
    send_refs, keep_refs, dy_refs = refs[:4], refs[4:8], refs[8:12]
    for lefts, out in ((send_refs, refs[12]), (keep_refs, refs[13])):
        total = dot_tn(lefts[0][...], dy_refs[0][...])
        for j in range(1, 4):
            total = total + dot_tn(lefts[j][...], dy_refs[j][...])
        out[...] = total.astype(BF16)


def expert_down_grads(where, acts, dy_routes):
    rows, columns = acts[0].shape
    width = dy_routes[0].shape[1] - LANES
    half = columns // 4
    out = pl.BlockSpec((half, width), lambda e, w: (e, 0))
    return pl.pallas_call(
        down_grads_body,
        grid_spec=pltpu.PrefetchScalarGridSpec(
            num_scalar_prefetch=1,
            grid=(2,),
            in_specs=[pl.BlockSpec((rows, half), lambda e, w: (0, 2 * e + 1 - w[0]))] * 4
            + [pl.BlockSpec((rows, half), lambda e, w: (0, 2 * e + w[0]))] * 4
            + [pl.BlockSpec((rows, width), lambda e, w: (0, 0))] * 4,
            out_specs=[out, out],
        ),
        out_shape=[jax.ShapeDtypeStruct((2 * half, width), BF16)] * 2,
        compiler_params=pltpu.CompilerParams(vmem_limit_bytes=26 * MEBIBYTE),
        cost_estimate=cost(20),
        name="expert_down_grads",
    )(where, *acts, *acts, *dy_routes)


class PlaneSum:
    def __init__(self, pieces, order):
        self.shape = pieces.shape[1:]
        self.order = order
        self.axes = [4, 2, 1]
        self.kept = pieces.reshape((2, 2, 2) + self.shape)
        self.step = 0
        self.send()

    def send(self):
        if self.step < 3:
            at = self.axes.index(self.order[self.step])
            self.mine = lax.index_in_dim(self.kept, 0, at, keepdims=False)
            other = lax.index_in_dim(self.kept, 1, at, keepdims=False)
            self.received = swap(other, self.order[self.step], 0)
        else:
            self.received = swap(self.kept, self.order[5 - self.step], 0)

    def receive(self, token):
        received = after(self.received, token)
        if self.step < 3:
            self.kept = (self.mine.astype(F32) + received.astype(F32)).astype(BF16)
            self.axes.remove(self.order[self.step])
        else:
            bit = self.order[5 - self.step]
            if self.step == 5:
                self.done = (self.kept.reshape((4,) + self.shape), received.reshape((4,) + self.shape))
                return received
            at = sum(1 for b in self.axes if b > bit)
            self.kept = jnp.stack([self.kept, received], at)
            self.axes = sorted(self.axes + [bit], reverse=True)
        self.step += 1
        self.send()
        return self.kept


def reorder_body(where_ref, even_ref, odd_ref, out_ref, *, first):
    for b in range(N_EXPERT):
        place = where_ref[0] ^ b
        low = place % first
        index = (place // (2 * first)) * first + low
        odd = (place // first) % 2

        @pl.when(odd == 0)
        def _(b=b, index=index):
            out_ref[b] = even_ref[index].astype(F32)

        @pl.when(odd == 1)
        def _(b=b, index=index):
            out_ref[b] = odd_ref[index].astype(F32)


def reorder(where, even, odd, columns, first):
    deep, width = even.shape[1:]
    results = []
    begin = 0
    for count in columns:
        wide = min(count, 512)
        start = begin // wide
        spec = pl.BlockSpec((N_EXPERT // 2, deep, wide), lambda i, w, start=start: (0, 0, start + i))
        results.append(
            pl.pallas_call(
                functools.partial(reorder_body, first=first),
                grid_spec=pltpu.PrefetchScalarGridSpec(
                    num_scalar_prefetch=1,
                    grid=(count // wide,),
                    in_specs=[spec, spec],
                    out_specs=pl.BlockSpec((N_EXPERT, deep, wide), lambda i, w: (0, 0, i)),
                ),
                out_shape=jax.ShapeDtypeStruct((N_EXPERT, deep, count), F32),
                cost_estimate=cost(2),
                name="reorder",
            )(where, even, odd).reshape(N_EXPERT * deep, count)
        )
        begin += count
    return results


def key_value_grad_body(*refs):
    lefts, rights, out_ref = refs[:4], refs[4:8], refs[8]
    rows, block = lefts[0].shape
    total = dot_tn(lefts[0][...], rights[0][:rows])
    small = rights[0][rows:, :block].astype(F32)
    for j in range(1, 4):
        total = total + dot_tn(lefts[j][...], rights[j][:rows])
        small = small + rights[j][rows:, :block].astype(F32)
    few = small.shape[0] // 2
    out_ref[:block] = total.astype(BF16)
    out_ref[block:, :block] = (small[:few] + small[few:]).astype(BF16)
    out_ref[block:, block:] = jnp.zeros_like(out_ref[block:, block:])


def key_value_grad(lefts, rights, block):
    rows = lefts[0].shape[0]
    columns = rights[0].shape[1]
    few = (rights[0].shape[0] - rows) // 2
    whole = lambda shape: pl.BlockSpec(shape, lambda i: (0, 0))
    return pl.pallas_call(
        key_value_grad_body,
        grid=(1,),
        in_specs=[whole((rows, block))] * 4 + [whole(rights[0].shape)] * 4,
        out_specs=whole((block + few, columns)),
        out_shape=jax.ShapeDtypeStruct((block + few, columns), BF16),
        cost_estimate=cost(3),
        name="key_value_grad",
    )(*lefts, *rights)


def place_body(where_ref, mine_ref, partner_ref, out_ref):
    @pl.when(pl.program_id(0) == 0)
    def _():
        out_ref[...] = mine_ref[...].astype(out_ref.dtype)

    @pl.when(pl.program_id(0) == 1)
    def _():
        out_ref[...] = partner_ref[...].astype(out_ref.dtype)


def place_halves(where, mine, partner, start, half, columns, first_column, dtype):
    wide = half // 2
    row = start // wide
    column = first_column // columns
    last = half // wide - 1

    def mine_map(h, i, w):
        return (row + jnp.where(h == 0, i, last), column)

    def partner_map(h, i, w):
        return (row + jnp.where(h == 0, 0, i), column)

    return pl.pallas_call(
        place_body,
        grid_spec=pltpu.PrefetchScalarGridSpec(
            num_scalar_prefetch=1,
            grid=(2, half // wide),
            in_specs=[
                pl.BlockSpec((wide, columns), mine_map),
                pl.BlockSpec((wide, columns), partner_map),
            ],
            out_specs=pl.BlockSpec((wide, columns), lambda h, i, w: ((w[0] ^ h) * 2 + i, 0)),
        ),
        out_shape=jax.ShapeDtypeStruct((2 * half, columns), dtype),
        cost_estimate=cost(3),
        name="place_halves",
    )(where, mine, partner)


def far_halves_body(where_ref, *refs):
    out_ref = refs[-1]
    for k, ref in enumerate(refs[:-1]):

        @pl.when(pl.program_id(0) == k)
        def _(ref=ref):
            out_ref[0] = ref[...]


def far_halves(where, own):
    hidden = own[0].shape[1]
    half = own[0].shape[0] // 2
    cuts = 2
    tall = half // cuts

    def in_map(k):
        step = lambda i, r: jnp.where(i < k, 0, jnp.where(i == k, r, cuts - 1))
        if k == 2:
            return lambda i, r, w: (step(i, r), w[0])
        return lambda i, r, w: (w[0] * cuts + step(i, r), 0)

    return pl.pallas_call(
        far_halves_body,
        grid_spec=pltpu.PrefetchScalarGridSpec(
            num_scalar_prefetch=1,
            grid=(3, cuts),
            in_specs=[pl.BlockSpec((tall, hidden), in_map(k)) for k in range(3)],
            out_specs=pl.BlockSpec((1, tall, hidden), lambda i, r, w: (i, r, 0)),
        ),
        out_shape=jax.ShapeDtypeStruct((3, half, hidden), BF16),
        cost_estimate=cost(3),
        name="far_halves",
    )(where, *own)


def pack_body(key_ref, value_ref, small_ref, out_ref):
    rows, low = key_ref.shape
    out_ref[:rows, :low] = key_ref[...]
    out_ref[:rows, low:] = value_ref[...]
    out_ref[rows:, : small_ref.shape[1]] = small_ref[...]
    out_ref[rows:, small_ref.shape[1] :] = jnp.zeros_like(out_ref[rows:, small_ref.shape[1] :])


def pack(w_key, w_value, small):
    rows, low = w_key.shape
    return pl.pallas_call(
        pack_body,
        out_shape=jax.ShapeDtypeStruct((rows + small.shape[0], 2 * low), BF16),
        cost_estimate=cost(2),
        name="pack",
    )(w_key, w_value, small)


def plus(part, received):
    return (part.astype(F32) + received.astype(F32)).astype(BF16)


def on_device_rings(
    hidden_in, segment_ids, routes, attn_gain, moe_gain, w_query, w_key, w_value, w_out, w_router,
    expert_gate, expert_up, expert_down, out_grad,
):
    rows, width = hidden_in.shape
    experts = w_router.shape[1]
    shard = lax.axis_index("shard")
    expert = lax.axis_index("expert")
    core = shard % 2
    where_shard = shard.astype(jnp.int32)[None]
    where_expert = expert.astype(jnp.int32)[None]
    where_core = core.astype(jnp.int32)[None]
    where_far_core = 1 - where_core
    block = width // N_SHARD
    low = KVH * HEAD

    own = (expert_gate[0], expert_up[0], expert_down[0])
    far_send = far_halves(where_core, own)
    far_part = swap(far_send, 1, 0)
    small = jnp.concatenate(
        [w_router.T, attn_gain[None], moe_gain[None], jnp.zeros((6, block), BF16)], 0
    )
    packed_own = pack(after(w_key, far_send), w_value, small)
    packed_y = swap(packed_own, 0, 2)
    mask = (routes[:, :, None] == jnp.arange(LANES, dtype=jnp.int32)[None, None, :]).any(1)
    dy_routes = [jnp.concatenate([out_grad, mask.astype(BF16)], 1)]
    for _ in range(3):
        dy_routes.append(next_plane(dy_routes[-1]))
    query_w_core = swap(w_query, 0, 1)
    query_w_y = swap(after(w_query, packed_y), 0, 2)
    packed_pair = swap(jnp.concatenate([packed_own, packed_y], 0), 0, 1)
    tall = packed_own.shape[0]
    packed = [packed_own, packed_pair[:tall], packed_y, packed_pair[tall:]]

    inputs = hidden_in.astype(F32)
    factor_attn = lax.rsqrt(jnp.mean(inputs * inputs, -1, keepdims=True) + EPSILON)
    unit_rel = jnp.concatenate(
        xor_blocks([inputs[:, j * block : (j + 1) * block] for j in range(4)], shard), 1
    ) * factor_attn
    gain_rel = jnp.concatenate([member[block + experts : block + experts + 1, :block] for member in packed], 1)
    gain_rel = gain_rel.astype(F32)
    h1_rel = after((unit_rel * gain_rel).astype(BF16), query_w_core)
    key_value_w = [member[:block] for member in packed]
    pre = sum(dot_nn(h1_rel[:, j * block : (j + 1) * block], key_value_w[j]) for j in range(4))
    positions = shard * rows + jnp.arange(rows, dtype=jnp.int32)
    cosine, sine = rope_tables(positions, HEAD)
    key_local = rotate(pre[:, :low], cosine, sine, HEAD)
    key_value = jnp.concatenate([key_local, pre[:, low:]], 1).astype(BF16)
    key_value = after(key_value, dy_routes[1])
    key_value_y = swap(key_value, 0, 2)
    query_w = [w_query, query_w_core, query_w_y, swap(query_w_y, 0, 1)]
    key_value_pair = swap(jnp.concatenate([key_value, key_value_y], 0), 0, 1)
    keys_values = jnp.concatenate(
        xor_blocks([key_value, key_value_pair[:rows], key_value_y, key_value_pair[rows:]], shard), 0
    )
    out_w_y = swap(after(w_out, query_w_y, key_value), 0, 2)
    out_w_core = swap(after(w_out, query_w_y), 0, 1)
    cosine_row = jnp.concatenate([cosine, cosine], 1)
    sine_row = jnp.concatenate([-sine, sine], 1)
    seg_query = lax.dynamic_slice_in_dim(segment_ids, shard * rows, rows)[:, None]
    queries, probs, attended = attention_forward(
        where_shard, after(h1_rel, out_w_core, dy_routes[2]), query_w, keys_values, cosine_row, sine_row, seg_query, segment_ids[None, :]
    )
    attended_late = after(attended, dy_routes[3])
    out_w_y = after(out_w_y, attended)
    out_w = [w_out, out_w_core, out_w_y, swap(out_w_y, 0, 1)]
    mid_state = inputs + sum(
        dot_nn(attended_late[:, j * block : (j + 1) * block], out_w[j]) for j in range(4)
    )
    factor_moe = lax.rsqrt(jnp.mean(mid_state * mid_state, -1, keepdims=True) + EPSILON)
    unit_moe = mid_state * factor_moe
    small_true = jnp.concatenate(xor_blocks([member[block:, :block] for member in packed], shard), 1)
    gain_moe = small_true[experts + 1 : experts + 2].astype(F32)
    router = small_true[:experts].astype(F32)
    h2 = [(unit_moe * gain_moe).astype(BF16)]

    far_part = after(far_part, attended)
    far_other = swap(far_part, 0, 1)
    hidden = own[0].shape[1]
    deep = width // 2
    far = (far_part, far_other)
    where_pair = jnp.stack([expert, core]).astype(jnp.int32)

    mixer_rows = [
        jnp.concatenate([h1_rel[:, j * block : (j + 1) * block], attended[:, j * block : (j + 1) * block]], 1)
        for j in range(4)
    ]
    mixer_rows = [mixer_rows[0]] + [swap(mixer_rows[j], 0, j) for j in (1, 2, 3)]
    add = lambda a, b: (a.astype(F32) + b.astype(F32)).astype(BF16)
    block_of = lambda j, *ready: expert_block(
        where_pair, after(h2[j], *ready), dy_routes[j], small_true, own, far
    )
    h2.append(next_plane(h2[0]))
    done = [block_of(0)]
    h2.append(next_plane(after(h2[1], done[0][0])))
    done.append(block_of(1, done[0][0], *mixer_rows))
    h2.append(next_plane(after(h2[2], done[1][0])))
    message = next_plane(done[1][0])
    done.append(block_of(2, done[1][0]))
    second = add(done[2][0], message)
    message = next_plane(second)
    done.append(block_of(3, second))
    third = add(done[3][0], message)
    message = next_plane(third)
    acts = [done[j][4] for j in range(4)]
    down_send, down_keep = expert_down_grads(after(where_core, third), acts, dy_routes)
    in_send, in_keep = expert_in_grads(
        after(where_core, down_send), h2, [done[j][2] for j in range(4)], [done[j][3] for j in range(4)]
    )
    down_swap = swap(down_send, 0, 1)
    in_swap = swap(in_send, 0, 1)
    message, down_swap, _ = together(message, down_swap, in_send)
    down_half = hidden // 2
    down_far = plus(down_keep[down_half:], down_swap[down_half:])
    down_received = swap(down_far, 1, 0)
    message = after(message, down_far)
    mixed = next_plane(after(done[1][1], message))
    total = done[0][0].astype(F32) + message.astype(F32)
    named = mask[:, :experts]
    logits = jnp.where(named, dot_nt(h2[0], small_true[:experts]), MASKED_SCORE)
    weights = jnp.where(named, jnp.exp(logits - jnp.max(logits, -1, keepdims=True)), 0.0)
    gate = weights / jnp.sum(weights, -1, keepdims=True)
    gate_grad = total[:, width : width + experts] + total[:, width + experts : width + 2 * experts]
    d_logits = gate * (gate_grad - jnp.sum(gate * gate_grad, -1, keepdims=True))
    d_h2 = total[:, :width] + jnp.dot(d_logits, router, precision=HIGHEST)
    router_grad = jnp.dot(d_logits.T, h2[0].astype(F32), precision=HIGHEST)
    d_mid_norm, gain_moe_grad = norm_backward(d_h2, unit_moe, factor_moe, gain_moe)
    d_mid = out_grad.astype(F32) + d_mid_norm
    d_branch = d_mid.astype(BF16)
    branch_core = swap(d_branch, 0, 1)
    branch_y = swap(d_branch, 0, 2)
    branches = [d_branch, branch_core, branch_y, swap(branch_y, 0, 1)]

    def mixer_grads(half, rights, name):
        n = rights[0].shape[1]
        (pieces,) = summed_products(
            where_expert, mixer_rows, [rights], (1,),
            pl.BlockSpec((rows, block), lambda i, w: (0, half)),
            pl.BlockSpec((rows, n), lambda i, w: (0, 0)),
            pl.BlockSpec((N_EXPERT, block // N_EXPERT, n), lambda i, w: (0, 0, 0)),
            (N_EXPERT, block // N_EXPERT, n), name,
        )
        return pieces

    d_q_pre, d_key_part, d_value_part, d_normed = attention_backward(
        where_shard, d_branch, out_w, attended, queries, probs, keys_values, query_w, cosine_row, sine_row
    )
    d_q_pre, d_key_part, d_value_part, branch_y, branch_core, in_swap, mixed = together(
        d_q_pre, d_key_part, d_value_part, branch_y, branch_core, in_swap, mixed
    )
    d_q_y = swap(d_q_pre, 0, 2)
    d_q_core = swap(d_q_pre, 0, 1)
    branch_far = swap(branch_y, 0, 1)
    d_parts = jnp.concatenate([d_key_part, d_value_part], 1).reshape(N_SHARD, rows, 2 * low)
    d_rel = xor_blocks([d_parts[j] for j in range(4)], shard)
    from_core = swap(jnp.stack([d_rel[1], d_rel[3]]), 0, 1)
    gate_far = plus(in_keep[0, :, hidden:], in_swap[0, :, hidden:])
    up_far = plus(in_keep[1, :, hidden:], in_swap[1, :, hidden:])
    mixed = add(done[2][1], mixed)

    d_q_core, branch_far, from_core, down_received, gate_far, up_far, mixed = together(
        d_q_core, branch_far, from_core, down_received, gate_far, up_far, mixed
    )
    gate_received = swap(gate_far, 1, 0)
    mixed = next_plane(mixed)
    d_far = add(d_rel[2], from_core[1])
    d_far_y = swap(d_far, 0, 2)
    down_part = plus(down_keep[:down_half].astype(F32) + down_swap[:down_half].astype(F32), down_received)
    out_pieces = mixer_grads(1, [d_branch, branch_core, branch_y, after(branch_far, down_part)], "w_out_grad")

    d_q_y, out_pieces = together(d_q_y, out_pieces)
    query_pieces = mixer_grads(0, [d_q_pre, d_q_core, d_q_y, swap(d_q_y, 0, 1)], "w_query_grad")

    query_pieces, d_far_y, mixed = together(query_pieces, d_far_y, mixed)
    query_sum = PlaneSum(query_pieces, (1, 2, 4))
    out_sum = PlaneSum(after(out_pieces, query_pieces), (1, 2, 4))
    down_y = swap(after(down_part, query_pieces), 0, 2)
    mixed = add(done[3][1], mixed)
    mixed = next_plane(mixed)
    d_key_value = d_rel[0].astype(F32) + from_core[0].astype(F32) + d_far_y.astype(F32)
    d_k_pre = rotate(d_key_value[:, :low], cosine, -sine, HEAD)
    d_kv_pre = jnp.concatenate([d_k_pre, d_key_value[:, low:]], 1).astype(BF16)

    d_normed = d_normed + jnp.concatenate([dot_nt(d_kv_pre, member) for member in key_value_w], 1)
    d_input_norm, gain_attn_grad = norm_backward(d_normed, unit_rel, factor_attn, gain_rel)
    d_input_norm = jnp.concatenate(
        xor_blocks([d_input_norm[:, j * block : (j + 1) * block] for j in range(4)], shard), 1
    )
    input_grad = d_mid + d_input_norm

    rest = jnp.concatenate([gain_moe_grad[None], router_grad, jnp.zeros((6, width), F32)], 0)
    rest = xor_blocks([rest[:, j * block : (j + 1) * block] for j in range(4)], shard)
    notes = []
    for j in range(4):
        piece = jnp.concatenate([gain_attn_grad[None, j * block : (j + 1) * block], rest[j]], 0)
        high = piece.astype(BF16)
        piece = jnp.concatenate([high, (piece - high.astype(F32)).astype(BF16)], 0)
        notes.append(jnp.concatenate([d_kv_pre, jnp.pad(piece, ((0, 0), (0, 2 * low - block)))], 0))
    notes_y = swap(jnp.concatenate([notes[2], notes[3]], 0), 0, 2)
    tall = notes[0].shape[0]

    gate_own = in_keep[0, :, :hidden].astype(F32) + in_swap[0, :, :hidden].astype(F32)
    gate_part = plus(gate_own, after(gate_received, notes[0]))
    down_total = plus(down_part, after(down_y, gate_part))
    up_received = swap(after(up_far, down_total), 1, 0)
    gate_y = swap(after(gate_part, down_total), 0, 2)
    layer_out = (mid_state + done[0][1].astype(F32) + after(mixed, down_total).astype(F32)).astype(BF16)
    token = query_sum.receive(layer_out)
    token = query_sum.receive(token)
    notes_y = after(notes_y, token)
    notes_core = swap(jnp.concatenate([notes[1], notes_y[tall:]], 0), 0, 1)
    token = out_sum.receive(notes_y)
    last = key_value_grad(
        mixer_rows, [notes[0], notes_core[:tall], after(notes_y[:tall], token), notes_core[tall:]], block
    )
    last_z = swap(last, 2, 0)
    down_core = swap(after(down_total, last), 0, 1)
    token = query_sum.receive(last)
    token = out_sum.receive(token)
    down_sum = place_halves(where_core, down_total, after(down_core, token), 0, hidden // 2, width, 0, F32)[None]
    token = query_sum.receive(down_sum)
    up_own = in_keep[1, :, :hidden].astype(F32) + in_swap[1, :, :hidden].astype(F32)
    up_part = plus(up_own, after(up_received, token))
    up_y = swap(up_part, 0, 2)
    token = out_sum.receive(up_part)
    gate_total = plus(gate_part, after(gate_y, token))
    gate_core = swap(gate_total, 0, 1)
    last = plus(last, after(last_z, gate_total))
    token = query_sum.receive(last)
    token = out_sum.receive(token)
    last_z = swap(after(last, token), 4, 0)
    gate_sum = place_halves(where_core, gate_total, after(gate_core, token), 0, deep, hidden, 0, F32)[None]
    token = out_sum.receive(gate_sum)
    token = query_sum.receive(token)
    (query_grad,) = reorder(where_expert, *query_sum.done, (width,), query_sum.order[0])
    up_total = plus(up_part, after(up_y, token))
    up_core = swap(up_total, 0, 1)
    last = plus(last, after(last_z, up_total))
    last_x = swap(last, 1, 0)
    up_sum = place_halves(where_core, up_total, after(up_core, last), 0, deep, hidden, 0, F32)[None]
    token = out_sum.receive(up_sum)
    (out_w_grad,) = reorder(where_expert, *out_sum.done, (width,), out_sum.order[0])
    last = last.astype(F32) + after(last_x, token).astype(F32)
    small_sums = last[block:, :block]
    return (
        layer_out,
        input_grad,
        small_sums[0],
        small_sums[1],
        query_grad,
        last[:block, :low],
        last[:block, low:],
        out_w_grad,
        small_sums[2 : 2 + experts].T,
        gate_sum,
        up_sum,
        down_sum,
    )


def on_device(hidden_in, segment_ids, routes, *rest):
    rows = hidden_in.shape[0]
    experts = rest[6].shape[1]
    capacity = rows * routes.shape[1] * 2 // experts
    shape = (lax.axis_size("expert"), lax.axis_size("shard"))
    if shape == (N_EXPERT, N_SHARD) and experts == N_EXPERT and capacity == rows:
        return on_device_rings(hidden_in, segment_ids, routes, *rest)
    return on_device_routed(hidden_in, segment_ids, routes, *rest)


def solution(mesh):
    placed = (
        P(("expert", "shard"), None),
        P("expert"),
        P(("expert", "shard"), None),
        P("shard"),
        P("shard"),
        P("shard", None),
        P("shard", None),
        P("shard", None),
        P("shard", None),
        P("shard", None),
        P("expert", None, None),
        P("expert", None, None),
        P("expert", None, None),
        P(("expert", "shard"), None),
    )
    return jax.shard_map(
        on_device,
        mesh=mesh,
        in_specs=placed,
        out_specs=(
            P(("expert", "shard"), None),
            P(("expert", "shard"), None),
            P("shard"),
            P("shard"),
            P("shard", None),
            P("shard", None),
            P("shard", None),
            P("shard", None),
            P("shard", None),
            P("expert", None, None),
            P("expert", None, None),
            P("expert", None, None),
        ),
        check_vma=False,
    )
```

```python
import functools
import types

import jax
import jax.numpy as jnp
from jax import lax
from jax.experimental import pallas as pl
from jax.experimental.pallas import tpu as pltpu
from jax.sharding import PartitionSpec as P

HQ = 12
KVH = 2
HEAD = 128


EPSILON = 1e-06
ROPE_BASE = 10000.0
MASKED_SCORE = -1e30
HIGHEST = lax.Precision.HIGHEST


def rope_tables(positions, head_size):
    half_size = head_size // 2
    frequency = ROPE_BASE ** (-(jnp.arange(half_size, dtype=jnp.float32) * 2.0 / head_size))
    angles = positions.astype(jnp.float32)[:, None] * frequency[None, :]
    return (jnp.cos(angles), jnp.sin(angles))


def rotate(values, cosine_table, sine_table, head_size):
    rows_count = values.shape[0]
    shaped = values.reshape(rows_count, -1, head_size)
    half_size = head_size // 2
    first_half = shaped[..., :half_size]
    second_half = shaped[..., half_size:]
    cosine_part = cosine_table[:, None, :]
    sine_part = sine_table[:, None, :]
    turned = jnp.concatenate(
        [
            first_half * cosine_part - second_half * sine_part,
            second_half * cosine_part + first_half * sine_part,
        ],
        -1,
    )
    return turned.reshape(rows_count, -1)


def norm_forward(values, gain):
    factor = lax.rsqrt(jnp.mean(values * values, -1, keepdims=True) + EPSILON)
    unit_rows = values * factor
    return (unit_rows, factor, (unit_rows * gain).astype(jnp.bfloat16))


def norm_backward(grad_rows, unit_rows, factor, gain):
    gain_grad = jnp.sum(grad_rows * unit_rows, 0)
    scaled_grad = grad_rows * gain
    return (
        factor * (scaled_grad - unit_rows * jnp.mean(scaled_grad * unit_rows, -1, keepdims=True)),
        gain_grad,
    )


def score_block(query_heads, key_heads, visible, score_scale):
    raw_scores = jnp.einsum(
        "tkgd,skd->kgts", query_heads, key_heads, preferred_element_type=jnp.float32
    )
    return jnp.where(visible, raw_scores * score_scale, MASKED_SCORE)


def on_device_routed(
    hidden_in,
    segment_ids,
    routes,
    attn_gain,
    moe_gain,
    w_query,
    w_key,
    w_value,
    w_out,
    w_router,
    expert_gate,
    expert_up,
    expert_down,
    out_grad,
):
    tok_rows = hidden_in.shape[0]
    top_count = routes.shape[1]
    experts = w_router.shape[1]
    capacity = tok_rows * top_count * 2 // experts
    groups = HQ // KVH
    score_scale = HEAD ** (-0.5)
    shard_index = lax.axis_index("shard")
    n_expert = lax.axis_size("expert")
    local_experts = expert_gate.shape[0]
    gain_attn, gain_moe, query_w, key_w, value_w, out_w, router_w = (
        lax.all_gather(attn_gain, "shard", axis=0, tiled=True),
        lax.all_gather(moe_gain, "shard", axis=0, tiled=True),
        lax.all_gather(w_query, "shard", axis=0, tiled=True),
        lax.all_gather(w_key, "shard", axis=0, tiled=True),
        lax.all_gather(w_value, "shard", axis=0, tiled=True),
        lax.all_gather(w_out, "shard", axis=0, tiled=True),
        lax.all_gather(w_router, "shard", axis=0, tiled=True),
    )
    gain_attn = gain_attn.astype(jnp.float32)
    gain_moe = gain_moe.astype(jnp.float32)
    inputs = hidden_in.astype(jnp.float32)
    unit_attn, factor_attn, normed = norm_forward(inputs, gain_attn)
    q_pre = jnp.dot(normed, query_w, preferred_element_type=jnp.float32)
    k_pre = jnp.dot(normed, key_w, preferred_element_type=jnp.float32)
    value_rows = jnp.dot(normed, value_w, preferred_element_type=jnp.float32).astype(jnp.bfloat16)
    positions = shard_index * tok_rows + jnp.arange(tok_rows, dtype=jnp.int32)
    cosine_table, sine_table = rope_tables(positions, HEAD)
    queries = rotate(q_pre, cosine_table, sine_table, HEAD).astype(jnp.bfloat16)
    key_local = rotate(k_pre, cosine_table, sine_table, HEAD).astype(jnp.bfloat16)
    key_rows, value_all = (
        lax.all_gather(key_local, "shard", axis=0, tiled=True),
        lax.all_gather(value_rows, "shard", axis=0, tiled=True),
    )
    seq_len = key_rows.shape[0]
    query_heads = queries.reshape(tok_rows, KVH, groups, HEAD)
    key_heads = key_rows.reshape(seq_len, KVH, HEAD)
    value_heads = value_all.reshape(seq_len, KVH, HEAD)
    seg_local = lax.dynamic_slice_in_dim(segment_ids, shard_index * tok_rows, tok_rows)
    visible = (positions[:, None] >= jnp.arange(seq_len, dtype=jnp.int32)[None, :]) & (
        seg_local[:, None] == segment_ids[None, :]
    )
    score_values = score_block(query_heads, key_heads, visible, score_scale)
    top_score = jnp.max(score_values, -1, keepdims=True)
    exponent = jnp.exp(score_values - top_score)
    denominators = jnp.sum(exponent, -1, keepdims=True)
    probabilities = exponent / denominators
    log_total = top_score + jnp.log(denominators)
    attended = (
        jnp.einsum(
            "kgts,skd->tkgd",
            probabilities.astype(jnp.bfloat16),
            value_heads,
            preferred_element_type=jnp.float32,
        )
        .reshape(tok_rows, -1)
        .astype(jnp.bfloat16)
    )
    mid_state = inputs + jnp.dot(attended, out_w, preferred_element_type=jnp.float32)
    unit_moe, factor_moe, normed_moe = norm_forward(mid_state, gain_moe)
    logits = jnp.dot(normed_moe, router_w, preferred_element_type=jnp.float32)
    onehot = (routes[:, :, None] == jnp.arange(experts, dtype=jnp.int32)[None, None, :]).astype(
        jnp.float32
    )
    chosen = jnp.sum(onehot * logits[:, None, :], -1)
    chosen = chosen - jnp.max(chosen, -1, keepdims=True)
    weights = jnp.exp(chosen)
    gate = weights / jnp.sum(weights, -1, keepdims=True)
    flat_routes = routes.reshape(-1)
    route_hot = (flat_routes[:, None] == jnp.arange(experts, dtype=jnp.int32)[None, :]).astype(
        jnp.int32
    )
    before = jnp.cumsum(route_hot, 0, dtype=jnp.int32) - route_hot
    slot_id = flat_routes * capacity + jnp.sum(before * route_hot, 1, dtype=jnp.int32)
    source = (
        jnp.zeros((experts * capacity,), jnp.int32)
        .at[slot_id]
        .set(jnp.arange(tok_rows * top_count, dtype=jnp.int32))
    )
    filled = jnp.zeros((experts * capacity,), jnp.bool_).at[slot_id].set(True)
    outgoing = jnp.where(filled[:, None], jnp.take(normed_moe, source // top_count, axis=0), 0)
    outgoing = outgoing.reshape(experts, capacity, -1)
    arrived = lax.all_to_all(outgoing, "expert", split_axis=0, concat_axis=0, tiled=True)
    item_count = arrived.shape[1]
    shaped = arrived.reshape(n_expert, local_experts, item_count, -1)
    gate_pre = jnp.einsum("nlcd,ldf->nlcf", shaped, expert_gate, preferred_element_type=jnp.float32)
    up_pre = jnp.einsum("nlcd,ldf->nlcf", shaped, expert_up, preferred_element_type=jnp.float32)
    hidden_rows = (gate_pre * jax.nn.sigmoid(gate_pre) * up_pre).astype(jnp.bfloat16)
    result = jnp.einsum(
        "nlcf,lfd->nlcd", hidden_rows, expert_down, preferred_element_type=jnp.float32
    )
    result = result.astype(jnp.bfloat16).reshape(arrived.shape)
    returned = lax.all_to_all(result, "expert", split_axis=0, concat_axis=0, tiled=True)
    outcome = (
        returned,
        arrived,
        gate_pre.reshape(n_expert * local_experts, item_count, -1),
        up_pre.reshape(n_expert * local_experts, item_count, -1),
        hidden_rows.reshape(n_expert * local_experts, item_count, -1),
    )
    returned_rows = jnp.take(outcome[0].reshape(experts * capacity, -1), slot_id, axis=0).reshape(
        tok_rows, top_count, -1
    )
    mixed = mid_state + jnp.sum(gate[:, :, None] * returned_rows, 1)
    layer_out = mixed.astype(jnp.bfloat16)
    grad_out = out_grad.astype(jnp.float32)
    gate_grad = jnp.sum(returned_rows * grad_out[:, None, :], -1)
    gate_slots = jnp.take(gate.reshape(-1), source, axis=0)
    d_send = jnp.where(
        filled[:, None], jnp.take(grad_out, source // top_count, axis=0) * gate_slots[:, None], 0.0
    )
    d_send = d_send.astype(jnp.bfloat16).reshape(experts, capacity, -1)
    d_arrived = lax.all_to_all(d_send, "expert", split_axis=0, concat_axis=0, tiled=True)
    d_shaped = d_arrived.reshape(n_expert, local_experts, capacity, -1)
    arrived_rows = outcome[1].reshape(n_expert, local_experts, capacity, -1)
    gate_pre = outcome[2].reshape(n_expert, local_experts, capacity, -1)
    up_pre = outcome[3].reshape(n_expert, local_experts, capacity, -1)
    hidden_rows = outcome[4].reshape(n_expert, local_experts, capacity, -1)
    sigmoid_gate = jax.nn.sigmoid(gate_pre)
    d_hidden = jnp.einsum(
        "nlcd,lfd->nlcf", d_shaped, expert_down, preferred_element_type=jnp.float32
    )
    down_grad = jnp.einsum(
        "nlcf,nlcd->lfd", hidden_rows, d_shaped, preferred_element_type=jnp.float32
    )
    d_gate = (d_hidden * up_pre * sigmoid_gate * (1.0 + gate_pre * (1.0 - sigmoid_gate))).astype(
        jnp.bfloat16
    )
    d_up = (d_hidden * gate_pre * sigmoid_gate).astype(jnp.bfloat16)
    gate_w_grad = jnp.einsum(
        "nlcd,nlcf->ldf", arrived_rows, d_gate, preferred_element_type=jnp.float32
    )
    up_w_grad = jnp.einsum("nlcd,nlcf->ldf", arrived_rows, d_up, preferred_element_type=jnp.float32)
    d_rows = jnp.einsum("nlcf,ldf->nlcd", d_gate, expert_gate, preferred_element_type=jnp.float32)
    d_rows = d_rows + jnp.einsum(
        "nlcf,ldf->nlcd", d_up, expert_up, preferred_element_type=jnp.float32
    )
    d_rows = d_rows.astype(jnp.bfloat16).reshape(experts, capacity, -1)
    d_returned = lax.all_to_all(d_rows, "expert", split_axis=0, concat_axis=0, tiled=True)
    expert_sums = (
        lax.psum(gate_w_grad.astype(jnp.bfloat16), "shard").astype(jnp.float32),
        lax.psum(up_w_grad.astype(jnp.bfloat16), "shard").astype(jnp.float32),
        lax.psum(down_grad.astype(jnp.bfloat16), "shard").astype(jnp.float32),
    )
    d_copies = jnp.take(d_returned.reshape(experts * capacity, -1), slot_id, axis=0).reshape(
        tok_rows, top_count, -1
    )
    d_normed_moe = jnp.sum(d_copies, 1, dtype=jnp.float32)
    d_chosen = gate * (gate_grad - jnp.sum(gate * gate_grad, -1, keepdims=True))
    d_logits = jnp.sum(onehot * d_chosen[:, :, None], 1)
    router_f32 = router_w.astype(jnp.float32)
    d_normed_moe = d_normed_moe + jnp.dot(d_logits, router_f32.T, precision=HIGHEST)
    router_grad = jnp.dot(normed_moe.astype(jnp.float32).T, d_logits, precision=HIGHEST)
    d_mid_norm, gain_moe_grad = norm_backward(d_normed_moe, unit_moe, factor_moe, gain_moe)
    d_mid = grad_out + d_mid_norm
    d_branch = d_mid.astype(jnp.bfloat16)
    out_w_grad = jnp.dot(attended.T, d_branch, preferred_element_type=jnp.float32)
    d_attended = jnp.dot(d_branch, out_w.T, preferred_element_type=jnp.float32).astype(jnp.bfloat16)
    d_attended = d_attended.reshape(tok_rows, KVH, groups, HEAD)
    score_again = score_block(query_heads, key_heads, visible, score_scale)
    prob_again = jnp.exp(score_again - log_total)
    d_probs = jnp.einsum(
        "tkgd,skd->kgts", d_attended, value_heads, preferred_element_type=jnp.float32
    )
    d_scores = (
        prob_again * (d_probs - jnp.sum(prob_again * d_probs, -1, keepdims=True)) * score_scale
    )
    d_scores = d_scores.astype(jnp.bfloat16)
    d_query = jnp.einsum(
        "kgts,skd->tkgd", d_scores, key_heads, preferred_element_type=jnp.float32
    ).reshape(tok_rows, -1)
    d_key_part = jnp.einsum(
        "kgts,tkgd->skd", d_scores, query_heads, preferred_element_type=jnp.float32
    ).reshape(seq_len, -1)
    d_value_part = jnp.einsum(
        "kgts,tkgd->skd",
        prob_again.astype(jnp.bfloat16),
        d_attended,
        preferred_element_type=jnp.float32,
    ).reshape(seq_len, -1)
    d_keys, d_values = (
        lax.psum_scatter(
            d_key_part.astype(jnp.bfloat16), "shard", scatter_dimension=0, tiled=True
        ).astype(jnp.float32),
        lax.psum_scatter(
            d_value_part.astype(jnp.bfloat16), "shard", scatter_dimension=0, tiled=True
        ).astype(jnp.float32),
    )
    d_q_pre = rotate(d_query, cosine_table, -sine_table, HEAD).astype(jnp.bfloat16)
    d_k_pre = rotate(d_keys, cosine_table, -sine_table, HEAD).astype(jnp.bfloat16)
    d_v_pre = d_values.astype(jnp.bfloat16)
    query_grad = jnp.dot(normed.T, d_q_pre, preferred_element_type=jnp.float32)
    key_grad = jnp.dot(normed.T, d_k_pre, preferred_element_type=jnp.float32)
    value_grad = jnp.dot(normed.T, d_v_pre, preferred_element_type=jnp.float32)
    d_normed = jnp.dot(d_q_pre, query_w.T, preferred_element_type=jnp.float32)
    d_normed = d_normed + jnp.dot(d_k_pre, key_w.T, preferred_element_type=jnp.float32)
    d_normed = d_normed + jnp.dot(d_v_pre, value_w.T, preferred_element_type=jnp.float32)
    d_input_norm, gain_attn_grad = norm_backward(d_normed, unit_attn, factor_attn, gain_attn)
    input_grad = d_mid + d_input_norm
    partial_sums = (
        gain_attn_grad,
        gain_moe_grad,
        query_grad,
        key_grad,
        value_grad,
        out_w_grad,
        router_grad,
    )
    summed = lax.psum(
        (
            partial_sums[0],
            partial_sums[1],
            partial_sums[2],
            partial_sums[3],
            partial_sums[4],
            partial_sums[5],
            partial_sums[6],
        ),
        ("expert", "shard"),
    )
    n_shard = lax.axis_size("shard")
    owned_grads = tuple(
        (
            lax.dynamic_slice_in_dim(
                member, shard_index * (member.shape[0] // n_shard), member.shape[0] // n_shard, 0
            )
            for member in summed
        )
    )
    return (
        layer_out,
        input_grad,
        owned_grads[0],
        owned_grads[1],
        owned_grads[2],
        owned_grads[3],
        owned_grads[4],
        owned_grads[5],
        owned_grads[6],
        expert_sums[0],
        expert_sums[1],
        expert_sums[2],
    )


AXES = ("expert", "shard")
N_EXPERT = 8
N_SHARD = 4
LANES = 128
MEBIBYTE = 1 << 20
BF16 = jnp.bfloat16
F32 = jnp.float32


COST_ATTENTION = 17
COST_IN = 1
COST_DOWN = 20
COST_PLACE = 3
COST_PRODUCTS = 5
OUT_BITS = (1, 2, 4)
QUERY_BITS = (1, 2, 4)
LAST_BITS = (2, 4, 1)
EVENTS = (
    "first_far", "branch", "mixed_0", "attention", "sync_1", "sync_2", "sync_3", "sync_4", "key_value", "mixed_2",
    "out", "norms", "first_part", "first_send", "query", "layer", "out", "up_far", "up_send", "query", "out",
    "notes", "query", "out", "last_grads", "query", "out", "up_part", "query", "last_1", "first_total", "out",
    "down_place", "gate_place", "last_2", "query", "up_total", "out_place", "query_place", "last_3", "up_place",
)


def cost(microseconds):
    return pl.CostEstimate(flops=microseconds * 10**9, bytes_accessed=10**5, transcendentals=0)


def swap(values, expert_bits, shard_bits):
    pairs = [
        (e * N_SHARD + s, (e ^ expert_bits) * N_SHARD + (s ^ shard_bits))
        for e in range(N_EXPERT)
        for s in range(N_SHARD)
    ]
    return lax.ppermute(values, AXES, pairs)


def next_plane(values):
    pairs = [
        (e * N_SHARD + s, ((e + 2) % N_EXPERT) * N_SHARD + s)
        for e in range(N_EXPERT)
        for s in range(N_SHARD)
    ]
    return lax.ppermute(values, AXES, pairs)


def gather_shards(values):
    other_core = swap(values, 0, 1)
    other_y = swap(values, 0, 2)
    return [values, other_core, other_y, swap(other_y, 0, 1)]


def xor_blocks(blocks, index):
    odd = (index & 1) == 1
    high = (index & 2) == 2
    once = [jnp.where(odd, blocks[j ^ 1], blocks[j]) for j in range(4)]
    return [jnp.where(high, once[j ^ 2], once[j]) for j in range(4)]


def together(*values):
    return lax.optimization_barrier(values)


def after(value, *others):
    return lax.optimization_barrier((value,) + others)[0]


def rejoin(mine, partner, low_first):
    return jnp.where(
        low_first,
        jnp.concatenate([mine, partner], 0),
        jnp.concatenate([partner, mine], 0),
    )


def dot_nn(left, right):
    return lax.dot_general(left, right, (((1,), (0,)), ((), ())), preferred_element_type=F32)


def dot_nt(left, right):
    return lax.dot_general(left, right, (((1,), (1,)), ((), ())), preferred_element_type=F32)


def dot_tn(left, right):
    return lax.dot_general(left, right, (((0,), (0,)), ((), ())), preferred_element_type=F32)


def turn(values, cosine, sine):
    return values * cosine + pltpu.roll(values, HEAD // 2, 1) * sine


def attention_forward_body(
    where_ref, h1_ref, w0, w1, w2, w3, key_ref, value_ref, cos_ref, sin_ref, segq_ref, segk_ref,
    query_out, prob_out, attended_out, bias_ref,
):
    rows, seq_len = bias_ref.shape

    @pl.when(pl.program_id(0) == 0)
    def _():
        base = where_ref[0] * rows
        query_pos = base + lax.broadcasted_iota(jnp.int32, (rows, seq_len), 0)
        key_pos = lax.broadcasted_iota(jnp.int32, (rows, seq_len), 1)
        visible = (query_pos >= key_pos) & (segq_ref[...] == segk_ref[...])
        bias_ref[...] = jnp.where(visible, 0.0, MASKED_SCORE)

    depth = w0.shape[0]
    pre = dot_nn(h1_ref[:, :depth], w0[...])
    for j, weight in enumerate((w1, w2, w3)):
        pre = pre + dot_nn(h1_ref[:, (j + 1) * depth : (j + 2) * depth], weight[...])
    for h in range(pre.shape[1] // HEAD):
        cols = slice(h * HEAD, (h + 1) * HEAD)
        query = turn(pre[:, cols], cos_ref[...], sin_ref[...]).astype(BF16)
        query_out[:, cols] = query
        scores = dot_nt(query, key_ref[...]) * HEAD ** (-0.5) + bias_ref[...]
        exponent = jnp.exp(scores - jnp.max(scores, -1, keepdims=True))
        total = jnp.sum(exponent, -1, keepdims=True)
        probs = (exponent * (1.0 / total)).astype(BF16)
        prob_out[h] = probs
        attended_out[:, cols] = dot_nn(probs, value_ref[...]).astype(BF16)


def attention_forward(where, h1_rel, w_query, keys_values, cosine, sine, seg_query, seg_key):
    rows, width = h1_rel.shape
    seq_len = keys_values.shape[0]
    cols = width // N_SHARD
    heads = cols // HEAD

    def whole(shape):
        return pl.BlockSpec(shape, lambda j, w: (0,) * len(shape))

    weight = pl.BlockSpec((cols, cols), lambda j, w: (0, w[0] ^ j))
    part = pl.BlockSpec((rows, cols), lambda j, w: (0, j))
    return pl.pallas_call(
        attention_forward_body,
        grid_spec=pltpu.PrefetchScalarGridSpec(
            num_scalar_prefetch=1,
            grid=(N_SHARD,),
            in_specs=[
                whole((rows, width)), weight, weight, weight, weight,
                pl.BlockSpec((seq_len, HEAD), lambda j, w: (0, (w[0] ^ j) // 2)),
                pl.BlockSpec((seq_len, HEAD), lambda j, w: (0, KVH + (w[0] ^ j) // 2)),
                whole((rows, HEAD)), whole((rows, HEAD)), whole((rows, 1)), whole((1, seq_len)),
            ],
            out_specs=[part, pl.BlockSpec((heads, rows, seq_len), lambda j, w: (j, 0, 0)), part],
            scratch_shapes=[pltpu.VMEM((rows, seq_len), F32)],
        ),
        out_shape=[
            jax.ShapeDtypeStruct((rows, width), BF16),
            jax.ShapeDtypeStruct((HQ, rows, seq_len), BF16),
            jax.ShapeDtypeStruct((rows, width), BF16),
        ],
        compiler_params=pltpu.CompilerParams(vmem_limit_bytes=28 * MEBIBYTE),
        cost_estimate=cost(15),
        name="attention_forward",
    )(where, h1_rel, *w_query, keys_values, keys_values, cosine, sine, seg_query, seg_key)


def attention_backward_body(
    where_ref, branch_ref, out0, out1, out2, out3, attended_ref, query_ref, prob_ref, key_ref, value_ref,
    w0, w1, w2, w3, cos_ref, sin_ref,
    dq_out, dk_out, dv_out, dh_out, dh_acc, dk_acc, dv_acc, da_ref,
):
    step = pl.program_id(0)
    depth = w0.shape[0]
    rows = branch_ref.shape[0]

    for j, weight in enumerate((out0, out1, out2, out3)):

        @pl.when(step == j)
        def _(weight=weight):
            da_ref[...] = dot_nt(branch_ref[...], weight[...]).astype(BF16)

    @pl.when(step % 2 == 0)
    def _():
        dk_acc[...] = jnp.zeros_like(dk_acc)
        dv_acc[...] = jnp.zeros_like(dv_acc)

    @pl.when(step == 0)
    def _():
        dh_acc[...] = jnp.zeros_like(dh_acc)

    d_pre = []
    for h in range(depth // HEAD):
        cols = slice(h * HEAD, (h + 1) * HEAD)
        d_att = da_ref[:, cols]
        probs = prob_ref[h]
        delta = jnp.sum(d_att.astype(F32) * attended_ref[:, cols].astype(F32), -1, keepdims=True)
        d_probs = dot_nt(d_att, value_ref[...])
        d_scores = (probs.astype(F32) * ((d_probs - delta) * HEAD ** (-0.5))).astype(BF16)
        d_query = dot_nn(d_scores, key_ref[...])
        d_pre.append(turn(d_query, cos_ref[...], -sin_ref[...]).astype(BF16))
        dk_acc[...] += dot_tn(query_ref[:, cols], d_scores)
        dv_acc[...] += dot_tn(d_att, probs)
    d_pre = jnp.concatenate(d_pre, 1)
    dq_out[...] = d_pre
    for j, weight in enumerate((w0, w1, w2, w3)):
        dh_acc[:, j * depth : (j + 1) * depth] += dot_nt(d_pre, weight[...])

    @pl.when(step % 2 == 1)
    def _():
        dk_out[...] = dk_acc[...].T.astype(BF16)
        dv_out[...] = dv_acc[...].T.astype(BF16)

    @pl.when(step == N_SHARD - 1)
    def _():
        dh_out[...] = dh_acc[...]


def attention_backward(where, branch, w_out, attended, queries, probs, keys_values, w_query, cosine, sine):
    rows, width = branch.shape
    seq_len = keys_values.shape[0]
    cols = width // N_SHARD
    heads = cols // HEAD

    def whole(shape):
        return pl.BlockSpec(shape, lambda j, w: (0,) * len(shape))

    weight = pl.BlockSpec((cols, cols), lambda j, w: (0, w[0] ^ j))
    part = pl.BlockSpec((rows, cols), lambda j, w: (0, j))
    head_part = pl.BlockSpec((seq_len, HEAD), lambda j, w: (0, (w[0] ^ j) // 2))
    return pl.pallas_call(
        attention_backward_body,
        grid_spec=pltpu.PrefetchScalarGridSpec(
            num_scalar_prefetch=1,
            grid=(N_SHARD,),
            in_specs=[whole((rows, width))] + [whole((cols, width))] * 4 + [
                part, part, pl.BlockSpec((heads, rows, seq_len), lambda j, w: (j, 0, 0)),
                head_part,
                pl.BlockSpec((seq_len, HEAD), lambda j, w: (0, KVH + (w[0] ^ j) // 2)),
                weight, weight, weight, weight, whole((rows, HEAD)), whole((rows, HEAD)),
            ],
            out_specs=[
                pl.BlockSpec((rows, cols), lambda j, w: (0, w[0] ^ j)),
                head_part, head_part, whole((rows, width)),
            ],
            scratch_shapes=[
                pltpu.VMEM((rows, width), F32),
                pltpu.VMEM((HEAD, seq_len), F32),
                pltpu.VMEM((HEAD, seq_len), F32),
                pltpu.VMEM((rows, cols), BF16),
            ],
        ),
        out_shape=[
            jax.ShapeDtypeStruct((rows, width), BF16),
            jax.ShapeDtypeStruct((seq_len, KVH * HEAD), BF16),
            jax.ShapeDtypeStruct((seq_len, KVH * HEAD), BF16),
            jax.ShapeDtypeStruct((rows, width), F32),
        ],
        compiler_params=pltpu.CompilerParams(vmem_limit_bytes=30 * MEBIBYTE),
        cost_estimate=cost(COST_ATTENTION),
        name="attention_backward",
    )(where, branch, *w_out, attended, queries, probs, keys_values, keys_values, *w_query, cosine, sine)


def expert_body(
    where_ref, h2_ref, dy_ref, router_ref, *refs,
):
    own, far = refs[:6], refs[6:12]
    message_out, mixed_out, da_out, db_out, act_out, gates_ref, dh_acc, y_acc, gg_acc = refs[12:]
    e = pl.program_id(0)
    f = pl.program_id(1)
    rows, width = h2_ref.shape
    half = width // 2
    lane = lax.broadcasted_iota(jnp.int32, (rows, LANES), 1)
    places = [pl.ds(pl.multiple_of((where_ref[1] ^ i) * half, LANES), half) for i in range(2)]

    @pl.when((e == 0) & (f == 0))
    def _():
        named = dy_ref[:, width:].astype(F32) > 0.5
        logits = dot_nt(h2_ref[...], router_ref[...])
        logits = jnp.concatenate([logits, jnp.zeros((rows, LANES - logits.shape[1]), F32)], 1)
        logits = jnp.where(named, logits, MASKED_SCORE)
        top = jnp.max(logits, -1, keepdims=True)
        weights = jnp.where(named, jnp.exp(logits - top), 0.0)
        gates_ref[...] = weights / jnp.sum(weights, -1, keepdims=True)
        dh_acc[...] = jnp.zeros_like(dh_acc)
        y_acc[...] = jnp.zeros_like(y_acc)
        gg_acc[...] = jnp.zeros_like(gg_acc)

    here = lane == (where_ref[0] ^ e)

    def work(members):
        gates, ups, downs = [[members[2 * k + i] for i in range(2)] for k in range(3)]
        gate = jnp.sum(jnp.where(here, gates_ref[...], 0.0), -1, keepdims=True)
        h2 = [h2_ref[:, place] for place in places]
        dy = [dy_ref[:, place] for place in places]
        load = lambda ref: ref[...].reshape(ref.shape[-2:])
        a = dot_nn(h2[0], load(gates[0])) + dot_nn(h2[1], load(gates[1]))
        b = dot_nn(h2[0], load(ups[0])) + dot_nn(h2[1], load(ups[1]))
        d_plain = dot_nt(dy[0], load(downs[0])) + dot_nt(dy[1], load(downs[1]))
        sigmoid = 1.0 / (1.0 + jnp.exp(-a))
        silu = a * sigmoid
        act = silu * b
        gate_grad = jnp.sum(act * d_plain, -1, keepdims=True)
        gg_acc[...] += jnp.where(here, gate_grad, 0.0)
        d_act = d_plain * gate
        d_a = (d_act * b * (sigmoid + silu * (1.0 - sigmoid))).astype(BF16)
        d_b = (d_act * silu).astype(BF16)
        scaled = (act * gate).astype(BF16)
        da_out[...] = d_a
        db_out[...] = d_b
        act_out[...] = scaled
        for i in range(2):
            dh_acc[i] += dot_nt(d_a, load(gates[i])) + dot_nt(d_b, load(ups[i]))
            y_acc[i] += dot_nn(scaled, load(downs[i]))

    @pl.when(e == 0)
    def _():
        work(own)

    @pl.when(e == 1)
    def _():
        work(far)

    @pl.when((e == pl.num_programs(0) - 1) & (f == pl.num_programs(1) - 1))
    def _():
        for i in range(2):
            message_out[:, places[i]] = dh_acc[i].astype(BF16)
            mixed_out[:, places[i]] = y_acc[i].astype(BF16)
        high = gg_acc[...].astype(BF16).astype(F32)
        low = pltpu.roll(gg_acc[...] - high, N_EXPERT, 1)
        message_out[:, width:] = (high + low).astype(BF16)


def expert_block(where, h2, dy_routes, router, own, far):
    rows, width = h2.shape
    hidden = own[0].shape[1]
    half = width // 2
    chunk = 256
    chunks = hidden // chunk

    def whole(shape):
        return pl.BlockSpec(shape, lambda e, f, w: (0,) * len(shape))

    own_step = lambda e, f: jnp.where(e == 0, f, chunks - 1)
    far_step = lambda e, f: jnp.where(e == 0, 0, f)
    own_in = [pl.BlockSpec((half, chunk), lambda e, f, w, i=i: (w[1] ^ i, own_step(e, f))) for i in range(2)]
    own_down = [pl.BlockSpec((chunk, half), lambda e, f, w, i=i: (own_step(e, f), w[1] ^ i)) for i in range(2)]
    far_in = [pl.BlockSpec((1, half, chunk), lambda e, f, w, k=k: (k, 0, far_step(e, f))) for k in range(2)]
    far_down = pl.BlockSpec((1, chunk, half), lambda e, f, w: (2, far_step(e, f), 0))
    part = pl.BlockSpec((rows, chunk), lambda e, f, w: (0, e * chunks + f))
    return pl.pallas_call(
        expert_body,
        grid_spec=pltpu.PrefetchScalarGridSpec(
            num_scalar_prefetch=1,
            grid=(2, chunks),
            in_specs=[whole((rows, width)), whole(dy_routes.shape), whole(router.shape)]
            + own_in + own_in + own_down
            + [far_in[0], far_in[0], far_in[1], far_in[1], far_down, far_down],
            out_specs=[whole((rows, width + LANES)), whole((rows, width)), part, part, part],
            scratch_shapes=[
                pltpu.VMEM((rows, LANES), F32),
                pltpu.VMEM((2, rows, half), F32),
                pltpu.VMEM((2, rows, half), F32),
                pltpu.VMEM((rows, LANES), F32),
            ],
        ),
        out_shape=[
            jax.ShapeDtypeStruct((rows, width + LANES), BF16),
            jax.ShapeDtypeStruct((rows, width), BF16),
            jax.ShapeDtypeStruct((rows, 2 * hidden), BF16),
            jax.ShapeDtypeStruct((rows, 2 * hidden), BF16),
            jax.ShapeDtypeStruct((rows, 2 * hidden), BF16),
        ],
        compiler_params=pltpu.CompilerParams(vmem_limit_bytes=28 * MEBIBYTE),
        cost_estimate=cost(20),
        name="expert_block",
    )(
        where, h2, dy_routes, router, own[0], own[0], own[1], own[1], own[2], own[2],
        far[0], far[1], far[0], far[1], far[0], far[1],
    )


def summed_products_body(where_ref, *refs, parts, sets):
    lefts = refs[:parts]
    rights = refs[parts : parts * (1 + sets)]
    outs = refs[parts * (1 + sets) :]
    for k in range(sets):
        total = dot_tn(lefts[0][...], rights[k * parts][...])
        for j in range(1, parts):
            total = total + dot_tn(lefts[j][...], rights[k * parts + j][...])
        out = outs[k]
        if len(out.shape) == 3:
            pieces = out.shape[0]
            deep = out.shape[1]
            for piece in range(pieces):
                out[where_ref[0] ^ piece] = total[piece * deep : (piece + 1) * deep].astype(out.dtype)
        else:
            out[...] = total.astype(out.dtype)


def summed_products(where, lefts, right_sets, grid, left_spec, right_spec, out_spec, out_shape, name):
    parts = len(lefts)
    sets = len(right_sets)
    return pl.pallas_call(
        functools.partial(summed_products_body, parts=parts, sets=sets),
        grid_spec=pltpu.PrefetchScalarGridSpec(
            num_scalar_prefetch=1,
            grid=grid,
            in_specs=[left_spec] * parts + [right_spec] * (parts * sets),
            out_specs=[out_spec] * sets,
        ),
        out_shape=[jax.ShapeDtypeStruct(out_shape, BF16)] * sets,
        compiler_params=pltpu.CompilerParams(vmem_limit_bytes=24 * MEBIBYTE),
        cost_estimate=cost(COST_PRODUCTS),
        name=name,
    )(where, *lefts, *[member for members in right_sets for member in members])


def in_grads_body(where_ref, *refs):
    h2_refs, da_refs, db_refs = refs[:4], refs[4:8], refs[8:12]
    send_ref, keep_ref, turned_ref = refs[12:]
    rows = h2_refs[0].shape[0]
    half = turned_ref.shape[0] // 2

    @pl.when(pl.program_id(0) == 0)
    def _():
        for j in range(4):
            turned_ref[:, j * rows : (j + 1) * rows] = h2_refs[j][...].T

    for k, member in enumerate((da_refs, db_refs)):
        for out, place in ((send_ref, 1 - where_ref[0]), (keep_ref, where_ref[0])):
            here = pl.ds(pl.multiple_of(place * half, LANES), half)
            total = dot_nn(turned_ref[here, :rows], member[0][...])
            for j in range(1, 4):
                total = total + dot_nn(turned_ref[here, j * rows : (j + 1) * rows], member[j][...])
            out[k] = total.astype(BF16)


def expert_in_grads(where, h2, d_a, d_b):
    rows, width = h2[0].shape
    columns = d_a[0].shape[1]
    chunk = 256
    half = width // 2
    part = pl.BlockSpec((rows, chunk), lambda i, w: (0, i))
    out = pl.BlockSpec((2, half, chunk), lambda i, w: (0, 0, i))
    return pl.pallas_call(
        in_grads_body,
        grid_spec=pltpu.PrefetchScalarGridSpec(
            num_scalar_prefetch=1,
            grid=(columns // chunk,),
            in_specs=[pl.BlockSpec((rows, width), lambda i, w: (0, 0))] * 4 + [part] * 8,
            out_specs=[out] * 2,
            scratch_shapes=[pltpu.VMEM((width, 4 * rows), BF16)],
        ),
        out_shape=[jax.ShapeDtypeStruct((2, half, columns), BF16)] * 2,
        compiler_params=pltpu.CompilerParams(vmem_limit_bytes=30 * MEBIBYTE),
        cost_estimate=cost(COST_IN),
        name="expert_in_grads",
    )(where, *h2, *d_a, *d_b)


def down_grads_body(where_ref, *refs):
    act_refs, send_refs, keep_refs = refs[:4], refs[4:8], refs[8:12]
    turned = [act[...].T for act in act_refs]
    for rights, out in ((send_refs, refs[12]), (keep_refs, refs[13])):
        total = dot_nn(turned[0], rights[0][...])
        for j in range(1, 4):
            total = total + dot_nn(turned[j], rights[j][...])
        out[0] = total.astype(BF16)


def expert_down_grads(where, acts, dy_routes):
    rows, columns = acts[0].shape
    width = dy_routes[0].shape[1] - LANES
    half = width // 2
    hidden = columns // 2
    out = pl.BlockSpec((1, hidden, half), lambda e, w: (e, 0, 0))
    return pl.pallas_call(
        down_grads_body,
        grid_spec=pltpu.PrefetchScalarGridSpec(
            num_scalar_prefetch=1,
            grid=(2,),
            in_specs=[pl.BlockSpec((rows, hidden), lambda e, w: (0, e))] * 4
            + [pl.BlockSpec((rows, half), lambda e, w: (0, 1 - w[0]))] * 4
            + [pl.BlockSpec((rows, half), lambda e, w: (0, w[0]))] * 4,
            out_specs=[out, out],
        ),
        out_shape=[jax.ShapeDtypeStruct((2, hidden, half), BF16)] * 2,
        compiler_params=pltpu.CompilerParams(vmem_limit_bytes=26 * MEBIBYTE),
        cost_estimate=cost(COST_DOWN),
        name="expert_down_grads",
    )(where, *acts, *dy_routes, *dy_routes)


class PlaneSum:
    def __init__(self, pieces, order):
        self.shape = pieces.shape[1:]
        self.order = order
        self.axes = [4, 2, 1]
        self.kept = pieces.reshape((2, 2, 2) + self.shape)
        self.step = 0
        self.send()

    def send(self):
        if self.step < 3:
            at = self.axes.index(self.order[self.step])
            self.mine = lax.index_in_dim(self.kept, 0, at, keepdims=False)
            other = lax.index_in_dim(self.kept, 1, at, keepdims=False)
            self.received = swap(other, self.order[self.step], 0)
        else:
            self.received = swap(self.kept, self.order[5 - self.step], 0)

    def receive(self, token):
        received = after(self.received, token)
        if self.step < 3:
            self.kept = (self.mine.astype(F32) + received.astype(F32)).astype(BF16)
            self.axes.remove(self.order[self.step])
        else:
            bit = self.order[5 - self.step]
            if self.step == 5:
                self.done = (self.kept.reshape((4,) + self.shape), received.reshape((4,) + self.shape))
                return received
            at = sum(1 for b in self.axes if b > bit)
            self.kept = jnp.stack([self.kept, received], at)
            self.axes = sorted(self.axes + [bit], reverse=True)
        self.step += 1
        self.send()
        return self.kept


def reorder_body(where_ref, even_ref, odd_ref, out_ref, *, first):
    for b in range(N_EXPERT):
        place = where_ref[0] ^ b
        low = place % first
        index = (place // (2 * first)) * first + low
        odd = (place // first) % 2

        @pl.when(odd == 0)
        def _(b=b, index=index):
            out_ref[b] = even_ref[index].astype(F32)

        @pl.when(odd == 1)
        def _(b=b, index=index):
            out_ref[b] = odd_ref[index].astype(F32)


def reorder(where, even, odd, columns, first):
    deep, width = even.shape[1:]
    results = []
    begin = 0
    for count in columns:
        wide = min(count, 512)
        start = begin // wide
        spec = pl.BlockSpec((N_EXPERT // 2, deep, wide), lambda i, w, start=start: (0, 0, start + i))
        results.append(
            pl.pallas_call(
                functools.partial(reorder_body, first=first),
                grid_spec=pltpu.PrefetchScalarGridSpec(
                    num_scalar_prefetch=1,
                    grid=(count // wide,),
                    in_specs=[spec, spec],
                    out_specs=pl.BlockSpec((N_EXPERT, deep, wide), lambda i, w: (0, 0, i)),
                ),
                out_shape=jax.ShapeDtypeStruct((N_EXPERT, deep, count), F32),
                cost_estimate=cost(COST_PLACE),
                name="reorder",
            )(where, even, odd).reshape(N_EXPERT * deep, count)
        )
        begin += count
    return results


def key_value_grad_body(*refs):
    lefts, rights, out_ref = refs[:4], refs[4:8], refs[8]
    rows, block = lefts[0].shape
    total = dot_tn(lefts[0][...], rights[0][:rows])
    small = rights[0][rows:, :block].astype(F32)
    for j in range(1, 4):
        total = total + dot_tn(lefts[j][...], rights[j][:rows])
        small = small + rights[j][rows:, :block].astype(F32)
    few = small.shape[0] // 2
    out_ref[:block] = total.astype(BF16)
    out_ref[block:, :block] = (small[:few] + small[few:]).astype(BF16)
    out_ref[block:, block:] = jnp.zeros_like(out_ref[block:, block:])


def key_value_grad(lefts, rights, block):
    rows = lefts[0].shape[0]
    columns = rights[0].shape[1]
    few = (rights[0].shape[0] - rows) // 2
    whole = lambda shape: pl.BlockSpec(shape, lambda i: (0, 0))
    return pl.pallas_call(
        key_value_grad_body,
        grid=(1,),
        in_specs=[whole((rows, block))] * 4 + [whole(rights[0].shape)] * 4,
        out_specs=whole((block + few, columns)),
        out_shape=jax.ShapeDtypeStruct((block + few, columns), BF16),
        cost_estimate=cost(COST_PRODUCTS),
        name="key_value_grad",
    )(*lefts, *rights)


def place_body(where_ref, mine_ref, partner_ref, out_ref):
    @pl.when(pl.program_id(0) == 0)
    def _():
        out_ref[...] = mine_ref[0].astype(out_ref.dtype)

    @pl.when(pl.program_id(0) == 1)
    def _():
        out_ref[...] = partner_ref[0].astype(out_ref.dtype)


def place_halves(where, mine, partner, member, by_rows):
    tall, wide = mine.shape[1:]
    cuts = 2
    deep = tall // cuts

    def mine_map(h, i, w):
        return (member, jnp.where(h == 0, i, cuts - 1), 0)

    def partner_map(h, i, w):
        return (member, jnp.where(h == 0, 0, i), 0)

    def out_map(h, i, w):
        return ((w[0] ^ h) * cuts + i, 0) if by_rows else (i, w[0] ^ h)

    return pl.pallas_call(
        place_body,
        grid_spec=pltpu.PrefetchScalarGridSpec(
            num_scalar_prefetch=1,
            grid=(2, cuts),
            in_specs=[pl.BlockSpec((1, deep, wide), mine_map), pl.BlockSpec((1, deep, wide), partner_map)],
            out_specs=pl.BlockSpec((deep, wide), out_map),
        ),
        out_shape=jax.ShapeDtypeStruct((2 * tall, wide) if by_rows else (tall, 2 * wide), F32),
        cost_estimate=cost(COST_PLACE),
        name="place_halves",
    )(where, mine, partner)


def far_halves_body(where_ref, *refs):
    out_ref = refs[-1]
    for k, ref in enumerate(refs[:-1]):

        @pl.when(pl.program_id(0) == k)
        def _(ref=ref):
            out_ref[0] = ref[...]


def far_halves(where, own):
    hidden = own[0].shape[1]
    half = own[0].shape[0] // 2
    cuts = 1
    tall = half // cuts

    def in_map(k):
        step = lambda i, r: jnp.where(i < k, 0, jnp.where(i == k, r, cuts - 1))
        if k == 2:
            return lambda i, r, w: (step(i, r), w[0])
        return lambda i, r, w: (w[0] * cuts + step(i, r), 0)

    return pl.pallas_call(
        far_halves_body,
        grid_spec=pltpu.PrefetchScalarGridSpec(
            num_scalar_prefetch=1,
            grid=(3, cuts),
            in_specs=[pl.BlockSpec((tall, hidden), in_map(k)) for k in range(3)],
            out_specs=pl.BlockSpec((1, tall, hidden), lambda i, r, w: (i, r, 0)),
        ),
        out_shape=jax.ShapeDtypeStruct((3, half, hidden), BF16),
        cost_estimate=cost(3),
        name="far_halves",
    )(where, *own)


def pack_body(key_ref, value_ref, small_ref, out_ref):
    rows, low = key_ref.shape
    out_ref[:rows, :low] = key_ref[...]
    out_ref[:rows, low:] = value_ref[...]
    out_ref[rows:, : small_ref.shape[1]] = small_ref[...]
    out_ref[rows:, small_ref.shape[1] :] = jnp.zeros_like(out_ref[rows:, small_ref.shape[1] :])


def pack(w_key, w_value, small):
    rows, low = w_key.shape
    return pl.pallas_call(
        pack_body,
        out_shape=jax.ShapeDtypeStruct((rows + small.shape[0], 2 * low), BF16),
        cost_estimate=cost(2),
        name="pack",
    )(w_key, w_value, small)


def plus(part, received):
    return (part.astype(F32) + received.astype(F32)).astype(BF16)


def on_device_rings(
    hidden_in, segment_ids, routes, attn_gain, moe_gain, w_query, w_key, w_value, w_out, w_router,
    expert_gate, expert_up, expert_down, out_grad,
):
    rows, width = hidden_in.shape
    experts = w_router.shape[1]
    shard = lax.axis_index("shard")
    expert = lax.axis_index("expert")
    core = shard % 2
    where_shard = shard.astype(jnp.int32)[None]
    where_expert = expert.astype(jnp.int32)[None]
    where_core = core.astype(jnp.int32)[None]
    where_far_core = 1 - where_core
    block = width // N_SHARD
    low = KVH * HEAD

    own = (expert_gate[0], expert_up[0], expert_down[0])
    far_send = far_halves(where_core, own)
    far_part = swap(far_send, 1, 0)
    small = jnp.concatenate(
        [w_router.T, attn_gain[None], moe_gain[None], jnp.zeros((6, block), BF16)], 0
    )
    packed_own = pack(after(w_key, far_send), w_value, small)
    packed_y = swap(packed_own, 0, 2)
    mask = (routes[:, :, None] == jnp.arange(LANES, dtype=jnp.int32)[None, None, :]).any(1)
    dy_routes = [jnp.concatenate([out_grad, mask.astype(BF16)], 1)]
    for _ in range(3):
        dy_routes.append(next_plane(dy_routes[-1]))
    query_w_core = swap(w_query, 0, 1)
    out_w_core = swap(w_out, 0, 1)
    query_w_y = swap(after(w_query, packed_y), 0, 2)
    packed_pair = swap(jnp.concatenate([packed_own, packed_y], 0), 0, 1)
    tall = packed_own.shape[0]
    packed = [packed_own, packed_pair[:tall], packed_y, packed_pair[tall:]]

    inputs = hidden_in.astype(F32)
    factor_attn = lax.rsqrt(jnp.mean(inputs * inputs, -1, keepdims=True) + EPSILON)
    unit_rel = jnp.concatenate(
        xor_blocks([inputs[:, j * block : (j + 1) * block] for j in range(4)], shard), 1
    ) * factor_attn
    gain_rel = jnp.concatenate([member[block + experts : block + experts + 1, :block] for member in packed], 1)
    gain_rel = gain_rel.astype(F32)
    h1_rel = after((unit_rel * gain_rel).astype(BF16), query_w_core, out_w_core)
    key_value_w = [member[:block] for member in packed]
    pre = sum(dot_nn(h1_rel[:, j * block : (j + 1) * block], key_value_w[j]) for j in range(4))
    positions = shard * rows + jnp.arange(rows, dtype=jnp.int32)
    cosine, sine = rope_tables(positions, HEAD)
    key_local = rotate(pre[:, :low], cosine, sine, HEAD)
    key_value = jnp.concatenate([key_local, pre[:, low:]], 1).astype(BF16)
    key_value = after(key_value, dy_routes[1])
    key_value_y = swap(key_value, 0, 2)
    query_w = [w_query, query_w_core, query_w_y, swap(query_w_y, 0, 1)]
    key_value_pair = swap(jnp.concatenate([key_value, key_value_y], 0), 0, 1)
    keys_values = jnp.concatenate(
        xor_blocks([key_value, key_value_pair[:rows], key_value_y, key_value_pair[rows:]], shard), 0
    )
    out_w_y = swap(after(w_out, query_w_y, key_value), 0, 2)
    cosine_row = jnp.concatenate([cosine, cosine], 1)
    sine_row = jnp.concatenate([-sine, sine], 1)
    seg_query = lax.dynamic_slice_in_dim(segment_ids, shard * rows, rows)[:, None]
    queries, probs, attended = attention_forward(
        where_shard, after(h1_rel, dy_routes[2]), query_w, keys_values, cosine_row, sine_row, seg_query, segment_ids[None, :]
    )
    attended_late = after(attended, dy_routes[3])
    out_w_y = after(out_w_y, attended)
    out_w = [w_out, out_w_core, out_w_y, swap(out_w_y, 0, 1)]
    mid_state = inputs + sum(
        dot_nn(attended_late[:, j * block : (j + 1) * block], out_w[j]) for j in range(4)
    )
    factor_moe = lax.rsqrt(jnp.mean(mid_state * mid_state, -1, keepdims=True) + EPSILON)
    unit_moe = mid_state * factor_moe
    small_true = jnp.concatenate(xor_blocks([member[block:, :block] for member in packed], shard), 1)
    gain_moe = small_true[experts + 1 : experts + 2].astype(F32)
    router = small_true[:experts].astype(F32)
    h2 = [(unit_moe * gain_moe).astype(BF16)]

    far_part = after(far_part, attended)
    far_other = swap(far_part, 0, 1)
    hidden = own[0].shape[1]
    deep = width // 2
    far = (far_part, far_other)
    where_pair = jnp.stack([expert, core]).astype(jnp.int32)

    mixer_rows = [
        jnp.concatenate([h1_rel[:, j * block : (j + 1) * block], attended[:, j * block : (j + 1) * block]], 1)
        for j in range(4)
    ]
    mixer_rows = [mixer_rows[0]] + [swap(mixer_rows[j], 0, j) for j in (1, 2, 3)]
    add = lambda a, b: (a.astype(F32) + b.astype(F32)).astype(BF16)
    block_of = lambda j, *ready: expert_block(
        where_pair, after(h2[j], *ready), dy_routes[j], small_true, own, far
    )
    h2.append(next_plane(h2[0]))
    done = [block_of(0)]
    h2.append(next_plane(after(h2[1], done[0][0])))
    done.append(block_of(1, done[0][0], *mixer_rows))
    h2[2] = after(h2[2], done[1][0])
    h2.append(next_plane(h2[2]))
    message = next_plane(after(done[1][0], h2[2]))
    done.append(block_of(2, done[1][0]))
    done.append(block_of(3, done[2][0]))
    second = add(done[2][0], after(message, done[3][0]))
    message = next_plane(second)

    acts = [done[j][4] for j in range(4)]
    down_send, down_keep = expert_down_grads(after(where_core, second), acts, dy_routes)
    in_send, in_keep = expert_in_grads(
        after(where_core, down_send), h2, [done[j][2] for j in range(4)], [done[j][3] for j in range(4)]
    )
    third = add(done[3][0], after(message, in_send))
    message = next_plane(third)
    v = types.SimpleNamespace(
        down_swap=swap(after(down_send, third), 0, 1), in_swap=swap(after(in_send, third), 0, 1)
    )

    def mixer_grads(half, rights, name):
        n = rights[0].shape[1]
        (pieces,) = summed_products(
            where_expert, mixer_rows, [rights], (n // 512,),
            pl.BlockSpec((rows, block), lambda i, w: (0, half)),
            pl.BlockSpec((rows, 512), lambda i, w: (0, i)),
            pl.BlockSpec((N_EXPERT, block // N_EXPERT, 512), lambda i, w: (0, 0, i)),
            (N_EXPERT, block // N_EXPERT, n), name,
        )
        return pieces


    def first_far(token):
        v.down_swap, v.in_swap, token = together(v.down_swap, v.in_swap, token)
        far = jnp.stack(
            [plus(down_keep[1], v.down_swap[1]), plus(in_keep[0, :, hidden:], v.in_swap[0, :, hidden:])]
        )
        v.first_received = swap(far, 1, 0)
        return far

    def up_far(token):
        v.in_swap = after(v.in_swap, token)
        v.up_far = plus(in_keep[1, :, hidden:], v.in_swap[1, :, hidden:])
        return v.up_far

    def up_send(token):
        v.up_received = swap(after(v.up_far, token), 1, 0)
        return token

    def branch(token):
        total = done[0][0].astype(F32) + after(message, token).astype(F32)
        named = mask[:, :experts]
        logits = jnp.where(named, dot_nt(h2[0], small_true[:experts]), MASKED_SCORE)
        weights = jnp.where(named, jnp.exp(logits - jnp.max(logits, -1, keepdims=True)), 0.0)
        gate = weights / jnp.sum(weights, -1, keepdims=True)
        gate_grad = total[:, width : width + experts] + total[:, width + experts : width + 2 * experts]
        d_logits = gate * (gate_grad - jnp.sum(gate * gate_grad, -1, keepdims=True))
        d_h2 = total[:, :width] + jnp.dot(d_logits, router, precision=HIGHEST)
        v.router_grad = jnp.dot(d_logits.T, h2[0].astype(F32), precision=HIGHEST)
        d_mid_norm, v.gain_moe_grad = norm_backward(d_h2, unit_moe, factor_moe, gain_moe)
        v.d_mid = out_grad.astype(F32) + d_mid_norm
        v.d_branch = v.d_mid.astype(BF16)
        v.branch_core = swap(v.d_branch, 0, 1)
        v.branch_y = swap(v.d_branch, 0, 2)
        return v.d_branch

    def mixed_0(token):
        v.mixed = next_plane(after(done[1][1], token))
        return token

    def attention(token):
        v.d_q_pre, v.d_key_part, v.d_value_part, v.d_normed = attention_backward(
            where_shard, after(v.d_branch, token), out_w, attended, queries, probs, keys_values, query_w,
            cosine_row, sine_row,
        )
        return v.d_q_pre

    def sync_1(token):
        v.d_q_pre, v.d_key_part, v.d_value_part, v.branch_y, v.branch_core, v.mixed = together(
            v.d_q_pre, v.d_key_part, v.d_value_part, v.branch_y, v.branch_core, v.mixed
        )
        v.d_q_y = swap(v.d_q_pre, 0, 2)
        v.d_q_core = swap(v.d_q_pre, 0, 1)
        v.branch_far = swap(v.branch_y, 0, 1)
        d_parts = jnp.concatenate([v.d_key_part, v.d_value_part], 1).reshape(N_SHARD, rows, 2 * low)
        v.d_rel = xor_blocks([d_parts[j] for j in range(4)], shard)
        v.from_core = swap(jnp.stack([v.d_rel[1], v.d_rel[3]]), 0, 1)
        v.mixed = add(done[2][1], v.mixed)
        return v.d_q_pre

    def sync_2(token):
        v.d_q_core, v.branch_far, v.from_core, v.mixed = together(
            v.d_q_core, v.branch_far, v.from_core, v.mixed
        )
        v.mixed = next_plane(v.mixed)
        d_far = add(v.d_rel[2], v.from_core[1])
        v.d_far_y = swap(d_far, 0, 2)
        rights = [v.d_branch, v.branch_core, v.branch_y, after(v.branch_far, d_far)]
        v.out_pieces = mixer_grads(1, rights, "w_out_grad")
        return v.out_pieces

    def sync_3(token):
        v.d_q_y, v.out_pieces, token = together(v.d_q_y, v.out_pieces, token)
        v.out_sum = PlaneSum(v.out_pieces, OUT_BITS)
        rights = [v.d_q_pre, v.d_q_core, v.d_q_y, swap(v.d_q_y, 0, 1)]
        v.query_pieces = mixer_grads(0, rights, "w_query_grad")
        return v.query_pieces

    def sync_4(token):
        v.query_pieces, v.d_far_y, token = together(v.query_pieces, v.d_far_y, token)
        v.query_sum = PlaneSum(v.query_pieces, QUERY_BITS)
        return v.query_pieces

    def mixed_2(token):
        total = add(done[3][1], after(v.mixed, token))
        v.mixed = next_plane(total)
        return total

    def first_part(token):
        received = after(v.first_received, token)
        down = down_keep[0].astype(F32) + v.down_swap[0].astype(F32) + received[0].astype(F32)
        gate = in_keep[0, :, :hidden].astype(F32) + v.in_swap[0, :, :hidden].astype(F32) + received[1].astype(F32)
        v.first_part = jnp.stack([down.astype(BF16), gate.astype(BF16)])
        return v.first_part

    def first_send(token):
        v.first_y = swap(after(v.first_part, token), 0, 2)
        return token

    def layer(token):
        mixed = after(v.mixed, token).astype(F32)
        v.layer_out = (mid_state + done[0][1].astype(F32) + mixed).astype(BF16)
        return v.layer_out

    def up_part(token):
        own_part = in_keep[1, :, :hidden].astype(F32) + v.in_swap[1, :, :hidden].astype(F32)
        v.up_part = plus(own_part, after(v.up_received, token))
        v.up_y = swap(v.up_part, 0, 2)
        return v.up_part

    def first_total(token):
        v.first_total = plus(v.first_part, after(v.first_y, token))
        v.first_core = swap(v.first_total, 0, 1)
        return v.first_total

    def up_total(token):
        v.up_total = plus(v.up_part, after(v.up_y, token))
        v.up_core = swap(v.up_total, 0, 1)
        return v.up_total

    def down_place(token):
        v.first_core = after(v.first_core, token)
        v.down_sum = place_halves(where_core, v.first_total, v.first_core, 0, False)[None]
        return v.down_sum

    def gate_place(token):
        v.first_core = after(v.first_core, token)
        v.gate_sum = place_halves(where_core, v.first_total, v.first_core, 1, True)[None]
        return v.gate_sum

    def up_place(token):
        v.up_sum = place_halves(where_core, v.up_total[None], after(v.up_core, token)[None], 0, True)[None]
        return v.up_sum

    def key_value(token):
        d_key_value = v.d_rel[0].astype(F32) + v.from_core[0].astype(F32) + after(v.d_far_y, token).astype(F32)
        d_k_pre = rotate(d_key_value[:, :low], cosine, -sine, HEAD)
        v.d_kv_pre = jnp.concatenate([d_k_pre, d_key_value[:, low:]], 1).astype(BF16)
        return v.d_kv_pre

    def norms(token):
        d_kv_pre = after(v.d_kv_pre, token)
        d_normed = v.d_normed + jnp.concatenate([dot_nt(d_kv_pre, member) for member in key_value_w], 1)
        d_input_norm, gain_attn_grad = norm_backward(d_normed, unit_rel, factor_attn, gain_rel)
        d_input_norm = jnp.concatenate(
            xor_blocks([d_input_norm[:, j * block : (j + 1) * block] for j in range(4)], shard), 1
        )
        v.input_grad = v.d_mid + d_input_norm
        rest = jnp.concatenate([v.gain_moe_grad[None], v.router_grad, jnp.zeros((6, width), F32)], 0)
        rest = xor_blocks([rest[:, j * block : (j + 1) * block] for j in range(4)], shard)
        v.notes = []
        for j in range(4):
            piece = jnp.concatenate([gain_attn_grad[None, j * block : (j + 1) * block], rest[j]], 0)
            high = piece.astype(BF16)
            piece = jnp.concatenate([high, (piece - high.astype(F32)).astype(BF16)], 0)
            v.notes.append(jnp.concatenate([d_kv_pre, jnp.pad(piece, ((0, 0), (0, 2 * low - block)))], 0))
        v.notes_y = swap(jnp.concatenate([v.notes[2], v.notes[3]], 0), 0, 2)
        return v.notes[0]

    def notes(token):
        tall = v.notes[0].shape[0]
        v.notes_y, token = together(v.notes_y, token)
        v.notes_core = swap(jnp.concatenate([v.notes[1], v.notes_y[tall:]], 0), 0, 1)
        return token

    def last_grads(token):
        tall = v.notes[0].shape[0]
        core_part = after(v.notes_core, token)
        v.last = key_value_grad(
            mixer_rows, [v.notes[0], core_part[:tall], v.notes_y[:tall], core_part[tall:]], block
        )
        v.last_far = swap(v.last, LAST_BITS[0], 0)
        return v.last

    def last_1(token):
        v.last = plus(v.last, after(v.last_far, token))
        v.last_far = swap(v.last, LAST_BITS[1], 0)
        return v.last

    def last_2(token):
        v.last = plus(v.last, after(v.last_far, token))
        v.last_far = swap(v.last, LAST_BITS[2], 0)
        return v.last

    def last_3(token):
        v.last = v.last.astype(F32) + after(v.last_far, token).astype(F32)
        return v.last

    def query(token):
        return v.query_sum.receive(token)

    def out(token):
        return v.out_sum.receive(token)

    def query_place(token):
        even, odd = v.query_sum.done
        (v.query_grad,) = reorder(where_expert, after(even, token), odd, (width,), QUERY_BITS[0])
        return v.query_grad

    def out_place(token):
        even, odd = v.out_sum.done
        (v.out_w_grad,) = reorder(where_expert, after(even, token), odd, (width,), OUT_BITS[0])
        return v.out_w_grad

    steps = locals()
    token = third
    for name in EVENTS:
        token = steps[name](token)
    layer_out, input_grad, query_grad, out_w_grad = v.layer_out, v.input_grad, v.query_grad, v.out_w_grad
    gate_sum, up_sum, down_sum, last = v.gate_sum, v.up_sum, v.down_sum, v.last
    small_sums = last[block:, :block]
    return (
        layer_out,
        input_grad,
        small_sums[0],
        small_sums[1],
        query_grad,
        last[:block, :low],
        last[:block, low:],
        out_w_grad,
        small_sums[2 : 2 + experts].T,
        gate_sum,
        up_sum,
        down_sum,
    )


def on_device(hidden_in, segment_ids, routes, *rest):
    rows = hidden_in.shape[0]
    experts = rest[6].shape[1]
    capacity = rows * routes.shape[1] * 2 // experts
    shape = (lax.axis_size("expert"), lax.axis_size("shard"))
    if shape == (N_EXPERT, N_SHARD) and experts == N_EXPERT and capacity == rows:
        return on_device_rings(hidden_in, segment_ids, routes, *rest)
    return on_device_routed(hidden_in, segment_ids, routes, *rest)


def solution(mesh):
    placed = (
        P(("expert", "shard"), None),
        P("expert"),
        P(("expert", "shard"), None),
        P("shard"),
        P("shard"),
        P("shard", None),
        P("shard", None),
        P("shard", None),
        P("shard", None),
        P("shard", None),
        P("expert", None, None),
        P("expert", None, None),
        P("expert", None, None),
        P(("expert", "shard"), None),
    )
    return jax.shard_map(
        on_device,
        mesh=mesh,
        in_specs=placed,
        out_specs=(
            P(("expert", "shard"), None),
            P(("expert", "shard"), None),
            P("shard"),
            P("shard"),
            P("shard", None),
            P("shard", None),
            P("shard", None),
            P("shard", None),
            P("shard", None),
            P("expert", None, None),
            P("expert", None, None),
            P("expert", None, None),
        ),
        check_vma=False,
    )
```

```python
import functools
import types

import jax
import jax.numpy as jnp
from jax import lax
from jax.experimental import pallas as pl
from jax.experimental.pallas import tpu as pltpu
from jax.sharding import PartitionSpec as P

HQ = 12
KVH = 2
HEAD = 128


EPSILON = 1e-06
ROPE_BASE = 10000.0
MASKED_SCORE = -1e30
HIGHEST = lax.Precision.HIGHEST


def rope_tables(positions, head_size):
    half_size = head_size // 2
    frequency = ROPE_BASE ** (-(jnp.arange(half_size, dtype=jnp.float32) * 2.0 / head_size))
    angles = positions.astype(jnp.float32)[:, None] * frequency[None, :]
    return (jnp.cos(angles), jnp.sin(angles))


def rotate(values, cosine_table, sine_table, head_size):
    rows_count = values.shape[0]
    shaped = values.reshape(rows_count, -1, head_size)
    half_size = head_size // 2
    first_half = shaped[..., :half_size]
    second_half = shaped[..., half_size:]
    cosine_part = cosine_table[:, None, :]
    sine_part = sine_table[:, None, :]
    turned = jnp.concatenate(
        [
            first_half * cosine_part - second_half * sine_part,
            second_half * cosine_part + first_half * sine_part,
        ],
        -1,
    )
    return turned.reshape(rows_count, -1)


def norm_forward(values, gain):
    factor = lax.rsqrt(jnp.mean(values * values, -1, keepdims=True) + EPSILON)
    unit_rows = values * factor
    return (unit_rows, factor, (unit_rows * gain).astype(jnp.bfloat16))


def norm_backward(grad_rows, unit_rows, factor, gain):
    gain_grad = jnp.sum(grad_rows * unit_rows, 0)
    scaled_grad = grad_rows * gain
    return (
        factor * (scaled_grad - unit_rows * jnp.mean(scaled_grad * unit_rows, -1, keepdims=True)),
        gain_grad,
    )


def score_block(query_heads, key_heads, visible, score_scale):
    raw_scores = jnp.einsum(
        "tkgd,skd->kgts", query_heads, key_heads, preferred_element_type=jnp.float32
    )
    return jnp.where(visible, raw_scores * score_scale, MASKED_SCORE)


def on_device_routed(
    hidden_in,
    segment_ids,
    routes,
    attn_gain,
    moe_gain,
    w_query,
    w_key,
    w_value,
    w_out,
    w_router,
    expert_gate,
    expert_up,
    expert_down,
    out_grad,
):
    tok_rows = hidden_in.shape[0]
    top_count = routes.shape[1]
    experts = w_router.shape[1]
    capacity = tok_rows * top_count * 2 // experts
    groups = HQ // KVH
    score_scale = HEAD ** (-0.5)
    shard_index = lax.axis_index("shard")
    n_expert = lax.axis_size("expert")
    local_experts = expert_gate.shape[0]
    gain_attn, gain_moe, query_w, key_w, value_w, out_w, router_w = (
        lax.all_gather(attn_gain, "shard", axis=0, tiled=True),
        lax.all_gather(moe_gain, "shard", axis=0, tiled=True),
        lax.all_gather(w_query, "shard", axis=0, tiled=True),
        lax.all_gather(w_key, "shard", axis=0, tiled=True),
        lax.all_gather(w_value, "shard", axis=0, tiled=True),
        lax.all_gather(w_out, "shard", axis=0, tiled=True),
        lax.all_gather(w_router, "shard", axis=0, tiled=True),
    )
    gain_attn = gain_attn.astype(jnp.float32)
    gain_moe = gain_moe.astype(jnp.float32)
    inputs = hidden_in.astype(jnp.float32)
    unit_attn, factor_attn, normed = norm_forward(inputs, gain_attn)
    q_pre = jnp.dot(normed, query_w, preferred_element_type=jnp.float32)
    k_pre = jnp.dot(normed, key_w, preferred_element_type=jnp.float32)
    value_rows = jnp.dot(normed, value_w, preferred_element_type=jnp.float32).astype(jnp.bfloat16)
    positions = shard_index * tok_rows + jnp.arange(tok_rows, dtype=jnp.int32)
    cosine_table, sine_table = rope_tables(positions, HEAD)
    queries = rotate(q_pre, cosine_table, sine_table, HEAD).astype(jnp.bfloat16)
    key_local = rotate(k_pre, cosine_table, sine_table, HEAD).astype(jnp.bfloat16)
    key_rows, value_all = (
        lax.all_gather(key_local, "shard", axis=0, tiled=True),
        lax.all_gather(value_rows, "shard", axis=0, tiled=True),
    )
    seq_len = key_rows.shape[0]
    query_heads = queries.reshape(tok_rows, KVH, groups, HEAD)
    key_heads = key_rows.reshape(seq_len, KVH, HEAD)
    value_heads = value_all.reshape(seq_len, KVH, HEAD)
    seg_local = lax.dynamic_slice_in_dim(segment_ids, shard_index * tok_rows, tok_rows)
    visible = (positions[:, None] >= jnp.arange(seq_len, dtype=jnp.int32)[None, :]) & (
        seg_local[:, None] == segment_ids[None, :]
    )
    score_values = score_block(query_heads, key_heads, visible, score_scale)
    top_score = jnp.max(score_values, -1, keepdims=True)
    exponent = jnp.exp(score_values - top_score)
    denominators = jnp.sum(exponent, -1, keepdims=True)
    probabilities = exponent / denominators
    log_total = top_score + jnp.log(denominators)
    attended = (
        jnp.einsum(
            "kgts,skd->tkgd",
            probabilities.astype(jnp.bfloat16),
            value_heads,
            preferred_element_type=jnp.float32,
        )
        .reshape(tok_rows, -1)
        .astype(jnp.bfloat16)
    )
    mid_state = inputs + jnp.dot(attended, out_w, preferred_element_type=jnp.float32)
    unit_moe, factor_moe, normed_moe = norm_forward(mid_state, gain_moe)
    logits = jnp.dot(normed_moe, router_w, preferred_element_type=jnp.float32)
    onehot = (routes[:, :, None] == jnp.arange(experts, dtype=jnp.int32)[None, None, :]).astype(
        jnp.float32
    )
    chosen = jnp.sum(onehot * logits[:, None, :], -1)
    chosen = chosen - jnp.max(chosen, -1, keepdims=True)
    weights = jnp.exp(chosen)
    gate = weights / jnp.sum(weights, -1, keepdims=True)
    flat_routes = routes.reshape(-1)
    route_hot = (flat_routes[:, None] == jnp.arange(experts, dtype=jnp.int32)[None, :]).astype(
        jnp.int32
    )
    before = jnp.cumsum(route_hot, 0, dtype=jnp.int32) - route_hot
    slot_id = flat_routes * capacity + jnp.sum(before * route_hot, 1, dtype=jnp.int32)
    source = (
        jnp.zeros((experts * capacity,), jnp.int32)
        .at[slot_id]
        .set(jnp.arange(tok_rows * top_count, dtype=jnp.int32))
    )
    filled = jnp.zeros((experts * capacity,), jnp.bool_).at[slot_id].set(True)
    outgoing = jnp.where(filled[:, None], jnp.take(normed_moe, source // top_count, axis=0), 0)
    outgoing = outgoing.reshape(experts, capacity, -1)
    arrived = lax.all_to_all(outgoing, "expert", split_axis=0, concat_axis=0, tiled=True)
    item_count = arrived.shape[1]
    shaped = arrived.reshape(n_expert, local_experts, item_count, -1)
    gate_pre = jnp.einsum("nlcd,ldf->nlcf", shaped, expert_gate, preferred_element_type=jnp.float32)
    up_pre = jnp.einsum("nlcd,ldf->nlcf", shaped, expert_up, preferred_element_type=jnp.float32)
    hidden_rows = (gate_pre * jax.nn.sigmoid(gate_pre) * up_pre).astype(jnp.bfloat16)
    result = jnp.einsum(
        "nlcf,lfd->nlcd", hidden_rows, expert_down, preferred_element_type=jnp.float32
    )
    result = result.astype(jnp.bfloat16).reshape(arrived.shape)
    returned = lax.all_to_all(result, "expert", split_axis=0, concat_axis=0, tiled=True)
    outcome = (
        returned,
        arrived,
        gate_pre.reshape(n_expert * local_experts, item_count, -1),
        up_pre.reshape(n_expert * local_experts, item_count, -1),
        hidden_rows.reshape(n_expert * local_experts, item_count, -1),
    )
    returned_rows = jnp.take(outcome[0].reshape(experts * capacity, -1), slot_id, axis=0).reshape(
        tok_rows, top_count, -1
    )
    mixed = mid_state + jnp.sum(gate[:, :, None] * returned_rows, 1)
    layer_out = mixed.astype(jnp.bfloat16)
    grad_out = out_grad.astype(jnp.float32)
    gate_grad = jnp.sum(returned_rows * grad_out[:, None, :], -1)
    gate_slots = jnp.take(gate.reshape(-1), source, axis=0)
    d_send = jnp.where(
        filled[:, None], jnp.take(grad_out, source // top_count, axis=0) * gate_slots[:, None], 0.0
    )
    d_send = d_send.astype(jnp.bfloat16).reshape(experts, capacity, -1)
    d_arrived = lax.all_to_all(d_send, "expert", split_axis=0, concat_axis=0, tiled=True)
    d_shaped = d_arrived.reshape(n_expert, local_experts, capacity, -1)
    arrived_rows = outcome[1].reshape(n_expert, local_experts, capacity, -1)
    gate_pre = outcome[2].reshape(n_expert, local_experts, capacity, -1)
    up_pre = outcome[3].reshape(n_expert, local_experts, capacity, -1)
    hidden_rows = outcome[4].reshape(n_expert, local_experts, capacity, -1)
    sigmoid_gate = jax.nn.sigmoid(gate_pre)
    d_hidden = jnp.einsum(
        "nlcd,lfd->nlcf", d_shaped, expert_down, preferred_element_type=jnp.float32
    )
    down_grad = jnp.einsum(
        "nlcf,nlcd->lfd", hidden_rows, d_shaped, preferred_element_type=jnp.float32
    )
    d_gate = (d_hidden * up_pre * sigmoid_gate * (1.0 + gate_pre * (1.0 - sigmoid_gate))).astype(
        jnp.bfloat16
    )
    d_up = (d_hidden * gate_pre * sigmoid_gate).astype(jnp.bfloat16)
    gate_w_grad = jnp.einsum(
        "nlcd,nlcf->ldf", arrived_rows, d_gate, preferred_element_type=jnp.float32
    )
    up_w_grad = jnp.einsum("nlcd,nlcf->ldf", arrived_rows, d_up, preferred_element_type=jnp.float32)
    d_rows = jnp.einsum("nlcf,ldf->nlcd", d_gate, expert_gate, preferred_element_type=jnp.float32)
    d_rows = d_rows + jnp.einsum(
        "nlcf,ldf->nlcd", d_up, expert_up, preferred_element_type=jnp.float32
    )
    d_rows = d_rows.astype(jnp.bfloat16).reshape(experts, capacity, -1)
    d_returned = lax.all_to_all(d_rows, "expert", split_axis=0, concat_axis=0, tiled=True)
    expert_sums = (
        lax.psum(gate_w_grad.astype(jnp.bfloat16), "shard").astype(jnp.float32),
        lax.psum(up_w_grad.astype(jnp.bfloat16), "shard").astype(jnp.float32),
        lax.psum(down_grad.astype(jnp.bfloat16), "shard").astype(jnp.float32),
    )
    d_copies = jnp.take(d_returned.reshape(experts * capacity, -1), slot_id, axis=0).reshape(
        tok_rows, top_count, -1
    )
    d_normed_moe = jnp.sum(d_copies, 1, dtype=jnp.float32)
    d_chosen = gate * (gate_grad - jnp.sum(gate * gate_grad, -1, keepdims=True))
    d_logits = jnp.sum(onehot * d_chosen[:, :, None], 1)
    router_f32 = router_w.astype(jnp.float32)
    d_normed_moe = d_normed_moe + jnp.dot(d_logits, router_f32.T, precision=HIGHEST)
    router_grad = jnp.dot(normed_moe.astype(jnp.float32).T, d_logits, precision=HIGHEST)
    d_mid_norm, gain_moe_grad = norm_backward(d_normed_moe, unit_moe, factor_moe, gain_moe)
    d_mid = grad_out + d_mid_norm
    d_branch = d_mid.astype(jnp.bfloat16)
    out_w_grad = jnp.dot(attended.T, d_branch, preferred_element_type=jnp.float32)
    d_attended = jnp.dot(d_branch, out_w.T, preferred_element_type=jnp.float32).astype(jnp.bfloat16)
    d_attended = d_attended.reshape(tok_rows, KVH, groups, HEAD)
    score_again = score_block(query_heads, key_heads, visible, score_scale)
    prob_again = jnp.exp(score_again - log_total)
    d_probs = jnp.einsum(
        "tkgd,skd->kgts", d_attended, value_heads, preferred_element_type=jnp.float32
    )
    d_scores = (
        prob_again * (d_probs - jnp.sum(prob_again * d_probs, -1, keepdims=True)) * score_scale
    )
    d_scores = d_scores.astype(jnp.bfloat16)
    d_query = jnp.einsum(
        "kgts,skd->tkgd", d_scores, key_heads, preferred_element_type=jnp.float32
    ).reshape(tok_rows, -1)
    d_key_part = jnp.einsum(
        "kgts,tkgd->skd", d_scores, query_heads, preferred_element_type=jnp.float32
    ).reshape(seq_len, -1)
    d_value_part = jnp.einsum(
        "kgts,tkgd->skd",
        prob_again.astype(jnp.bfloat16),
        d_attended,
        preferred_element_type=jnp.float32,
    ).reshape(seq_len, -1)
    d_keys, d_values = (
        lax.psum_scatter(
            d_key_part.astype(jnp.bfloat16), "shard", scatter_dimension=0, tiled=True
        ).astype(jnp.float32),
        lax.psum_scatter(
            d_value_part.astype(jnp.bfloat16), "shard", scatter_dimension=0, tiled=True
        ).astype(jnp.float32),
    )
    d_q_pre = rotate(d_query, cosine_table, -sine_table, HEAD).astype(jnp.bfloat16)
    d_k_pre = rotate(d_keys, cosine_table, -sine_table, HEAD).astype(jnp.bfloat16)
    d_v_pre = d_values.astype(jnp.bfloat16)
    query_grad = jnp.dot(normed.T, d_q_pre, preferred_element_type=jnp.float32)
    key_grad = jnp.dot(normed.T, d_k_pre, preferred_element_type=jnp.float32)
    value_grad = jnp.dot(normed.T, d_v_pre, preferred_element_type=jnp.float32)
    d_normed = jnp.dot(d_q_pre, query_w.T, preferred_element_type=jnp.float32)
    d_normed = d_normed + jnp.dot(d_k_pre, key_w.T, preferred_element_type=jnp.float32)
    d_normed = d_normed + jnp.dot(d_v_pre, value_w.T, preferred_element_type=jnp.float32)
    d_input_norm, gain_attn_grad = norm_backward(d_normed, unit_attn, factor_attn, gain_attn)
    input_grad = d_mid + d_input_norm
    partial_sums = (
        gain_attn_grad,
        gain_moe_grad,
        query_grad,
        key_grad,
        value_grad,
        out_w_grad,
        router_grad,
    )
    summed = lax.psum(
        (
            partial_sums[0],
            partial_sums[1],
            partial_sums[2],
            partial_sums[3],
            partial_sums[4],
            partial_sums[5],
            partial_sums[6],
        ),
        ("expert", "shard"),
    )
    n_shard = lax.axis_size("shard")
    owned_grads = tuple(
        (
            lax.dynamic_slice_in_dim(
                member, shard_index * (member.shape[0] // n_shard), member.shape[0] // n_shard, 0
            )
            for member in summed
        )
    )
    return (
        layer_out,
        input_grad,
        owned_grads[0],
        owned_grads[1],
        owned_grads[2],
        owned_grads[3],
        owned_grads[4],
        owned_grads[5],
        owned_grads[6],
        expert_sums[0],
        expert_sums[1],
        expert_sums[2],
    )


AXES = ("expert", "shard")
N_EXPERT = 8
N_SHARD = 4
LANES = 128
MEBIBYTE = 1 << 20
BF16 = jnp.bfloat16
F32 = jnp.float32


COST_ATTENTION = 17
COST_IN = 1
COST_DOWN = 20
COST_PLACE = 3
COST_PRODUCTS = 5
OUT_BITS = (1, 2, 4)
QUERY_BITS = (1, 2, 4)
LAST_BITS = (1, 2, 4)
EVENTS = (
    "first_far", "branch", "mixed_0", "attention", "sync_1", "sync_2", "sync_3", "sync_4", "key_value", "norms",
    "out", "first_part", "down_send", "query", "notes", "layer", "out", "last_grads", "up_far", "up_send",
    "query", "out", "gate_send", "query", "out", "last_1", "down_total", "query", "up_part", "out", "last_2",
    "query", "down_place", "gate_total", "out", "out_place", "query", "query_place", "up_total", "gate_place",
    "last_3", "up_place",
)


def cost(microseconds):
    return pl.CostEstimate(flops=microseconds * 10**9, bytes_accessed=10**5, transcendentals=0)


def swap(values, expert_bits, shard_bits):
    pairs = [
        (e * N_SHARD + s, (e ^ expert_bits) * N_SHARD + (s ^ shard_bits))
        for e in range(N_EXPERT)
        for s in range(N_SHARD)
    ]
    return lax.ppermute(values, AXES, pairs)


def next_plane(values):
    pairs = [
        (e * N_SHARD + s, ((e + 2) % N_EXPERT) * N_SHARD + s)
        for e in range(N_EXPERT)
        for s in range(N_SHARD)
    ]
    return lax.ppermute(values, AXES, pairs)


def gather_shards(values):
    other_core = swap(values, 0, 1)
    other_y = swap(values, 0, 2)
    return [values, other_core, other_y, swap(other_y, 0, 1)]


def xor_blocks(blocks, index):
    odd = (index & 1) == 1
    high = (index & 2) == 2
    once = [jnp.where(odd, blocks[j ^ 1], blocks[j]) for j in range(4)]
    return [jnp.where(high, once[j ^ 2], once[j]) for j in range(4)]


def together(*values):
    return lax.optimization_barrier(values)


def after(value, *others):
    return lax.optimization_barrier((value,) + others)[0]


def rejoin(mine, partner, low_first):
    return jnp.where(
        low_first,
        jnp.concatenate([mine, partner], 0),
        jnp.concatenate([partner, mine], 0),
    )


def dot_nn(left, right):
    return lax.dot_general(left, right, (((1,), (0,)), ((), ())), preferred_element_type=F32)


def dot_nt(left, right):
    return lax.dot_general(left, right, (((1,), (1,)), ((), ())), preferred_element_type=F32)


def dot_tn(left, right):
    return lax.dot_general(left, right, (((0,), (0,)), ((), ())), preferred_element_type=F32)


def turn(values, cosine, sine):
    return values * cosine + pltpu.roll(values, HEAD // 2, 1) * sine


def attention_forward_body(
    where_ref, h1_ref, w0, w1, w2, w3, key_ref, value_ref, cos_ref, sin_ref, segq_ref, segk_ref,
    query_out, prob_out, attended_out, bias_ref,
):
    rows, seq_len = bias_ref.shape

    @pl.when(pl.program_id(0) == 0)
    def _():
        base = where_ref[0] * rows
        query_pos = base + lax.broadcasted_iota(jnp.int32, (rows, seq_len), 0)
        key_pos = lax.broadcasted_iota(jnp.int32, (rows, seq_len), 1)
        visible = (query_pos >= key_pos) & (segq_ref[...] == segk_ref[...])
        bias_ref[...] = jnp.where(visible, 0.0, MASKED_SCORE)

    depth = w0.shape[0]
    pre = dot_nn(h1_ref[:, :depth], w0[...])
    for j, weight in enumerate((w1, w2, w3)):
        pre = pre + dot_nn(h1_ref[:, (j + 1) * depth : (j + 2) * depth], weight[...])
    for h in range(pre.shape[1] // HEAD):
        cols = slice(h * HEAD, (h + 1) * HEAD)
        query = turn(pre[:, cols], cos_ref[...], sin_ref[...]).astype(BF16)
        query_out[:, cols] = query
        scores = dot_nt(query, key_ref[...]) * HEAD ** (-0.5) + bias_ref[...]
        exponent = jnp.exp(scores - jnp.max(scores, -1, keepdims=True))
        total = jnp.sum(exponent, -1, keepdims=True)
        probs = (exponent * (1.0 / total)).astype(BF16)
        prob_out[h] = probs
        attended_out[:, cols] = dot_nn(probs, value_ref[...]).astype(BF16)


def attention_forward(where, h1_rel, w_query, keys_values, cosine, sine, seg_query, seg_key):
    rows, width = h1_rel.shape
    seq_len = keys_values.shape[0]
    cols = width // N_SHARD
    heads = cols // HEAD

    def whole(shape):
        return pl.BlockSpec(shape, lambda j, w: (0,) * len(shape))

    weight = pl.BlockSpec((cols, cols), lambda j, w: (0, w[0] ^ j))
    part = pl.BlockSpec((rows, cols), lambda j, w: (0, j))
    return pl.pallas_call(
        attention_forward_body,
        grid_spec=pltpu.PrefetchScalarGridSpec(
            num_scalar_prefetch=1,
            grid=(N_SHARD,),
            in_specs=[
                whole((rows, width)), weight, weight, weight, weight,
                pl.BlockSpec((seq_len, HEAD), lambda j, w: (0, (w[0] ^ j) // 2)),
                pl.BlockSpec((seq_len, HEAD), lambda j, w: (0, KVH + (w[0] ^ j) // 2)),
                whole((rows, HEAD)), whole((rows, HEAD)), whole((rows, 1)), whole((1, seq_len)),
            ],
            out_specs=[part, pl.BlockSpec((heads, rows, seq_len), lambda j, w: (j, 0, 0)), part],
            scratch_shapes=[pltpu.VMEM((rows, seq_len), F32)],
        ),
        out_shape=[
            jax.ShapeDtypeStruct((rows, width), BF16),
            jax.ShapeDtypeStruct((HQ, rows, seq_len), BF16),
            jax.ShapeDtypeStruct((rows, width), BF16),
        ],
        compiler_params=pltpu.CompilerParams(vmem_limit_bytes=28 * MEBIBYTE),
        cost_estimate=cost(15),
        name="attention_forward",
    )(where, h1_rel, *w_query, keys_values, keys_values, cosine, sine, seg_query, seg_key)


def attention_backward_body(
    where_ref, branch_ref, out0, out1, out2, out3, attended_ref, query_ref, prob_ref, key_ref, value_ref,
    w0, w1, w2, w3, cos_ref, sin_ref,
    dq_out, dk_out, dv_out, dh_out, dh_acc, dk_acc, dv_acc, da_ref,
):
    step = pl.program_id(0)
    depth = w0.shape[0]
    rows = branch_ref.shape[0]

    for j, weight in enumerate((out0, out1, out2, out3)):

        @pl.when(step == j)
        def _(weight=weight):
            da_ref[...] = dot_nt(branch_ref[...], weight[...]).astype(BF16)

    @pl.when(step % 2 == 0)
    def _():
        dk_acc[...] = jnp.zeros_like(dk_acc)
        dv_acc[...] = jnp.zeros_like(dv_acc)

    @pl.when(step == 0)
    def _():
        dh_acc[...] = jnp.zeros_like(dh_acc)

    d_pre = []
    for h in range(depth // HEAD):
        cols = slice(h * HEAD, (h + 1) * HEAD)
        d_att = da_ref[:, cols]
        probs = prob_ref[h]
        delta = jnp.sum(d_att.astype(F32) * attended_ref[:, cols].astype(F32), -1, keepdims=True)
        d_probs = dot_nt(d_att, value_ref[...])
        d_scores = (probs.astype(F32) * ((d_probs - delta) * HEAD ** (-0.5))).astype(BF16)
        d_query = dot_nn(d_scores, key_ref[...])
        d_pre.append(turn(d_query, cos_ref[...], -sin_ref[...]).astype(BF16))
        dk_acc[...] += dot_tn(query_ref[:, cols], d_scores)
        dv_acc[...] += dot_tn(d_att, probs)
    d_pre = jnp.concatenate(d_pre, 1)
    dq_out[...] = d_pre
    for j, weight in enumerate((w0, w1, w2, w3)):
        dh_acc[:, j * depth : (j + 1) * depth] += dot_nt(d_pre, weight[...])

    @pl.when(step % 2 == 1)
    def _():
        dk_out[...] = dk_acc[...].T.astype(BF16)
        dv_out[...] = dv_acc[...].T.astype(BF16)

    @pl.when(step == N_SHARD - 1)
    def _():
        dh_out[...] = dh_acc[...]


def attention_backward(where, branch, w_out, attended, queries, probs, keys_values, w_query, cosine, sine):
    rows, width = branch.shape
    seq_len = keys_values.shape[0]
    cols = width // N_SHARD
    heads = cols // HEAD

    def whole(shape):
        return pl.BlockSpec(shape, lambda j, w: (0,) * len(shape))

    weight = pl.BlockSpec((cols, cols), lambda j, w: (0, w[0] ^ j))
    part = pl.BlockSpec((rows, cols), lambda j, w: (0, j))
    head_part = pl.BlockSpec((seq_len, HEAD), lambda j, w: (0, (w[0] ^ j) // 2))
    return pl.pallas_call(
        attention_backward_body,
        grid_spec=pltpu.PrefetchScalarGridSpec(
            num_scalar_prefetch=1,
            grid=(N_SHARD,),
            in_specs=[whole((rows, width))] + [whole((cols, width))] * 4 + [
                part, part, pl.BlockSpec((heads, rows, seq_len), lambda j, w: (j, 0, 0)),
                head_part,
                pl.BlockSpec((seq_len, HEAD), lambda j, w: (0, KVH + (w[0] ^ j) // 2)),
                weight, weight, weight, weight, whole((rows, HEAD)), whole((rows, HEAD)),
            ],
            out_specs=[
                pl.BlockSpec((rows, cols), lambda j, w: (0, w[0] ^ j)),
                head_part, head_part, whole((rows, width)),
            ],
            scratch_shapes=[
                pltpu.VMEM((rows, width), F32),
                pltpu.VMEM((HEAD, seq_len), F32),
                pltpu.VMEM((HEAD, seq_len), F32),
                pltpu.VMEM((rows, cols), BF16),
            ],
        ),
        out_shape=[
            jax.ShapeDtypeStruct((rows, width), BF16),
            jax.ShapeDtypeStruct((seq_len, KVH * HEAD), BF16),
            jax.ShapeDtypeStruct((seq_len, KVH * HEAD), BF16),
            jax.ShapeDtypeStruct((rows, width), F32),
        ],
        compiler_params=pltpu.CompilerParams(vmem_limit_bytes=30 * MEBIBYTE),
        cost_estimate=cost(COST_ATTENTION),
        name="attention_backward",
    )(where, branch, *w_out, attended, queries, probs, keys_values, keys_values, *w_query, cosine, sine)


def expert_body(
    where_ref, h2_ref, dy_ref, router_ref, *refs,
):
    own, far = refs[:6], refs[6:12]
    message_out, mixed_out, da_out, db_out, act_out, gates_ref, dh_acc, y_acc, gg_acc = refs[12:]
    e = pl.program_id(0)
    f = pl.program_id(1)
    rows, width = h2_ref.shape
    half = width // 2
    lane = lax.broadcasted_iota(jnp.int32, (rows, LANES), 1)
    places = [pl.ds(pl.multiple_of((where_ref[1] ^ i) * half, LANES), half) for i in range(2)]

    @pl.when((e == 0) & (f == 0))
    def _():
        named = dy_ref[:, width:].astype(F32) > 0.5
        logits = dot_nt(h2_ref[...], router_ref[...])
        logits = jnp.concatenate([logits, jnp.zeros((rows, LANES - logits.shape[1]), F32)], 1)
        logits = jnp.where(named, logits, MASKED_SCORE)
        top = jnp.max(logits, -1, keepdims=True)
        weights = jnp.where(named, jnp.exp(logits - top), 0.0)
        gates_ref[...] = weights / jnp.sum(weights, -1, keepdims=True)
        dh_acc[...] = jnp.zeros_like(dh_acc)
        y_acc[...] = jnp.zeros_like(y_acc)
        gg_acc[...] = jnp.zeros_like(gg_acc)

    here = lane == (where_ref[0] ^ e)

    def work(members):
        gates, ups, downs = [[members[2 * k + i] for i in range(2)] for k in range(3)]
        gate = jnp.sum(jnp.where(here, gates_ref[...], 0.0), -1, keepdims=True)
        h2 = [h2_ref[:, place] for place in places]
        dy = [dy_ref[:, place] for place in places]
        load = lambda ref: ref[...].reshape(ref.shape[-2:])
        a = dot_nn(h2[0], load(gates[0])) + dot_nn(h2[1], load(gates[1]))
        b = dot_nn(h2[0], load(ups[0])) + dot_nn(h2[1], load(ups[1]))
        d_plain = dot_nt(dy[0], load(downs[0])) + dot_nt(dy[1], load(downs[1]))
        sigmoid = 1.0 / (1.0 + jnp.exp(-a))
        silu = a * sigmoid
        act = silu * b
        gate_grad = jnp.sum(act * d_plain, -1, keepdims=True)
        gg_acc[...] += jnp.where(here, gate_grad, 0.0)
        d_act = d_plain * gate
        d_a = (d_act * b * (sigmoid + silu * (1.0 - sigmoid))).astype(BF16)
        d_b = (d_act * silu).astype(BF16)
        scaled = (act * gate).astype(BF16)
        da_out[...] = d_a
        db_out[...] = d_b
        act_out[...] = scaled
        for i in range(2):
            dh_acc[i] += dot_nt(d_a, load(gates[i])) + dot_nt(d_b, load(ups[i]))
            y_acc[i] += dot_nn(scaled, load(downs[i]))

    @pl.when(e == 0)
    def _():
        work(own)

    @pl.when(e == 1)
    def _():
        work(far)

    @pl.when((e == pl.num_programs(0) - 1) & (f == pl.num_programs(1) - 1))
    def _():
        for i in range(2):
            message_out[:, places[i]] = dh_acc[i].astype(BF16)
            mixed_out[:, places[i]] = y_acc[i].astype(BF16)
        high = gg_acc[...].astype(BF16).astype(F32)
        low = pltpu.roll(gg_acc[...] - high, N_EXPERT, 1)
        message_out[:, width:] = (high + low).astype(BF16)


def expert_block(where, h2, dy_routes, router, own, far):
    rows, width = h2.shape
    hidden = own[0].shape[1]
    half = width // 2
    chunk = 256
    chunks = hidden // chunk

    def whole(shape):
        return pl.BlockSpec(shape, lambda e, f, w: (0,) * len(shape))

    own_step = lambda e, f: jnp.where(e == 0, f, chunks - 1)
    far_step = lambda e, f: jnp.where(e == 0, 0, f)
    own_in = [pl.BlockSpec((half, chunk), lambda e, f, w, i=i: (w[1] ^ i, own_step(e, f))) for i in range(2)]
    own_down = [pl.BlockSpec((chunk, half), lambda e, f, w, i=i: (own_step(e, f), w[1] ^ i)) for i in range(2)]
    far_in = [pl.BlockSpec((1, half, chunk), lambda e, f, w, k=k: (k, 0, far_step(e, f))) for k in range(2)]
    far_down = pl.BlockSpec((1, chunk, half), lambda e, f, w: (2, far_step(e, f), 0))
    part = pl.BlockSpec((rows, chunk), lambda e, f, w: (0, e * chunks + f))
    return pl.pallas_call(
        expert_body,
        grid_spec=pltpu.PrefetchScalarGridSpec(
            num_scalar_prefetch=1,
            grid=(2, chunks),
            in_specs=[whole((rows, width)), whole(dy_routes.shape), whole(router.shape)]
            + own_in + own_in + own_down
            + [far_in[0], far_in[0], far_in[1], far_in[1], far_down, far_down],
            out_specs=[whole((rows, width + LANES)), whole((rows, width)), part, part, part],
            scratch_shapes=[
                pltpu.VMEM((rows, LANES), F32),
                pltpu.VMEM((2, rows, half), F32),
                pltpu.VMEM((2, rows, half), F32),
                pltpu.VMEM((rows, LANES), F32),
            ],
        ),
        out_shape=[
            jax.ShapeDtypeStruct((rows, width + LANES), BF16),
            jax.ShapeDtypeStruct((rows, width), BF16),
            jax.ShapeDtypeStruct((rows, 2 * hidden), BF16),
            jax.ShapeDtypeStruct((rows, 2 * hidden), BF16),
            jax.ShapeDtypeStruct((rows, 2 * hidden), BF16),
        ],
        compiler_params=pltpu.CompilerParams(vmem_limit_bytes=28 * MEBIBYTE),
        cost_estimate=cost(20),
        name="expert_block",
    )(
        where, h2, dy_routes, router, own[0], own[0], own[1], own[1], own[2], own[2],
        far[0], far[1], far[0], far[1], far[0], far[1],
    )


def summed_products_body(where_ref, *refs, parts, sets):
    lefts = refs[:parts]
    rights = refs[parts : parts * (1 + sets)]
    outs = refs[parts * (1 + sets) :]
    for k in range(sets):
        total = dot_tn(lefts[0][...], rights[k * parts][...])
        for j in range(1, parts):
            total = total + dot_tn(lefts[j][...], rights[k * parts + j][...])
        out = outs[k]
        if len(out.shape) == 3:
            pieces = out.shape[0]
            deep = out.shape[1]
            for piece in range(pieces):
                out[where_ref[0] ^ piece] = total[piece * deep : (piece + 1) * deep].astype(out.dtype)
        else:
            out[...] = total.astype(out.dtype)


def summed_products(where, lefts, right_sets, grid, left_spec, right_spec, out_spec, out_shape, name):
    parts = len(lefts)
    sets = len(right_sets)
    return pl.pallas_call(
        functools.partial(summed_products_body, parts=parts, sets=sets),
        grid_spec=pltpu.PrefetchScalarGridSpec(
            num_scalar_prefetch=1,
            grid=grid,
            in_specs=[left_spec] * parts + [right_spec] * (parts * sets),
            out_specs=[out_spec] * sets,
        ),
        out_shape=[jax.ShapeDtypeStruct(out_shape, BF16)] * sets,
        compiler_params=pltpu.CompilerParams(vmem_limit_bytes=24 * MEBIBYTE),
        cost_estimate=cost(COST_PRODUCTS),
        name=name,
    )(where, *lefts, *[member for members in right_sets for member in members])


def in_grads_body(where_ref, *refs):
    h2_refs, da_refs, db_refs = refs[:4], refs[4:8], refs[8:12]
    send_ref, keep_ref, turned_ref = refs[12:]
    rows = h2_refs[0].shape[0]
    half = turned_ref.shape[0] // 2

    @pl.when(pl.program_id(0) == 0)
    def _():
        for j in range(4):
            turned_ref[:, j * rows : (j + 1) * rows] = h2_refs[j][...].T

    for k, member in enumerate((da_refs, db_refs)):
        for out, place in ((send_ref, 1 - where_ref[0]), (keep_ref, where_ref[0])):
            here = pl.ds(pl.multiple_of(place * half, LANES), half)
            total = dot_nn(turned_ref[here, :rows], member[0][...])
            for j in range(1, 4):
                total = total + dot_nn(turned_ref[here, j * rows : (j + 1) * rows], member[j][...])
            out[k] = total.astype(BF16)


def expert_in_grads(where, h2, d_a, d_b):
    rows, width = h2[0].shape
    columns = d_a[0].shape[1]
    chunk = 256
    half = width // 2
    part = pl.BlockSpec((rows, chunk), lambda i, w: (0, i))
    out = pl.BlockSpec((2, half, chunk), lambda i, w: (0, 0, i))
    return pl.pallas_call(
        in_grads_body,
        grid_spec=pltpu.PrefetchScalarGridSpec(
            num_scalar_prefetch=1,
            grid=(columns // chunk,),
            in_specs=[pl.BlockSpec((rows, width), lambda i, w: (0, 0))] * 4 + [part] * 8,
            out_specs=[out] * 2,
            scratch_shapes=[pltpu.VMEM((width, 4 * rows), BF16)],
        ),
        out_shape=[jax.ShapeDtypeStruct((2, half, columns), BF16)] * 2,
        compiler_params=pltpu.CompilerParams(vmem_limit_bytes=30 * MEBIBYTE),
        cost_estimate=cost(COST_IN),
        name="expert_in_grads",
    )(where, *h2, *d_a, *d_b)


def down_grads_body(where_ref, *refs):
    act_refs, send_refs, keep_refs = refs[:4], refs[4:8], refs[8:12]
    turned = [act[...].T for act in act_refs]
    for rights, out in ((send_refs, refs[12]), (keep_refs, refs[13])):
        total = dot_nn(turned[0], rights[0][...])
        for j in range(1, 4):
            total = total + dot_nn(turned[j], rights[j][...])
        out[0] = total.astype(BF16)


def expert_down_grads(where, acts, dy_routes):
    rows, columns = acts[0].shape
    width = dy_routes[0].shape[1] - LANES
    half = width // 2
    hidden = columns // 2
    out = pl.BlockSpec((1, hidden, half), lambda e, w: (e, 0, 0))
    return pl.pallas_call(
        down_grads_body,
        grid_spec=pltpu.PrefetchScalarGridSpec(
            num_scalar_prefetch=1,
            grid=(2,),
            in_specs=[pl.BlockSpec((rows, hidden), lambda e, w: (0, e))] * 4
            + [pl.BlockSpec((rows, half), lambda e, w: (0, 1 - w[0]))] * 4
            + [pl.BlockSpec((rows, half), lambda e, w: (0, w[0]))] * 4,
            out_specs=[out, out],
        ),
        out_shape=[jax.ShapeDtypeStruct((2, hidden, half), BF16)] * 2,
        compiler_params=pltpu.CompilerParams(vmem_limit_bytes=26 * MEBIBYTE),
        cost_estimate=cost(COST_DOWN),
        name="expert_down_grads",
    )(where, *acts, *dy_routes, *dy_routes)


class PlaneSum:
    def __init__(self, pieces, order):
        self.shape = pieces.shape[1:]
        self.order = order
        self.axes = [4, 2, 1]
        self.kept = pieces.reshape((2, 2, 2) + self.shape)
        self.step = 0
        self.send()

    def send(self):
        if self.step < 3:
            at = self.axes.index(self.order[self.step])
            self.mine = lax.index_in_dim(self.kept, 0, at, keepdims=False)
            other = lax.index_in_dim(self.kept, 1, at, keepdims=False)
            self.received = swap(other, self.order[self.step], 0)
        else:
            self.received = swap(self.kept, self.order[5 - self.step], 0)

    def receive(self, token):
        received = after(self.received, token)
        if self.step < 3:
            self.kept = (self.mine.astype(F32) + received.astype(F32)).astype(BF16)
            self.axes.remove(self.order[self.step])
        else:
            bit = self.order[5 - self.step]
            if self.step == 5:
                self.done = (self.kept.reshape((4,) + self.shape), received.reshape((4,) + self.shape))
                return received
            at = sum(1 for b in self.axes if b > bit)
            self.kept = jnp.stack([self.kept, received], at)
            self.axes = sorted(self.axes + [bit], reverse=True)
        self.step += 1
        self.send()
        return self.kept


def reorder_body(where_ref, even_ref, odd_ref, out_ref, *, first):
    for b in range(N_EXPERT):
        place = where_ref[0] ^ b
        low = place % first
        index = (place // (2 * first)) * first + low
        odd = (place // first) % 2

        @pl.when(odd == 0)
        def _(b=b, index=index):
            out_ref[b] = even_ref[index].astype(F32)

        @pl.when(odd == 1)
        def _(b=b, index=index):
            out_ref[b] = odd_ref[index].astype(F32)


def reorder(where, even, odd, columns, first):
    deep, width = even.shape[1:]
    results = []
    begin = 0
    for count in columns:
        wide = min(count, 512)
        start = begin // wide
        spec = pl.BlockSpec((N_EXPERT // 2, deep, wide), lambda i, w, start=start: (0, 0, start + i))
        results.append(
            pl.pallas_call(
                functools.partial(reorder_body, first=first),
                grid_spec=pltpu.PrefetchScalarGridSpec(
                    num_scalar_prefetch=1,
                    grid=(count // wide,),
                    in_specs=[spec, spec],
                    out_specs=pl.BlockSpec((N_EXPERT, deep, wide), lambda i, w: (0, 0, i)),
                ),
                out_shape=jax.ShapeDtypeStruct((N_EXPERT, deep, count), F32),
                cost_estimate=cost(COST_PLACE),
                name="reorder",
            )(where, even, odd).reshape(N_EXPERT * deep, count)
        )
        begin += count
    return results


def key_value_grad_body(*refs):
    lefts, rights, out_ref = refs[:4], refs[4:8], refs[8]
    rows, block = lefts[0].shape
    total = dot_tn(lefts[0][...], rights[0][:rows])
    small = rights[0][rows:, :block].astype(F32)
    for j in range(1, 4):
        total = total + dot_tn(lefts[j][...], rights[j][:rows])
        small = small + rights[j][rows:, :block].astype(F32)
    few = small.shape[0] // 2
    out_ref[:block] = total.astype(BF16)
    out_ref[block:, :block] = (small[:few] + small[few:]).astype(BF16)
    out_ref[block:, block:] = jnp.zeros_like(out_ref[block:, block:])


def key_value_grad(lefts, rights, block):
    rows = lefts[0].shape[0]
    columns = rights[0].shape[1]
    few = (rights[0].shape[0] - rows) // 2
    whole = lambda shape: pl.BlockSpec(shape, lambda i: (0, 0))
    return pl.pallas_call(
        key_value_grad_body,
        grid=(1,),
        in_specs=[whole((rows, block))] * 4 + [whole(rights[0].shape)] * 4,
        out_specs=whole((block + few, columns)),
        out_shape=jax.ShapeDtypeStruct((block + few, columns), BF16),
        cost_estimate=cost(COST_PRODUCTS),
        name="key_value_grad",
    )(*lefts, *rights)


def place_body(where_ref, mine_ref, partner_ref, out_ref):
    @pl.when(pl.program_id(0) == 0)
    def _():
        out_ref[...] = mine_ref[0].astype(out_ref.dtype)

    @pl.when(pl.program_id(0) == 1)
    def _():
        out_ref[...] = partner_ref[0].astype(out_ref.dtype)


def place_halves(where, mine, partner, member, by_rows):
    tall, wide = mine.shape[1:]
    cuts = 2
    deep = tall // cuts

    def mine_map(h, i, w):
        return (member, jnp.where(h == 0, i, cuts - 1), 0)

    def partner_map(h, i, w):
        return (member, jnp.where(h == 0, 0, i), 0)

    def out_map(h, i, w):
        return ((w[0] ^ h) * cuts + i, 0) if by_rows else (i, w[0] ^ h)

    return pl.pallas_call(
        place_body,
        grid_spec=pltpu.PrefetchScalarGridSpec(
            num_scalar_prefetch=1,
            grid=(2, cuts),
            in_specs=[pl.BlockSpec((1, deep, wide), mine_map), pl.BlockSpec((1, deep, wide), partner_map)],
            out_specs=pl.BlockSpec((deep, wide), out_map),
        ),
        out_shape=jax.ShapeDtypeStruct((2 * tall, wide) if by_rows else (tall, 2 * wide), F32),
        cost_estimate=cost(COST_PLACE),
        name="place_halves",
    )(where, mine, partner)


def far_halves_body(where_ref, *refs):
    out_ref = refs[-1]
    for k, ref in enumerate(refs[:-1]):

        @pl.when(pl.program_id(0) == k)
        def _(ref=ref):
            out_ref[0] = ref[...]


def far_halves(where, own):
    hidden = own[0].shape[1]
    half = own[0].shape[0] // 2
    cuts = 1
    tall = half // cuts

    def in_map(k):
        step = lambda i, r: jnp.where(i < k, 0, jnp.where(i == k, r, cuts - 1))
        if k == 2:
            return lambda i, r, w: (step(i, r), w[0])
        return lambda i, r, w: (w[0] * cuts + step(i, r), 0)

    return pl.pallas_call(
        far_halves_body,
        grid_spec=pltpu.PrefetchScalarGridSpec(
            num_scalar_prefetch=1,
            grid=(3, cuts),
            in_specs=[pl.BlockSpec((tall, hidden), in_map(k)) for k in range(3)],
            out_specs=pl.BlockSpec((1, tall, hidden), lambda i, r, w: (i, r, 0)),
        ),
        out_shape=jax.ShapeDtypeStruct((3, half, hidden), BF16),
        cost_estimate=cost(3),
        name="far_halves",
    )(where, *own)


def pack_body(key_ref, value_ref, small_ref, out_ref):
    rows, low = key_ref.shape
    out_ref[:rows, :low] = key_ref[...]
    out_ref[:rows, low:] = value_ref[...]
    out_ref[rows:, : small_ref.shape[1]] = small_ref[...]
    out_ref[rows:, small_ref.shape[1] :] = jnp.zeros_like(out_ref[rows:, small_ref.shape[1] :])


def pack(w_key, w_value, small):
    rows, low = w_key.shape
    return pl.pallas_call(
        pack_body,
        out_shape=jax.ShapeDtypeStruct((rows + small.shape[0], 2 * low), BF16),
        cost_estimate=cost(2),
        name="pack",
    )(w_key, w_value, small)


def plus(part, received):
    return (part.astype(F32) + received.astype(F32)).astype(BF16)


def on_device_rings(
    hidden_in, segment_ids, routes, attn_gain, moe_gain, w_query, w_key, w_value, w_out, w_router,
    expert_gate, expert_up, expert_down, out_grad,
):
    rows, width = hidden_in.shape
    experts = w_router.shape[1]
    shard = lax.axis_index("shard")
    expert = lax.axis_index("expert")
    core = shard % 2
    where_shard = shard.astype(jnp.int32)[None]
    where_expert = expert.astype(jnp.int32)[None]
    where_core = core.astype(jnp.int32)[None]
    where_far_core = 1 - where_core
    block = width // N_SHARD
    low = KVH * HEAD

    own = (expert_gate[0], expert_up[0], expert_down[0])
    far_send = far_halves(where_core, own)
    far_part = swap(far_send, 1, 0)
    small = jnp.concatenate(
        [w_router.T, attn_gain[None], moe_gain[None], jnp.zeros((6, block), BF16)], 0
    )
    packed_own = pack(after(w_key, far_send), w_value, small)
    packed_y = swap(packed_own, 0, 2)
    mask = (routes[:, :, None] == jnp.arange(LANES, dtype=jnp.int32)[None, None, :]).any(1)
    dy_routes = [jnp.concatenate([out_grad, mask.astype(BF16)], 1)]
    for _ in range(3):
        dy_routes.append(next_plane(dy_routes[-1]))
    query_w_core = swap(w_query, 0, 1)
    out_w_core = swap(w_out, 0, 1)
    query_w_y = swap(after(w_query, packed_y), 0, 2)
    packed_pair = swap(jnp.concatenate([packed_own, packed_y], 0), 0, 1)
    tall = packed_own.shape[0]
    packed = [packed_own, packed_pair[:tall], packed_y, packed_pair[tall:]]

    inputs = hidden_in.astype(F32)
    factor_attn = lax.rsqrt(jnp.mean(inputs * inputs, -1, keepdims=True) + EPSILON)
    unit_rel = jnp.concatenate(
        xor_blocks([inputs[:, j * block : (j + 1) * block] for j in range(4)], shard), 1
    ) * factor_attn
    gain_rel = jnp.concatenate([member[block + experts : block + experts + 1, :block] for member in packed], 1)
    gain_rel = gain_rel.astype(F32)
    h1_rel = after((unit_rel * gain_rel).astype(BF16), query_w_core, out_w_core)
    key_value_w = [member[:block] for member in packed]
    pre = sum(dot_nn(h1_rel[:, j * block : (j + 1) * block], key_value_w[j]) for j in range(4))
    positions = shard * rows + jnp.arange(rows, dtype=jnp.int32)
    cosine, sine = rope_tables(positions, HEAD)
    key_local = rotate(pre[:, :low], cosine, sine, HEAD)
    key_value = jnp.concatenate([key_local, pre[:, low:]], 1).astype(BF16)
    key_value = after(key_value, dy_routes[1])
    key_value_y = swap(key_value, 0, 2)
    query_w = [w_query, query_w_core, query_w_y, swap(query_w_y, 0, 1)]
    key_value_pair = swap(jnp.concatenate([key_value, key_value_y], 0), 0, 1)
    keys_values = jnp.concatenate(
        xor_blocks([key_value, key_value_pair[:rows], key_value_y, key_value_pair[rows:]], shard), 0
    )
    out_w_y = swap(after(w_out, query_w_y, key_value), 0, 2)
    cosine_row = jnp.concatenate([cosine, cosine], 1)
    sine_row = jnp.concatenate([-sine, sine], 1)
    seg_query = lax.dynamic_slice_in_dim(segment_ids, shard * rows, rows)[:, None]
    queries, probs, attended = attention_forward(
        where_shard, after(h1_rel, dy_routes[2]), query_w, keys_values, cosine_row, sine_row, seg_query, segment_ids[None, :]
    )
    attended_late = after(attended, dy_routes[3])
    out_w_y = after(out_w_y, attended)
    out_w = [w_out, out_w_core, out_w_y, swap(out_w_y, 0, 1)]
    mid_state = inputs + sum(
        dot_nn(attended_late[:, j * block : (j + 1) * block], out_w[j]) for j in range(4)
    )
    factor_moe = lax.rsqrt(jnp.mean(mid_state * mid_state, -1, keepdims=True) + EPSILON)
    unit_moe = mid_state * factor_moe
    small_true = jnp.concatenate(xor_blocks([member[block:, :block] for member in packed], shard), 1)
    gain_moe = small_true[experts + 1 : experts + 2].astype(F32)
    router = small_true[:experts].astype(F32)
    h2 = [(unit_moe * gain_moe).astype(BF16)]

    far_part = after(far_part, attended)
    far_other = swap(far_part, 0, 1)
    hidden = own[0].shape[1]
    deep = width // 2
    far = (far_part, far_other)
    where_pair = jnp.stack([expert, core]).astype(jnp.int32)

    mixer_rows = [
        jnp.concatenate([h1_rel[:, j * block : (j + 1) * block], attended[:, j * block : (j + 1) * block]], 1)
        for j in range(4)
    ]
    mixer_rows = [mixer_rows[0]] + [swap(mixer_rows[j], 0, j) for j in (1, 2, 3)]
    add = lambda a, b: (a.astype(F32) + b.astype(F32)).astype(BF16)
    block_of = lambda j, *ready: expert_block(
        where_pair, after(h2[j], *ready), dy_routes[j], small_true, own, far
    )
    h2.append(next_plane(h2[0]))
    done = [block_of(0)]
    h2.append(next_plane(after(h2[1], done[0][0])))
    done.append(block_of(1, done[0][0], *mixer_rows))
    h2[2] = after(h2[2], done[1][0])
    h2.append(next_plane(h2[2]))
    message = next_plane(after(done[1][0], h2[2]))
    done.append(block_of(2, done[1][0]))
    done.append(block_of(3, done[2][0]))
    second = add(done[2][0], after(message, done[3][0]))
    message = next_plane(second)

    acts = [done[j][4] for j in range(4)]
    down_send, down_keep = expert_down_grads(after(where_core, second), acts, dy_routes)
    in_send, in_keep = expert_in_grads(
        after(where_core, down_send), h2, [done[j][2] for j in range(4)], [done[j][3] for j in range(4)]
    )
    third = add(done[3][0], after(message, in_send))
    message = next_plane(third)
    v = types.SimpleNamespace(
        down_swap=swap(after(down_send, third), 0, 1), in_swap=swap(after(in_send, third), 0, 1)
    )

    def mixer_grads(half, rights, name):
        n = rights[0].shape[1]
        (pieces,) = summed_products(
            where_expert, mixer_rows, [rights], (n // 512,),
            pl.BlockSpec((rows, block), lambda i, w: (0, half)),
            pl.BlockSpec((rows, 512), lambda i, w: (0, i)),
            pl.BlockSpec((N_EXPERT, block // N_EXPERT, 512), lambda i, w: (0, 0, i)),
            (N_EXPERT, block // N_EXPERT, n), name,
        )
        return pieces


    def first_far(token):
        v.down_swap, v.in_swap, token = together(v.down_swap, v.in_swap, token)
        far = jnp.stack(
            [plus(down_keep[1], v.down_swap[1]), plus(in_keep[0, :, hidden:], v.in_swap[0, :, hidden:])]
        )
        v.first_received = swap(far, 1, 0)
        return far

    def up_far(token):
        v.in_swap = after(v.in_swap, token)
        v.up_far = plus(in_keep[1, :, hidden:], v.in_swap[1, :, hidden:])
        return v.up_far

    def up_send(token):
        v.up_received = swap(after(v.up_far, token), 1, 0)
        return token

    def branch(token):
        total = done[0][0].astype(F32) + after(message, token).astype(F32)
        named = mask[:, :experts]
        logits = jnp.where(named, dot_nt(h2[0], small_true[:experts]), MASKED_SCORE)
        weights = jnp.where(named, jnp.exp(logits - jnp.max(logits, -1, keepdims=True)), 0.0)
        gate = weights / jnp.sum(weights, -1, keepdims=True)
        gate_grad = total[:, width : width + experts] + total[:, width + experts : width + 2 * experts]
        d_logits = gate * (gate_grad - jnp.sum(gate * gate_grad, -1, keepdims=True))
        d_h2 = total[:, :width] + jnp.dot(d_logits, router, precision=HIGHEST)
        v.router_grad = jnp.dot(d_logits.T, h2[0].astype(F32), precision=HIGHEST)
        d_mid_norm, v.gain_moe_grad = norm_backward(d_h2, unit_moe, factor_moe, gain_moe)
        v.d_mid = out_grad.astype(F32) + d_mid_norm
        v.d_branch = v.d_mid.astype(BF16)
        v.branch_core = swap(v.d_branch, 0, 1)
        v.branch_y = swap(v.d_branch, 0, 2)
        return v.d_branch

    def mixed_0(token):
        v.mixed = next_plane(after(done[1][1], token))
        return token

    def attention(token):
        v.d_q_pre, v.d_key_part, v.d_value_part, v.d_normed = attention_backward(
            where_shard, after(v.d_branch, token), out_w, attended, queries, probs, keys_values, query_w,
            cosine_row, sine_row,
        )
        return v.d_q_pre

    def sync_1(token):
        v.d_q_pre, v.d_key_part, v.d_value_part, v.branch_y, v.branch_core, v.mixed = together(
            v.d_q_pre, v.d_key_part, v.d_value_part, v.branch_y, v.branch_core, v.mixed
        )
        v.d_q_y = swap(v.d_q_pre, 0, 2)
        v.d_q_core = swap(v.d_q_pre, 0, 1)
        v.branch_far = swap(v.branch_y, 0, 1)
        d_parts = jnp.concatenate([v.d_key_part, v.d_value_part], 1).reshape(N_SHARD, rows, 2 * low)
        v.d_rel = xor_blocks([d_parts[j] for j in range(4)], shard)
        v.from_core = swap(jnp.stack([v.d_rel[1], v.d_rel[3]]), 0, 1)
        v.mixed = add(done[2][1], v.mixed)
        return v.d_q_pre

    def sync_2(token):
        v.d_q_core, v.branch_far, v.from_core, v.mixed = together(
            v.d_q_core, v.branch_far, v.from_core, v.mixed
        )
        v.mixed = next_plane(v.mixed)
        d_far = add(v.d_rel[2], v.from_core[1])
        v.d_far_y = swap(d_far, 0, 2)
        rights = [v.d_branch, v.branch_core, v.branch_y, after(v.branch_far, d_far)]
        v.out_pieces = mixer_grads(1, rights, "w_out_grad")
        return v.out_pieces

    def sync_3(token):
        v.d_q_y, v.out_pieces, v.mixed, token = together(v.d_q_y, v.out_pieces, v.mixed, token)
        v.out_sum = PlaneSum(v.out_pieces, OUT_BITS)
        v.mixed = next_plane(add(done[3][1], v.mixed))
        rights = [v.d_q_pre, v.d_q_core, v.d_q_y, swap(v.d_q_y, 0, 1)]
        v.query_pieces = mixer_grads(0, rights, "w_query_grad")
        return v.query_pieces

    def sync_4(token):
        v.query_pieces, v.d_far_y, token = together(v.query_pieces, v.d_far_y, token)
        v.query_sum = PlaneSum(v.query_pieces, QUERY_BITS)
        return v.query_pieces

    def first_part(token):
        received = after(v.first_received, token)
        down = down_keep[0].astype(F32) + v.down_swap[0].astype(F32) + received[0].astype(F32)
        gate = in_keep[0, :, :hidden].astype(F32) + v.in_swap[0, :, :hidden].astype(F32) + received[1].astype(F32)
        v.down_part, v.gate_part = together(down.astype(BF16), gate.astype(BF16))
        return v.down_part

    def down_send(token):
        v.down_y = swap(after(v.down_part, token), 0, 2)
        return token

    def gate_send(token):
        v.gate_y = swap(after(v.gate_part, token), 0, 2)
        return token

    def down_total(token):
        v.down_total = plus(v.down_part, after(v.down_y, token))
        v.down_core = swap(v.down_total, 0, 1)
        return v.down_total

    def gate_total(token):
        v.gate_total = plus(v.gate_part, after(v.gate_y, token))
        v.gate_core = swap(v.gate_total, 0, 1)
        return v.gate_total

    def layer(token):
        mixed = after(v.mixed, token).astype(F32)
        v.layer_out = (mid_state + done[0][1].astype(F32) + mixed).astype(BF16)
        return v.layer_out

    def up_part(token):
        own_part = in_keep[1, :, :hidden].astype(F32) + v.in_swap[1, :, :hidden].astype(F32)
        v.up_part = plus(own_part, after(v.up_received, token))
        v.up_y = swap(v.up_part, 0, 2)
        return v.up_part

    def up_total(token):
        v.up_total = plus(v.up_part, after(v.up_y, token))
        v.up_core = swap(v.up_total, 0, 1)
        return v.up_total

    def down_place(token):
        v.down_sum = place_halves(where_core, v.down_total[None], after(v.down_core, token)[None], 0, False)[None]
        return v.down_sum

    def gate_place(token):
        v.gate_sum = place_halves(where_core, v.gate_total[None], after(v.gate_core, token)[None], 0, True)[None]
        return v.gate_sum

    def up_place(token):
        v.up_sum = place_halves(where_core, v.up_total[None], after(v.up_core, token)[None], 0, True)[None]
        return v.up_sum

    def key_value(token):
        d_key_value = v.d_rel[0].astype(F32) + v.from_core[0].astype(F32) + after(v.d_far_y, token).astype(F32)
        d_k_pre = rotate(d_key_value[:, :low], cosine, -sine, HEAD)
        v.d_kv_pre = jnp.concatenate([d_k_pre, d_key_value[:, low:]], 1).astype(BF16)
        return v.d_kv_pre

    def norms(token):
        d_kv_pre = after(v.d_kv_pre, token)
        d_normed = v.d_normed + jnp.concatenate([dot_nt(d_kv_pre, member) for member in key_value_w], 1)
        d_input_norm, gain_attn_grad = norm_backward(d_normed, unit_rel, factor_attn, gain_rel)
        d_input_norm = jnp.concatenate(
            xor_blocks([d_input_norm[:, j * block : (j + 1) * block] for j in range(4)], shard), 1
        )
        v.input_grad = v.d_mid + d_input_norm
        rest = jnp.concatenate([v.gain_moe_grad[None], v.router_grad, jnp.zeros((6, width), F32)], 0)
        rest = xor_blocks([rest[:, j * block : (j + 1) * block] for j in range(4)], shard)
        v.notes = []
        for j in range(4):
            piece = jnp.concatenate([gain_attn_grad[None, j * block : (j + 1) * block], rest[j]], 0)
            high = piece.astype(BF16)
            piece = jnp.concatenate([high, (piece - high.astype(F32)).astype(BF16)], 0)
            v.notes.append(jnp.concatenate([d_kv_pre, jnp.pad(piece, ((0, 0), (0, 2 * low - block)))], 0))
        v.notes_y = swap(jnp.concatenate([v.notes[2], v.notes[3]], 0), 0, 2)
        return v.notes[0]

    def notes(token):
        tall = v.notes[0].shape[0]
        v.notes_y, token = together(v.notes_y, token)
        v.notes_core = swap(jnp.concatenate([v.notes[1], v.notes_y[tall:]], 0), 0, 1)
        return token

    def last_grads(token):
        tall = v.notes[0].shape[0]
        core_part = after(v.notes_core, token)
        v.last = key_value_grad(
            mixer_rows, [v.notes[0], core_part[:tall], v.notes_y[:tall], core_part[tall:]], block
        )
        v.last_far = swap(v.last, LAST_BITS[0], 0)
        return v.last

    def last_1(token):
        v.last = plus(v.last, after(v.last_far, token))
        v.last_far = swap(v.last, LAST_BITS[1], 0)
        return v.last

    def last_2(token):
        v.last = plus(v.last, after(v.last_far, token))
        v.last_far = swap(v.last, LAST_BITS[2], 0)
        return v.last

    def last_3(token):
        v.last = v.last.astype(F32) + after(v.last_far, token).astype(F32)
        return v.last

    def query(token):
        return v.query_sum.receive(token)

    def out(token):
        return v.out_sum.receive(token)

    def query_place(token):
        even, odd = v.query_sum.done
        (v.query_grad,) = reorder(where_expert, after(even, token), odd, (width,), QUERY_BITS[0])
        return v.query_grad

    def out_place(token):
        even, odd = v.out_sum.done
        (v.out_w_grad,) = reorder(where_expert, after(even, token), odd, (width,), OUT_BITS[0])
        return v.out_w_grad

    steps = locals()
    token = third
    for name in EVENTS:
        token = steps[name](token)
    layer_out, input_grad, query_grad, out_w_grad = v.layer_out, v.input_grad, v.query_grad, v.out_w_grad
    gate_sum, up_sum, down_sum, last = v.gate_sum, v.up_sum, v.down_sum, v.last
    small_sums = last[block:, :block]
    return (
        layer_out,
        input_grad,
        small_sums[0],
        small_sums[1],
        query_grad,
        last[:block, :low],
        last[:block, low:],
        out_w_grad,
        small_sums[2 : 2 + experts].T,
        gate_sum,
        up_sum,
        down_sum,
    )


def on_device(hidden_in, segment_ids, routes, *rest):
    rows = hidden_in.shape[0]
    experts = rest[6].shape[1]
    capacity = rows * routes.shape[1] * 2 // experts
    shape = (lax.axis_size("expert"), lax.axis_size("shard"))
    if shape == (N_EXPERT, N_SHARD) and experts == N_EXPERT and capacity == rows:
        return on_device_rings(hidden_in, segment_ids, routes, *rest)
    return on_device_routed(hidden_in, segment_ids, routes, *rest)


def solution(mesh):
    placed = (
        P(("expert", "shard"), None),
        P("expert"),
        P(("expert", "shard"), None),
        P("shard"),
        P("shard"),
        P("shard", None),
        P("shard", None),
        P("shard", None),
        P("shard", None),
        P("shard", None),
        P("expert", None, None),
        P("expert", None, None),
        P("expert", None, None),
        P(("expert", "shard"), None),
    )
    return jax.shard_map(
        on_device,
        mesh=mesh,
        in_specs=placed,
        out_specs=(
            P(("expert", "shard"), None),
            P(("expert", "shard"), None),
            P("shard"),
            P("shard"),
            P("shard", None),
            P("shard", None),
            P("shard", None),
            P("shard", None),
            P("shard", None),
            P("expert", None, None),
            P("expert", None, None),
            P("expert", None, None),
        ),
        check_vma=False,
    )
```

```python
import functools
import types

import jax
import jax.numpy as jnp
from jax import lax
from jax.experimental import pallas as pl
from jax.experimental.pallas import tpu as pltpu
from jax.sharding import PartitionSpec as P

HQ = 12
KVH = 2
HEAD = 128


EPSILON = 1e-06
ROPE_BASE = 10000.0
MASKED_SCORE = -1e30
HIGHEST = lax.Precision.HIGHEST


def rope_tables(positions, head_size):
    half_size = head_size // 2
    frequency = ROPE_BASE ** (-(jnp.arange(half_size, dtype=jnp.float32) * 2.0 / head_size))
    angles = positions.astype(jnp.float32)[:, None] * frequency[None, :]
    return (jnp.cos(angles), jnp.sin(angles))


def rotate(values, cosine_table, sine_table, head_size):
    rows_count = values.shape[0]
    shaped = values.reshape(rows_count, -1, head_size)
    half_size = head_size // 2
    first_half = shaped[..., :half_size]
    second_half = shaped[..., half_size:]
    cosine_part = cosine_table[:, None, :]
    sine_part = sine_table[:, None, :]
    turned = jnp.concatenate(
        [
            first_half * cosine_part - second_half * sine_part,
            second_half * cosine_part + first_half * sine_part,
        ],
        -1,
    )
    return turned.reshape(rows_count, -1)


def norm_forward(values, gain):
    factor = lax.rsqrt(jnp.mean(values * values, -1, keepdims=True) + EPSILON)
    unit_rows = values * factor
    return (unit_rows, factor, (unit_rows * gain).astype(jnp.bfloat16))


def norm_backward(grad_rows, unit_rows, factor, gain):
    gain_grad = jnp.sum(grad_rows * unit_rows, 0)
    scaled_grad = grad_rows * gain
    return (
        factor * (scaled_grad - unit_rows * jnp.mean(scaled_grad * unit_rows, -1, keepdims=True)),
        gain_grad,
    )


def score_block(query_heads, key_heads, visible, score_scale):
    raw_scores = jnp.einsum(
        "tkgd,skd->kgts", query_heads, key_heads, preferred_element_type=jnp.float32
    )
    return jnp.where(visible, raw_scores * score_scale, MASKED_SCORE)


def on_device_routed(
    hidden_in,
    segment_ids,
    routes,
    attn_gain,
    moe_gain,
    w_query,
    w_key,
    w_value,
    w_out,
    w_router,
    expert_gate,
    expert_up,
    expert_down,
    out_grad,
):
    tok_rows = hidden_in.shape[0]
    top_count = routes.shape[1]
    experts = w_router.shape[1]
    capacity = tok_rows * top_count * 2 // experts
    groups = HQ // KVH
    score_scale = HEAD ** (-0.5)
    shard_index = lax.axis_index("shard")
    n_expert = lax.axis_size("expert")
    local_experts = expert_gate.shape[0]
    gain_attn, gain_moe, query_w, key_w, value_w, out_w, router_w = (
        lax.all_gather(attn_gain, "shard", axis=0, tiled=True),
        lax.all_gather(moe_gain, "shard", axis=0, tiled=True),
        lax.all_gather(w_query, "shard", axis=0, tiled=True),
        lax.all_gather(w_key, "shard", axis=0, tiled=True),
        lax.all_gather(w_value, "shard", axis=0, tiled=True),
        lax.all_gather(w_out, "shard", axis=0, tiled=True),
        lax.all_gather(w_router, "shard", axis=0, tiled=True),
    )
    gain_attn = gain_attn.astype(jnp.float32)
    gain_moe = gain_moe.astype(jnp.float32)
    inputs = hidden_in.astype(jnp.float32)
    unit_attn, factor_attn, normed = norm_forward(inputs, gain_attn)
    q_pre = jnp.dot(normed, query_w, preferred_element_type=jnp.float32)
    k_pre = jnp.dot(normed, key_w, preferred_element_type=jnp.float32)
    value_rows = jnp.dot(normed, value_w, preferred_element_type=jnp.float32).astype(jnp.bfloat16)
    positions = shard_index * tok_rows + jnp.arange(tok_rows, dtype=jnp.int32)
    cosine_table, sine_table = rope_tables(positions, HEAD)
    queries = rotate(q_pre, cosine_table, sine_table, HEAD).astype(jnp.bfloat16)
    key_local = rotate(k_pre, cosine_table, sine_table, HEAD).astype(jnp.bfloat16)
    key_rows, value_all = (
        lax.all_gather(key_local, "shard", axis=0, tiled=True),
        lax.all_gather(value_rows, "shard", axis=0, tiled=True),
    )
    seq_len = key_rows.shape[0]
    query_heads = queries.reshape(tok_rows, KVH, groups, HEAD)
    key_heads = key_rows.reshape(seq_len, KVH, HEAD)
    value_heads = value_all.reshape(seq_len, KVH, HEAD)
    seg_local = lax.dynamic_slice_in_dim(segment_ids, shard_index * tok_rows, tok_rows)
    visible = (positions[:, None] >= jnp.arange(seq_len, dtype=jnp.int32)[None, :]) & (
        seg_local[:, None] == segment_ids[None, :]
    )
    score_values = score_block(query_heads, key_heads, visible, score_scale)
    top_score = jnp.max(score_values, -1, keepdims=True)
    exponent = jnp.exp(score_values - top_score)
    denominators = jnp.sum(exponent, -1, keepdims=True)
    probabilities = exponent / denominators
    log_total = top_score + jnp.log(denominators)
    attended = (
        jnp.einsum(
            "kgts,skd->tkgd",
            probabilities.astype(jnp.bfloat16),
            value_heads,
            preferred_element_type=jnp.float32,
        )
        .reshape(tok_rows, -1)
        .astype(jnp.bfloat16)
    )
    mid_state = inputs + jnp.dot(attended, out_w, preferred_element_type=jnp.float32)
    unit_moe, factor_moe, normed_moe = norm_forward(mid_state, gain_moe)
    logits = jnp.dot(normed_moe, router_w, preferred_element_type=jnp.float32)
    onehot = (routes[:, :, None] == jnp.arange(experts, dtype=jnp.int32)[None, None, :]).astype(
        jnp.float32
    )
    chosen = jnp.sum(onehot * logits[:, None, :], -1)
    chosen = chosen - jnp.max(chosen, -1, keepdims=True)
    weights = jnp.exp(chosen)
    gate = weights / jnp.sum(weights, -1, keepdims=True)
    flat_routes = routes.reshape(-1)
    route_hot = (flat_routes[:, None] == jnp.arange(experts, dtype=jnp.int32)[None, :]).astype(
        jnp.int32
    )
    before = jnp.cumsum(route_hot, 0, dtype=jnp.int32) - route_hot
    slot_id = flat_routes * capacity + jnp.sum(before * route_hot, 1, dtype=jnp.int32)
    source = (
        jnp.zeros((experts * capacity,), jnp.int32)
        .at[slot_id]
        .set(jnp.arange(tok_rows * top_count, dtype=jnp.int32))
    )
    filled = jnp.zeros((experts * capacity,), jnp.bool_).at[slot_id].set(True)
    outgoing = jnp.where(filled[:, None], jnp.take(normed_moe, source // top_count, axis=0), 0)
    outgoing = outgoing.reshape(experts, capacity, -1)
    arrived = lax.all_to_all(outgoing, "expert", split_axis=0, concat_axis=0, tiled=True)
    item_count = arrived.shape[1]
    shaped = arrived.reshape(n_expert, local_experts, item_count, -1)
    gate_pre = jnp.einsum("nlcd,ldf->nlcf", shaped, expert_gate, preferred_element_type=jnp.float32)
    up_pre = jnp.einsum("nlcd,ldf->nlcf", shaped, expert_up, preferred_element_type=jnp.float32)
    hidden_rows = (gate_pre * jax.nn.sigmoid(gate_pre) * up_pre).astype(jnp.bfloat16)
    result = jnp.einsum(
        "nlcf,lfd->nlcd", hidden_rows, expert_down, preferred_element_type=jnp.float32
    )
    result = result.astype(jnp.bfloat16).reshape(arrived.shape)
    returned = lax.all_to_all(result, "expert", split_axis=0, concat_axis=0, tiled=True)
    outcome = (
        returned,
        arrived,
        gate_pre.reshape(n_expert * local_experts, item_count, -1),
        up_pre.reshape(n_expert * local_experts, item_count, -1),
        hidden_rows.reshape(n_expert * local_experts, item_count, -1),
    )
    returned_rows = jnp.take(outcome[0].reshape(experts * capacity, -1), slot_id, axis=0).reshape(
        tok_rows, top_count, -1
    )
    mixed = mid_state + jnp.sum(gate[:, :, None] * returned_rows, 1)
    layer_out = mixed.astype(jnp.bfloat16)
    grad_out = out_grad.astype(jnp.float32)
    gate_grad = jnp.sum(returned_rows * grad_out[:, None, :], -1)
    gate_slots = jnp.take(gate.reshape(-1), source, axis=0)
    d_send = jnp.where(
        filled[:, None], jnp.take(grad_out, source // top_count, axis=0) * gate_slots[:, None], 0.0
    )
    d_send = d_send.astype(jnp.bfloat16).reshape(experts, capacity, -1)
    d_arrived = lax.all_to_all(d_send, "expert", split_axis=0, concat_axis=0, tiled=True)
    d_shaped = d_arrived.reshape(n_expert, local_experts, capacity, -1)
    arrived_rows = outcome[1].reshape(n_expert, local_experts, capacity, -1)
    gate_pre = outcome[2].reshape(n_expert, local_experts, capacity, -1)
    up_pre = outcome[3].reshape(n_expert, local_experts, capacity, -1)
    hidden_rows = outcome[4].reshape(n_expert, local_experts, capacity, -1)
    sigmoid_gate = jax.nn.sigmoid(gate_pre)
    d_hidden = jnp.einsum(
        "nlcd,lfd->nlcf", d_shaped, expert_down, preferred_element_type=jnp.float32
    )
    down_grad = jnp.einsum(
        "nlcf,nlcd->lfd", hidden_rows, d_shaped, preferred_element_type=jnp.float32
    )
    d_gate = (d_hidden * up_pre * sigmoid_gate * (1.0 + gate_pre * (1.0 - sigmoid_gate))).astype(
        jnp.bfloat16
    )
    d_up = (d_hidden * gate_pre * sigmoid_gate).astype(jnp.bfloat16)
    gate_w_grad = jnp.einsum(
        "nlcd,nlcf->ldf", arrived_rows, d_gate, preferred_element_type=jnp.float32
    )
    up_w_grad = jnp.einsum("nlcd,nlcf->ldf", arrived_rows, d_up, preferred_element_type=jnp.float32)
    d_rows = jnp.einsum("nlcf,ldf->nlcd", d_gate, expert_gate, preferred_element_type=jnp.float32)
    d_rows = d_rows + jnp.einsum(
        "nlcf,ldf->nlcd", d_up, expert_up, preferred_element_type=jnp.float32
    )
    d_rows = d_rows.astype(jnp.bfloat16).reshape(experts, capacity, -1)
    d_returned = lax.all_to_all(d_rows, "expert", split_axis=0, concat_axis=0, tiled=True)
    expert_sums = (
        lax.psum(gate_w_grad.astype(jnp.bfloat16), "shard").astype(jnp.float32),
        lax.psum(up_w_grad.astype(jnp.bfloat16), "shard").astype(jnp.float32),
        lax.psum(down_grad.astype(jnp.bfloat16), "shard").astype(jnp.float32),
    )
    d_copies = jnp.take(d_returned.reshape(experts * capacity, -1), slot_id, axis=0).reshape(
        tok_rows, top_count, -1
    )
    d_normed_moe = jnp.sum(d_copies, 1, dtype=jnp.float32)
    d_chosen = gate * (gate_grad - jnp.sum(gate * gate_grad, -1, keepdims=True))
    d_logits = jnp.sum(onehot * d_chosen[:, :, None], 1)
    router_f32 = router_w.astype(jnp.float32)
    d_normed_moe = d_normed_moe + jnp.dot(d_logits, router_f32.T, precision=HIGHEST)
    router_grad = jnp.dot(normed_moe.astype(jnp.float32).T, d_logits, precision=HIGHEST)
    d_mid_norm, gain_moe_grad = norm_backward(d_normed_moe, unit_moe, factor_moe, gain_moe)
    d_mid = grad_out + d_mid_norm
    d_branch = d_mid.astype(jnp.bfloat16)
    out_w_grad = jnp.dot(attended.T, d_branch, preferred_element_type=jnp.float32)
    d_attended = jnp.dot(d_branch, out_w.T, preferred_element_type=jnp.float32).astype(jnp.bfloat16)
    d_attended = d_attended.reshape(tok_rows, KVH, groups, HEAD)
    score_again = score_block(query_heads, key_heads, visible, score_scale)
    prob_again = jnp.exp(score_again - log_total)
    d_probs = jnp.einsum(
        "tkgd,skd->kgts", d_attended, value_heads, preferred_element_type=jnp.float32
    )
    d_scores = (
        prob_again * (d_probs - jnp.sum(prob_again * d_probs, -1, keepdims=True)) * score_scale
    )
    d_scores = d_scores.astype(jnp.bfloat16)
    d_query = jnp.einsum(
        "kgts,skd->tkgd", d_scores, key_heads, preferred_element_type=jnp.float32
    ).reshape(tok_rows, -1)
    d_key_part = jnp.einsum(
        "kgts,tkgd->skd", d_scores, query_heads, preferred_element_type=jnp.float32
    ).reshape(seq_len, -1)
    d_value_part = jnp.einsum(
        "kgts,tkgd->skd",
        prob_again.astype(jnp.bfloat16),
        d_attended,
        preferred_element_type=jnp.float32,
    ).reshape(seq_len, -1)
    d_keys, d_values = (
        lax.psum_scatter(
            d_key_part.astype(jnp.bfloat16), "shard", scatter_dimension=0, tiled=True
        ).astype(jnp.float32),
        lax.psum_scatter(
            d_value_part.astype(jnp.bfloat16), "shard", scatter_dimension=0, tiled=True
        ).astype(jnp.float32),
    )
    d_q_pre = rotate(d_query, cosine_table, -sine_table, HEAD).astype(jnp.bfloat16)
    d_k_pre = rotate(d_keys, cosine_table, -sine_table, HEAD).astype(jnp.bfloat16)
    d_v_pre = d_values.astype(jnp.bfloat16)
    query_grad = jnp.dot(normed.T, d_q_pre, preferred_element_type=jnp.float32)
    key_grad = jnp.dot(normed.T, d_k_pre, preferred_element_type=jnp.float32)
    value_grad = jnp.dot(normed.T, d_v_pre, preferred_element_type=jnp.float32)
    d_normed = jnp.dot(d_q_pre, query_w.T, preferred_element_type=jnp.float32)
    d_normed = d_normed + jnp.dot(d_k_pre, key_w.T, preferred_element_type=jnp.float32)
    d_normed = d_normed + jnp.dot(d_v_pre, value_w.T, preferred_element_type=jnp.float32)
    d_input_norm, gain_attn_grad = norm_backward(d_normed, unit_attn, factor_attn, gain_attn)
    input_grad = d_mid + d_input_norm
    partial_sums = (
        gain_attn_grad,
        gain_moe_grad,
        query_grad,
        key_grad,
        value_grad,
        out_w_grad,
        router_grad,
    )
    summed = lax.psum(
        (
            partial_sums[0],
            partial_sums[1],
            partial_sums[2],
            partial_sums[3],
            partial_sums[4],
            partial_sums[5],
            partial_sums[6],
        ),
        ("expert", "shard"),
    )
    n_shard = lax.axis_size("shard")
    owned_grads = tuple(
        (
            lax.dynamic_slice_in_dim(
                member, shard_index * (member.shape[0] // n_shard), member.shape[0] // n_shard, 0
            )
            for member in summed
        )
    )
    return (
        layer_out,
        input_grad,
        owned_grads[0],
        owned_grads[1],
        owned_grads[2],
        owned_grads[3],
        owned_grads[4],
        owned_grads[5],
        owned_grads[6],
        expert_sums[0],
        expert_sums[1],
        expert_sums[2],
    )


AXES = ("expert", "shard")
N_EXPERT = 8
N_SHARD = 4
LANES = 128
MEBIBYTE = 1 << 20
BF16 = jnp.bfloat16
F32 = jnp.float32


COST_ATTENTION = 17
COST_IN = 1
COST_DOWN = 20
COST_PLACE = 3
COST_PRODUCTS = 5
OUT_BITS = (1, 2, 4)
QUERY_BITS = (1, 2, 4)
LAST_BITS = (2, 1, 4)
EVENTS = (
    "first_far", "mixed_0", "branch", "attention", "sync_1", "sync_2", "sync_3", "sync_4", "key_value", "norms",
    "out", "first_part", "gate_send", "query", "notes", "down_far", "down_cross", "layer", "out", "last_grads",
    "query", "out", "up_send", "query", "out", "last_1", "gate_total", "down_part", "down_send", "query", "out",
    "last_2", "query", "gate_place", "up_total", "out", "out_place", "query", "query_place", "down_total",
    "up_place", "last_3", "down_place",
)


def cost(microseconds):
    return pl.CostEstimate(flops=microseconds * 10**9, bytes_accessed=10**5, transcendentals=0)


def swap(values, expert_bits, shard_bits):
    pairs = [
        (e * N_SHARD + s, (e ^ expert_bits) * N_SHARD + (s ^ shard_bits))
        for e in range(N_EXPERT)
        for s in range(N_SHARD)
    ]
    return lax.ppermute(values, AXES, pairs)


def next_plane(values):
    pairs = [
        (e * N_SHARD + s, ((e + 2) % N_EXPERT) * N_SHARD + s)
        for e in range(N_EXPERT)
        for s in range(N_SHARD)
    ]
    return lax.ppermute(values, AXES, pairs)


def gather_shards(values):
    other_core = swap(values, 0, 1)
    other_y = swap(values, 0, 2)
    return [values, other_core, other_y, swap(other_y, 0, 1)]


def xor_blocks(blocks, index):
    odd = (index & 1) == 1
    high = (index & 2) == 2
    once = [jnp.where(odd, blocks[j ^ 1], blocks[j]) for j in range(4)]
    return [jnp.where(high, once[j ^ 2], once[j]) for j in range(4)]


def together(*values):
    return lax.optimization_barrier(values)


def after(value, *others):
    return lax.optimization_barrier((value,) + others)[0]


def rejoin(mine, partner, low_first):
    return jnp.where(
        low_first,
        jnp.concatenate([mine, partner], 0),
        jnp.concatenate([partner, mine], 0),
    )


def dot_nn(left, right):
    return lax.dot_general(left, right, (((1,), (0,)), ((), ())), preferred_element_type=F32)


def dot_nt(left, right):
    return lax.dot_general(left, right, (((1,), (1,)), ((), ())), preferred_element_type=F32)


def dot_tn(left, right):
    return lax.dot_general(left, right, (((0,), (0,)), ((), ())), preferred_element_type=F32)


def turn(values, cosine, sine):
    return values * cosine + pltpu.roll(values, HEAD // 2, 1) * sine


def attention_forward_body(
    where_ref, h1_ref, w0, w1, w2, w3, key_ref, value_ref, cos_ref, sin_ref, segq_ref, segk_ref,
    query_out, prob_out, attended_out, bias_ref,
):
    rows, seq_len = bias_ref.shape

    @pl.when(pl.program_id(0) == 0)
    def _():
        base = where_ref[0] * rows
        query_pos = base + lax.broadcasted_iota(jnp.int32, (rows, seq_len), 0)
        key_pos = lax.broadcasted_iota(jnp.int32, (rows, seq_len), 1)
        visible = (query_pos >= key_pos) & (segq_ref[...] == segk_ref[...])
        bias_ref[...] = jnp.where(visible, 0.0, MASKED_SCORE)

    depth = w0.shape[0]
    pre = dot_nn(h1_ref[:, :depth], w0[...])
    for j, weight in enumerate((w1, w2, w3)):
        pre = pre + dot_nn(h1_ref[:, (j + 1) * depth : (j + 2) * depth], weight[...])
    for h in range(pre.shape[1] // HEAD):
        cols = slice(h * HEAD, (h + 1) * HEAD)
        query = turn(pre[:, cols], cos_ref[...], sin_ref[...]).astype(BF16)
        query_out[:, cols] = query
        scores = dot_nt(query, key_ref[...]) * HEAD ** (-0.5) + bias_ref[...]
        exponent = jnp.exp(scores - jnp.max(scores, -1, keepdims=True))
        total = jnp.sum(exponent, -1, keepdims=True)
        probs = (exponent * (1.0 / total)).astype(BF16)
        prob_out[h] = probs
        attended_out[:, cols] = dot_nn(probs, value_ref[...]).astype(BF16)


def attention_forward(where, h1_rel, w_query, keys_values, cosine, sine, seg_query, seg_key):
    rows, width = h1_rel.shape
    seq_len = keys_values.shape[0]
    cols = width // N_SHARD
    heads = cols // HEAD

    def whole(shape):
        return pl.BlockSpec(shape, lambda j, w: (0,) * len(shape))

    weight = pl.BlockSpec((cols, cols), lambda j, w: (0, w[0] ^ j))
    part = pl.BlockSpec((rows, cols), lambda j, w: (0, j))
    return pl.pallas_call(
        attention_forward_body,
        grid_spec=pltpu.PrefetchScalarGridSpec(
            num_scalar_prefetch=1,
            grid=(N_SHARD,),
            in_specs=[
                whole((rows, width)), weight, weight, weight, weight,
                pl.BlockSpec((seq_len, HEAD), lambda j, w: (0, (w[0] ^ j) // 2)),
                pl.BlockSpec((seq_len, HEAD), lambda j, w: (0, KVH + (w[0] ^ j) // 2)),
                whole((rows, HEAD)), whole((rows, HEAD)), whole((rows, 1)), whole((1, seq_len)),
            ],
            out_specs=[part, pl.BlockSpec((heads, rows, seq_len), lambda j, w: (j, 0, 0)), part],
            scratch_shapes=[pltpu.VMEM((rows, seq_len), F32)],
        ),
        out_shape=[
            jax.ShapeDtypeStruct((rows, width), BF16),
            jax.ShapeDtypeStruct((HQ, rows, seq_len), BF16),
            jax.ShapeDtypeStruct((rows, width), BF16),
        ],
        compiler_params=pltpu.CompilerParams(vmem_limit_bytes=28 * MEBIBYTE),
        cost_estimate=cost(15),
        name="attention_forward",
    )(where, h1_rel, *w_query, keys_values, keys_values, cosine, sine, seg_query, seg_key)


def attention_backward_body(
    where_ref, branch_ref, out0, out1, out2, out3, attended_ref, query_ref, prob_ref, key_ref, value_ref,
    w0, w1, w2, w3, cos_ref, sin_ref,
    dq_out, dk_out, dv_out, dh_out, dh_acc, dk_acc, dv_acc, da_ref,
):
    step = pl.program_id(0)
    depth = w0.shape[0]
    rows = branch_ref.shape[0]

    for j, weight in enumerate((out0, out1, out2, out3)):

        @pl.when(step == j)
        def _(weight=weight):
            da_ref[...] = dot_nt(branch_ref[...], weight[...]).astype(BF16)

    @pl.when(step % 2 == 0)
    def _():
        dk_acc[...] = jnp.zeros_like(dk_acc)
        dv_acc[...] = jnp.zeros_like(dv_acc)

    @pl.when(step == 0)
    def _():
        dh_acc[...] = jnp.zeros_like(dh_acc)

    d_pre = []
    for h in range(depth // HEAD):
        cols = slice(h * HEAD, (h + 1) * HEAD)
        d_att = da_ref[:, cols]
        probs = prob_ref[h]
        delta = jnp.sum(d_att.astype(F32) * attended_ref[:, cols].astype(F32), -1, keepdims=True)
        d_probs = dot_nt(d_att, value_ref[...])
        d_scores = (probs.astype(F32) * ((d_probs - delta) * HEAD ** (-0.5))).astype(BF16)
        d_query = dot_nn(d_scores, key_ref[...])
        d_pre.append(turn(d_query, cos_ref[...], -sin_ref[...]).astype(BF16))
        dk_acc[...] += dot_tn(query_ref[:, cols], d_scores)
        dv_acc[...] += dot_tn(d_att, probs)
    d_pre = jnp.concatenate(d_pre, 1)
    dq_out[...] = d_pre
    for j, weight in enumerate((w0, w1, w2, w3)):
        dh_acc[:, j * depth : (j + 1) * depth] += dot_nt(d_pre, weight[...])

    @pl.when(step % 2 == 1)
    def _():
        dk_out[...] = dk_acc[...].T.astype(BF16)
        dv_out[...] = dv_acc[...].T.astype(BF16)

    @pl.when(step == N_SHARD - 1)
    def _():
        dh_out[...] = dh_acc[...]


def attention_backward(where, branch, w_out, attended, queries, probs, keys_values, w_query, cosine, sine):
    rows, width = branch.shape
    seq_len = keys_values.shape[0]
    cols = width // N_SHARD
    heads = cols // HEAD

    def whole(shape):
        return pl.BlockSpec(shape, lambda j, w: (0,) * len(shape))

    weight = pl.BlockSpec((cols, cols), lambda j, w: (0, w[0] ^ j))
    part = pl.BlockSpec((rows, cols), lambda j, w: (0, j))
    head_part = pl.BlockSpec((seq_len, HEAD), lambda j, w: (0, (w[0] ^ j) // 2))
    return pl.pallas_call(
        attention_backward_body,
        grid_spec=pltpu.PrefetchScalarGridSpec(
            num_scalar_prefetch=1,
            grid=(N_SHARD,),
            in_specs=[whole((rows, width))] + [whole((cols, width))] * 4 + [
                part, part, pl.BlockSpec((heads, rows, seq_len), lambda j, w: (j, 0, 0)),
                head_part,
                pl.BlockSpec((seq_len, HEAD), lambda j, w: (0, KVH + (w[0] ^ j) // 2)),
                weight, weight, weight, weight, whole((rows, HEAD)), whole((rows, HEAD)),
            ],
            out_specs=[
                pl.BlockSpec((rows, cols), lambda j, w: (0, w[0] ^ j)),
                head_part, head_part, whole((rows, width)),
            ],
            scratch_shapes=[
                pltpu.VMEM((rows, width), F32),
                pltpu.VMEM((HEAD, seq_len), F32),
                pltpu.VMEM((HEAD, seq_len), F32),
                pltpu.VMEM((rows, cols), BF16),
            ],
        ),
        out_shape=[
            jax.ShapeDtypeStruct((rows, width), BF16),
            jax.ShapeDtypeStruct((seq_len, KVH * HEAD), BF16),
            jax.ShapeDtypeStruct((seq_len, KVH * HEAD), BF16),
            jax.ShapeDtypeStruct((rows, width), F32),
        ],
        compiler_params=pltpu.CompilerParams(vmem_limit_bytes=30 * MEBIBYTE),
        cost_estimate=cost(COST_ATTENTION),
        name="attention_backward",
    )(where, branch, *w_out, attended, queries, probs, keys_values, keys_values, *w_query, cosine, sine)


def expert_body(
    where_ref, h2_ref, dy_ref, router_ref, *refs,
):
    own, far = refs[:6], refs[6:12]
    message_out, mixed_out, da_out, db_out, act_out, gates_ref, dh_acc, y_acc, gg_acc = refs[12:]
    e = pl.program_id(0)
    f = pl.program_id(1)
    rows, width = h2_ref.shape
    half = width // 2
    lane = lax.broadcasted_iota(jnp.int32, (rows, LANES), 1)
    places = [pl.ds(pl.multiple_of((where_ref[1] ^ i) * half, LANES), half) for i in range(2)]

    @pl.when((e == 0) & (f == 0))
    def _():
        named = dy_ref[:, width:].astype(F32) > 0.5
        logits = dot_nt(h2_ref[...], router_ref[...])
        logits = jnp.concatenate([logits, jnp.zeros((rows, LANES - logits.shape[1]), F32)], 1)
        logits = jnp.where(named, logits, MASKED_SCORE)
        top = jnp.max(logits, -1, keepdims=True)
        weights = jnp.where(named, jnp.exp(logits - top), 0.0)
        gates_ref[...] = weights / jnp.sum(weights, -1, keepdims=True)
        dh_acc[...] = jnp.zeros_like(dh_acc)
        y_acc[...] = jnp.zeros_like(y_acc)
        gg_acc[...] = jnp.zeros_like(gg_acc)

    here = lane == (where_ref[0] ^ e)

    def work(members):
        gates, ups, downs = [[members[2 * k + i] for i in range(2)] for k in range(3)]
        gate = jnp.sum(jnp.where(here, gates_ref[...], 0.0), -1, keepdims=True)
        h2 = [h2_ref[:, place] for place in places]
        dy = [dy_ref[:, place] for place in places]
        load = lambda ref: ref[...].reshape(ref.shape[-2:])
        a = dot_nn(h2[0], load(gates[0])) + dot_nn(h2[1], load(gates[1]))
        b = dot_nn(h2[0], load(ups[0])) + dot_nn(h2[1], load(ups[1]))
        d_plain = dot_nt(dy[0], load(downs[0])) + dot_nt(dy[1], load(downs[1]))
        sigmoid = 1.0 / (1.0 + jnp.exp(-a))
        silu = a * sigmoid
        act = silu * b
        gate_grad = jnp.sum(act * d_plain, -1, keepdims=True)
        gg_acc[...] += jnp.where(here, gate_grad, 0.0)
        d_act = d_plain * gate
        d_a = (d_act * b * (sigmoid + silu * (1.0 - sigmoid))).astype(BF16)
        d_b = (d_act * silu).astype(BF16)
        scaled = (act * gate).astype(BF16)
        da_out[...] = d_a
        db_out[...] = d_b
        act_out[...] = scaled
        for i in range(2):
            dh_acc[i] += dot_nt(d_a, load(gates[i])) + dot_nt(d_b, load(ups[i]))
            y_acc[i] += dot_nn(scaled, load(downs[i]))

    @pl.when(e == 0)
    def _():
        work(own)

    @pl.when(e == 1)
    def _():
        work(far)

    @pl.when((e == pl.num_programs(0) - 1) & (f == pl.num_programs(1) - 1))
    def _():
        for i in range(2):
            message_out[:, places[i]] = dh_acc[i].astype(BF16)
            mixed_out[:, places[i]] = y_acc[i].astype(BF16)
        high = gg_acc[...].astype(BF16).astype(F32)
        low = pltpu.roll(gg_acc[...] - high, N_EXPERT, 1)
        message_out[:, width:] = (high + low).astype(BF16)


def expert_block(where, h2, dy_routes, router, own, far):
    rows, width = h2.shape
    hidden = own[0].shape[1]
    half = width // 2
    chunk = 256
    chunks = hidden // chunk

    def whole(shape):
        return pl.BlockSpec(shape, lambda e, f, w: (0,) * len(shape))

    own_step = lambda e, f: jnp.where(e == 0, f, chunks - 1)
    far_step = lambda e, f: jnp.where(e == 0, 0, f)
    own_in = [pl.BlockSpec((half, chunk), lambda e, f, w, i=i: (w[1] ^ i, own_step(e, f))) for i in range(2)]
    own_down = [pl.BlockSpec((chunk, half), lambda e, f, w, i=i: (own_step(e, f), w[1] ^ i)) for i in range(2)]
    far_in = [pl.BlockSpec((1, half, chunk), lambda e, f, w, k=k: (k, 0, far_step(e, f))) for k in range(2)]
    far_down = pl.BlockSpec((1, chunk, half), lambda e, f, w: (2, far_step(e, f), 0))
    part = pl.BlockSpec((rows, chunk), lambda e, f, w: (0, e * chunks + f))
    return pl.pallas_call(
        expert_body,
        grid_spec=pltpu.PrefetchScalarGridSpec(
            num_scalar_prefetch=1,
            grid=(2, chunks),
            in_specs=[whole((rows, width)), whole(dy_routes.shape), whole(router.shape)]
            + own_in + own_in + own_down
            + [far_in[0], far_in[0], far_in[1], far_in[1], far_down, far_down],
            out_specs=[whole((rows, width + LANES)), whole((rows, width)), part, part, part],
            scratch_shapes=[
                pltpu.VMEM((rows, LANES), F32),
                pltpu.VMEM((2, rows, half), F32),
                pltpu.VMEM((2, rows, half), F32),
                pltpu.VMEM((rows, LANES), F32),
            ],
        ),
        out_shape=[
            jax.ShapeDtypeStruct((rows, width + LANES), BF16),
            jax.ShapeDtypeStruct((rows, width), BF16),
            jax.ShapeDtypeStruct((rows, 2 * hidden), BF16),
            jax.ShapeDtypeStruct((rows, 2 * hidden), BF16),
            jax.ShapeDtypeStruct((rows, 2 * hidden), BF16),
        ],
        compiler_params=pltpu.CompilerParams(vmem_limit_bytes=22 * MEBIBYTE),
        cost_estimate=cost(20),
        name="expert_block",
    )(
        where, h2, dy_routes, router, own[0], own[0], own[1], own[1], own[2], own[2],
        far[0], far[1], far[0], far[1], far[0], far[1],
    )


def summed_products_body(where_ref, *refs, parts, sets):
    lefts = refs[:parts]
    rights = refs[parts : parts * (1 + sets)]
    outs = refs[parts * (1 + sets) :]
    for k in range(sets):
        total = dot_tn(lefts[0][...], rights[k * parts][...])
        for j in range(1, parts):
            total = total + dot_tn(lefts[j][...], rights[k * parts + j][...])
        out = outs[k]
        if len(out.shape) == 3:
            pieces = out.shape[0]
            deep = out.shape[1]
            for piece in range(pieces):
                out[where_ref[0] ^ piece] = total[piece * deep : (piece + 1) * deep].astype(out.dtype)
        else:
            out[...] = total.astype(out.dtype)


def summed_products(where, lefts, right_sets, grid, left_spec, right_spec, out_spec, out_shape, name):
    parts = len(lefts)
    sets = len(right_sets)
    return pl.pallas_call(
        functools.partial(summed_products_body, parts=parts, sets=sets),
        grid_spec=pltpu.PrefetchScalarGridSpec(
            num_scalar_prefetch=1,
            grid=grid,
            in_specs=[left_spec] * parts + [right_spec] * (parts * sets),
            out_specs=[out_spec] * sets,
        ),
        out_shape=[jax.ShapeDtypeStruct(out_shape, BF16)] * sets,
        compiler_params=pltpu.CompilerParams(vmem_limit_bytes=24 * MEBIBYTE),
        cost_estimate=cost(COST_PRODUCTS),
        name=name,
    )(where, *lefts, *[member for members in right_sets for member in members])


def in_grads_body(where_ref, *refs):
    h2_refs, da_refs, db_refs = refs[:4], refs[4:8], refs[8:12]
    send_ref, keep_ref, turned_ref = refs[12:]
    rows = h2_refs[0].shape[0]
    half = turned_ref.shape[0] // 2

    @pl.when(pl.program_id(0) == 0)
    def _():
        for j in range(4):
            turned_ref[:, j * rows : (j + 1) * rows] = h2_refs[j][...].T

    for k, member in enumerate((da_refs, db_refs)):
        for out, place in ((send_ref, 1 - where_ref[0]), (keep_ref, where_ref[0])):
            here = pl.ds(pl.multiple_of(place * half, LANES), half)
            total = dot_nn(turned_ref[here, :rows], member[0][...])
            for j in range(1, 4):
                total = total + dot_nn(turned_ref[here, j * rows : (j + 1) * rows], member[j][...])
            out[k] = total.astype(BF16)


def expert_in_grads(where, h2, d_a, d_b):
    rows, width = h2[0].shape
    columns = d_a[0].shape[1]
    chunk = 256
    half = width // 2
    part = pl.BlockSpec((rows, chunk), lambda i, w: (0, i))
    out = pl.BlockSpec((2, half, chunk), lambda i, w: (0, 0, i))
    return pl.pallas_call(
        in_grads_body,
        grid_spec=pltpu.PrefetchScalarGridSpec(
            num_scalar_prefetch=1,
            grid=(columns // chunk,),
            in_specs=[pl.BlockSpec((rows, width), lambda i, w: (0, 0))] * 4 + [part] * 8,
            out_specs=[out] * 2,
            scratch_shapes=[pltpu.VMEM((width, 4 * rows), BF16)],
        ),
        out_shape=[jax.ShapeDtypeStruct((2, half, columns), BF16)] * 2,
        compiler_params=pltpu.CompilerParams(vmem_limit_bytes=24 * MEBIBYTE),
        cost_estimate=cost(COST_IN),
        name="expert_in_grads",
    )(where, *h2, *d_a, *d_b)


def down_grads_body(where_ref, *refs):
    act_refs, send_refs, keep_refs = refs[:4], refs[4:8], refs[8:12]
    turned = [act[...].T for act in act_refs]
    for rights, out in ((send_refs, refs[12]), (keep_refs, refs[13])):
        total = dot_nn(turned[0], rights[0][...])
        for j in range(1, 4):
            total = total + dot_nn(turned[j], rights[j][...])
        out[0] = total.astype(BF16)


def expert_down_grads(where, acts, dy_routes):
    rows, columns = acts[0].shape
    width = dy_routes[0].shape[1] - LANES
    half = width // 2
    hidden = columns // 2
    out = pl.BlockSpec((1, hidden, half), lambda e, w: (e, 0, 0))
    return pl.pallas_call(
        down_grads_body,
        grid_spec=pltpu.PrefetchScalarGridSpec(
            num_scalar_prefetch=1,
            grid=(2,),
            in_specs=[pl.BlockSpec((rows, hidden), lambda e, w: (0, e))] * 4
            + [pl.BlockSpec((rows, half), lambda e, w: (0, 1 - w[0]))] * 4
            + [pl.BlockSpec((rows, half), lambda e, w: (0, w[0]))] * 4,
            out_specs=[out, out],
        ),
        out_shape=[jax.ShapeDtypeStruct((2, hidden, half), BF16)] * 2,
        compiler_params=pltpu.CompilerParams(vmem_limit_bytes=22 * MEBIBYTE),
        cost_estimate=cost(COST_DOWN),
        name="expert_down_grads",
    )(where, *acts, *dy_routes, *dy_routes)


class PlaneSum:
    def __init__(self, pieces, order):
        self.shape = pieces.shape[1:]
        self.order = order
        self.axes = [4, 2, 1]
        self.kept = pieces.reshape((2, 2, 2) + self.shape)
        self.step = 0
        self.send()

    def send(self):
        if self.step < 3:
            at = self.axes.index(self.order[self.step])
            self.mine = lax.index_in_dim(self.kept, 0, at, keepdims=False)
            other = lax.index_in_dim(self.kept, 1, at, keepdims=False)
            self.received = swap(other, self.order[self.step], 0)
        else:
            self.received = swap(self.kept, self.order[5 - self.step], 0)

    def receive(self, token):
        received = after(self.received, token)
        if self.step < 3:
            self.kept = (self.mine.astype(F32) + received.astype(F32)).astype(BF16)
            self.axes.remove(self.order[self.step])
        else:
            bit = self.order[5 - self.step]
            if self.step == 5:
                self.done = (self.kept.reshape((4,) + self.shape), received.reshape((4,) + self.shape))
                return received
            at = sum(1 for b in self.axes if b > bit)
            self.kept = jnp.stack([self.kept, received], at)
            self.axes = sorted(self.axes + [bit], reverse=True)
        self.step += 1
        self.send()
        return self.kept


def reorder_body(where_ref, even_ref, odd_ref, out_ref, *, first):
    for b in range(N_EXPERT):
        place = where_ref[0] ^ b
        low = place % first
        index = (place // (2 * first)) * first + low
        odd = (place // first) % 2

        @pl.when(odd == 0)
        def _(b=b, index=index):
            out_ref[b] = even_ref[index].astype(F32)

        @pl.when(odd == 1)
        def _(b=b, index=index):
            out_ref[b] = odd_ref[index].astype(F32)


def reorder(where, even, odd, columns, first):
    deep, width = even.shape[1:]
    results = []
    begin = 0
    for count in columns:
        wide = min(count, 512)
        start = begin // wide
        spec = pl.BlockSpec((N_EXPERT // 2, deep, wide), lambda i, w, start=start: (0, 0, start + i))
        results.append(
            pl.pallas_call(
                functools.partial(reorder_body, first=first),
                grid_spec=pltpu.PrefetchScalarGridSpec(
                    num_scalar_prefetch=1,
                    grid=(count // wide,),
                    in_specs=[spec, spec],
                    out_specs=pl.BlockSpec((N_EXPERT, deep, wide), lambda i, w: (0, 0, i)),
                ),
                out_shape=jax.ShapeDtypeStruct((N_EXPERT, deep, count), F32),
                cost_estimate=cost(COST_PLACE),
                name="reorder",
            )(where, even, odd).reshape(N_EXPERT * deep, count)
        )
        begin += count
    return results


def key_value_grad_body(*refs):
    lefts, rights, out_ref = refs[:4], refs[4:8], refs[8]
    rows, block = lefts[0].shape
    total = dot_tn(lefts[0][...], rights[0][:rows])
    small = rights[0][rows:, :block].astype(F32)
    for j in range(1, 4):
        total = total + dot_tn(lefts[j][...], rights[j][:rows])
        small = small + rights[j][rows:, :block].astype(F32)
    few = small.shape[0] // 2
    out_ref[:block] = total.astype(BF16)
    out_ref[block:, :block] = (small[:few] + small[few:]).astype(BF16)
    out_ref[block:, block:] = jnp.zeros_like(out_ref[block:, block:])


def key_value_grad(lefts, rights, block):
    rows = lefts[0].shape[0]
    columns = rights[0].shape[1]
    few = (rights[0].shape[0] - rows) // 2
    whole = lambda shape: pl.BlockSpec(shape, lambda i: (0, 0))
    return pl.pallas_call(
        key_value_grad_body,
        grid=(1,),
        in_specs=[whole((rows, block))] * 4 + [whole(rights[0].shape)] * 4,
        out_specs=whole((block + few, columns)),
        out_shape=jax.ShapeDtypeStruct((block + few, columns), BF16),
        cost_estimate=cost(COST_PRODUCTS),
        name="key_value_grad",
    )(*lefts, *rights)


def place_body(where_ref, mine_ref, partner_ref, out_ref):
    @pl.when(pl.program_id(0) == 0)
    def _():
        out_ref[...] = mine_ref[0].astype(out_ref.dtype)

    @pl.when(pl.program_id(0) == 1)
    def _():
        out_ref[...] = partner_ref[0].astype(out_ref.dtype)


def place_halves(where, mine, partner, member, by_rows):
    tall, wide = mine.shape[1:]
    cuts = 2
    deep = tall // cuts

    def mine_map(h, i, w):
        return (member, jnp.where(h == 0, i, cuts - 1), 0)

    def partner_map(h, i, w):
        return (member, jnp.where(h == 0, 0, i), 0)

    def out_map(h, i, w):
        return ((w[0] ^ h) * cuts + i, 0) if by_rows else (i, w[0] ^ h)

    return pl.pallas_call(
        place_body,
        grid_spec=pltpu.PrefetchScalarGridSpec(
            num_scalar_prefetch=1,
            grid=(2, cuts),
            in_specs=[pl.BlockSpec((1, deep, wide), mine_map), pl.BlockSpec((1, deep, wide), partner_map)],
            out_specs=pl.BlockSpec((deep, wide), out_map),
        ),
        out_shape=jax.ShapeDtypeStruct((2 * tall, wide) if by_rows else (tall, 2 * wide), F32),
        cost_estimate=cost(COST_PLACE),
        name="place_halves",
    )(where, mine, partner)


def far_halves_body(where_ref, *refs):
    out_ref = refs[-1]
    for k, ref in enumerate(refs[:-1]):

        @pl.when(pl.program_id(0) == k)
        def _(ref=ref):
            out_ref[0] = ref[...]


def far_halves(where, own):
    hidden = own[0].shape[1]
    half = own[0].shape[0] // 2
    cuts = 1
    tall = half // cuts

    def in_map(k):
        step = lambda i, r: jnp.where(i < k, 0, jnp.where(i == k, r, cuts - 1))
        if k == 2:
            return lambda i, r, w: (step(i, r), w[0])
        return lambda i, r, w: (w[0] * cuts + step(i, r), 0)

    return pl.pallas_call(
        far_halves_body,
        grid_spec=pltpu.PrefetchScalarGridSpec(
            num_scalar_prefetch=1,
            grid=(3, cuts),
            in_specs=[pl.BlockSpec((tall, hidden), in_map(k)) for k in range(3)],
            out_specs=pl.BlockSpec((1, tall, hidden), lambda i, r, w: (i, r, 0)),
        ),
        out_shape=jax.ShapeDtypeStruct((3, half, hidden), BF16),
        cost_estimate=cost(3),
        name="far_halves",
    )(where, *own)


def pack_body(key_ref, value_ref, small_ref, out_ref):
    rows, low = key_ref.shape
    out_ref[:rows, :low] = key_ref[...]
    out_ref[:rows, low:] = value_ref[...]
    out_ref[rows:, : small_ref.shape[1]] = small_ref[...]
    out_ref[rows:, small_ref.shape[1] :] = jnp.zeros_like(out_ref[rows:, small_ref.shape[1] :])


def pack(w_key, w_value, small):
    rows, low = w_key.shape
    return pl.pallas_call(
        pack_body,
        out_shape=jax.ShapeDtypeStruct((rows + small.shape[0], 2 * low), BF16),
        cost_estimate=cost(2),
        name="pack",
    )(w_key, w_value, small)


def plus(part, received):
    return (part.astype(F32) + received.astype(F32)).astype(BF16)


def on_device_rings(
    hidden_in, segment_ids, routes, attn_gain, moe_gain, w_query, w_key, w_value, w_out, w_router,
    expert_gate, expert_up, expert_down, out_grad,
):
    rows, width = hidden_in.shape
    experts = w_router.shape[1]
    shard = lax.axis_index("shard")
    expert = lax.axis_index("expert")
    core = shard % 2
    where_shard = shard.astype(jnp.int32)[None]
    where_expert = expert.astype(jnp.int32)[None]
    where_core = core.astype(jnp.int32)[None]
    where_far_core = 1 - where_core
    block = width // N_SHARD
    low = KVH * HEAD

    own = (expert_gate[0], expert_up[0], expert_down[0])
    far_send = far_halves(where_core, own)
    far_part = swap(far_send, 1, 0)
    small = jnp.concatenate(
        [w_router.T, attn_gain[None], moe_gain[None], jnp.zeros((6, block), BF16)], 0
    )
    packed_own = pack(after(w_key, far_send), w_value, small)
    packed_y = swap(packed_own, 0, 2)
    mask = (routes[:, :, None] == jnp.arange(LANES, dtype=jnp.int32)[None, None, :]).any(1)
    dy_routes = [jnp.concatenate([out_grad, mask.astype(BF16)], 1)]
    for _ in range(3):
        dy_routes.append(next_plane(dy_routes[-1]))
    query_w_core = swap(w_query, 0, 1)
    out_w_core = swap(w_out, 0, 1)
    query_w_y = swap(after(w_query, packed_y), 0, 2)
    packed_pair = swap(jnp.concatenate([packed_own, packed_y], 0), 0, 1)
    tall = packed_own.shape[0]
    packed = [packed_own, packed_pair[:tall], packed_y, packed_pair[tall:]]

    inputs = hidden_in.astype(F32)
    factor_attn = lax.rsqrt(jnp.mean(inputs * inputs, -1, keepdims=True) + EPSILON)
    unit_rel = jnp.concatenate(
        xor_blocks([inputs[:, j * block : (j + 1) * block] for j in range(4)], shard), 1
    ) * factor_attn
    gain_rel = jnp.concatenate([member[block + experts : block + experts + 1, :block] for member in packed], 1)
    gain_rel = gain_rel.astype(F32)
    h1_rel = after((unit_rel * gain_rel).astype(BF16), query_w_core, out_w_core)
    key_value_w = [member[:block] for member in packed]
    pre = sum(dot_nn(h1_rel[:, j * block : (j + 1) * block], key_value_w[j]) for j in range(4))
    positions = shard * rows + jnp.arange(rows, dtype=jnp.int32)
    cosine, sine = rope_tables(positions, HEAD)
    key_local = rotate(pre[:, :low], cosine, sine, HEAD)
    key_value = jnp.concatenate([key_local, pre[:, low:]], 1).astype(BF16)
    key_value = after(key_value, dy_routes[1])
    key_value_y = swap(key_value, 0, 2)
    query_w = [w_query, query_w_core, query_w_y, swap(query_w_y, 0, 1)]
    key_value_pair = swap(jnp.concatenate([key_value, key_value_y], 0), 0, 1)
    keys_values = jnp.concatenate(
        xor_blocks([key_value, key_value_pair[:rows], key_value_y, key_value_pair[rows:]], shard), 0
    )
    out_w_y = swap(after(w_out, query_w_y, key_value), 0, 2)
    cosine_row = jnp.concatenate([cosine, cosine], 1)
    sine_row = jnp.concatenate([-sine, sine], 1)
    seg_query = lax.dynamic_slice_in_dim(segment_ids, shard * rows, rows)[:, None]
    queries, probs, attended = attention_forward(
        where_shard, after(h1_rel, dy_routes[2]), query_w, keys_values, cosine_row, sine_row, seg_query, segment_ids[None, :]
    )
    attended_late = after(attended, dy_routes[3])
    out_w_y = after(out_w_y, attended)
    out_w = [w_out, out_w_core, out_w_y, swap(out_w_y, 0, 1)]
    mid_state = inputs + sum(
        dot_nn(attended_late[:, j * block : (j + 1) * block], out_w[j]) for j in range(4)
    )
    factor_moe = lax.rsqrt(jnp.mean(mid_state * mid_state, -1, keepdims=True) + EPSILON)
    unit_moe = mid_state * factor_moe
    small_true = jnp.concatenate(xor_blocks([member[block:, :block] for member in packed], shard), 1)
    gain_moe = small_true[experts + 1 : experts + 2].astype(F32)
    router = small_true[:experts].astype(F32)
    h2 = [(unit_moe * gain_moe).astype(BF16)]

    far_part = after(far_part, attended)
    far_other = swap(far_part, 0, 1)
    hidden = own[0].shape[1]
    deep = width // 2
    far = (far_part, far_other)
    where_pair = jnp.stack([expert, core]).astype(jnp.int32)

    mixer_rows = [
        jnp.concatenate([h1_rel[:, j * block : (j + 1) * block], attended[:, j * block : (j + 1) * block]], 1)
        for j in range(4)
    ]
    mixer_rows = [mixer_rows[0]] + [swap(mixer_rows[j], 0, j) for j in (1, 2, 3)]
    add = lambda a, b: (a.astype(F32) + b.astype(F32)).astype(BF16)
    block_of = lambda j, *ready: expert_block(
        where_pair, after(h2[j], *ready), dy_routes[j], small_true, own, far
    )
    h2.append(next_plane(h2[0]))
    done = [block_of(0)]
    h2.append(next_plane(after(h2[1], done[0][0])))
    done.append(block_of(1, done[0][0], *mixer_rows))
    h2[2] = after(h2[2], done[1][0])
    h2.append(next_plane(h2[2]))
    message = next_plane(after(done[1][0], h2[2]))
    done.append(block_of(2, done[1][0]))
    done.append(block_of(3, done[2][0]))
    second = add(done[2][0], after(message, done[3][0]))
    message = next_plane(second)

    acts = [done[j][4] for j in range(4)]
    in_send, in_keep = expert_in_grads(
        after(where_core, second), h2, [done[j][2] for j in range(4)], [done[j][3] for j in range(4)]
    )
    third = add(done[3][0], after(message, in_send))
    message = next_plane(third)
    v = types.SimpleNamespace(in_swap=swap(after(in_send, third), 0, 1))

    def mixer_grads(half, rights, name):
        n = rights[0].shape[1]
        (pieces,) = summed_products(
            where_expert, mixer_rows, [rights], (n // 512,),
            pl.BlockSpec((rows, block), lambda i, w: (0, half)),
            pl.BlockSpec((rows, 512), lambda i, w: (0, i)),
            pl.BlockSpec((N_EXPERT, block // N_EXPERT, 512), lambda i, w: (0, 0, i)),
            (N_EXPERT, block // N_EXPERT, n), name,
        )
        return pieces


    def first_far(token):
        v.in_swap, token = together(v.in_swap, token)
        far = jnp.stack([plus(in_keep[k, :, hidden:], v.in_swap[k, :, hidden:]) for k in range(2)])
        v.first_received = swap(far, 1, 0)
        return far

    def down_far(token):
        v.down_swap = after(v.down_swap, token)
        v.down_far = plus(v.down_keep[1], v.down_swap[1])
        return v.down_far

    def down_cross(token):
        v.down_received = swap(after(v.down_far, token), 1, 0)
        return token

    def branch(token):
        total = done[0][0].astype(F32) + after(message, token).astype(F32)
        named = mask[:, :experts]
        logits = jnp.where(named, dot_nt(h2[0], small_true[:experts]), MASKED_SCORE)
        weights = jnp.where(named, jnp.exp(logits - jnp.max(logits, -1, keepdims=True)), 0.0)
        gate = weights / jnp.sum(weights, -1, keepdims=True)
        gate_grad = total[:, width : width + experts] + total[:, width + experts : width + 2 * experts]
        d_logits = gate * (gate_grad - jnp.sum(gate * gate_grad, -1, keepdims=True))
        d_h2 = total[:, :width] + jnp.dot(d_logits, router, precision=HIGHEST)
        v.router_grad = jnp.dot(d_logits.T, h2[0].astype(F32), precision=HIGHEST)
        d_mid_norm, v.gain_moe_grad = norm_backward(d_h2, unit_moe, factor_moe, gain_moe)
        v.d_mid = out_grad.astype(F32) + d_mid_norm
        v.d_branch = v.d_mid.astype(BF16)
        v.branch_core = swap(v.d_branch, 0, 1)
        v.branch_y = swap(v.d_branch, 0, 2)
        return v.d_branch

    def mixed_0(token):
        v.mixed = next_plane(after(done[1][1], token))
        return token

    def attention(token):
        v.d_q_pre, v.d_key_part, v.d_value_part, v.d_normed = attention_backward(
            where_shard, after(v.d_branch, token), out_w, attended, queries, probs, keys_values, query_w,
            cosine_row, sine_row,
        )
        return v.d_q_pre

    def sync_1(token):
        v.d_q_pre, v.d_key_part, v.d_value_part, v.branch_y, v.branch_core, v.mixed = together(
            v.d_q_pre, v.d_key_part, v.d_value_part, v.branch_y, v.branch_core, v.mixed
        )
        v.d_q_y = swap(v.d_q_pre, 0, 2)
        v.d_q_core = swap(v.d_q_pre, 0, 1)
        v.branch_far = swap(v.branch_y, 0, 1)
        d_parts = jnp.concatenate([v.d_key_part, v.d_value_part], 1).reshape(N_SHARD, rows, 2 * low)
        v.d_rel = xor_blocks([d_parts[j] for j in range(4)], shard)
        v.from_core = swap(jnp.stack([v.d_rel[1], v.d_rel[3]]), 0, 1)
        v.mixed = add(done[2][1], v.mixed)
        return v.d_q_pre

    def sync_2(token):
        v.d_q_core, v.branch_far, v.from_core, v.mixed = together(
            v.d_q_core, v.branch_far, v.from_core, v.mixed
        )
        v.mixed = next_plane(v.mixed)
        d_far = add(v.d_rel[2], v.from_core[1])
        v.d_far_y = swap(d_far, 0, 2)
        rights = [v.d_branch, v.branch_core, v.branch_y, after(v.branch_far, d_far)]
        v.out_pieces = mixer_grads(1, rights, "w_out_grad")
        down_send, v.down_keep = expert_down_grads(after(where_core, v.out_pieces), acts, dy_routes)
        v.down_swap = swap(down_send, 0, 1)
        return down_send

    def sync_3(token):
        v.d_q_y, v.out_pieces, v.mixed, v.down_keep, token = together(
            v.d_q_y, v.out_pieces, v.mixed, v.down_keep, token
        )
        v.out_sum = PlaneSum(v.out_pieces, OUT_BITS)
        v.mixed = next_plane(add(done[3][1], v.mixed))
        rights = [v.d_q_pre, v.d_q_core, v.d_q_y, swap(v.d_q_y, 0, 1)]
        v.query_pieces = mixer_grads(0, rights, "w_query_grad")
        return v.query_pieces

    def sync_4(token):
        v.query_pieces, v.d_far_y, token = together(v.query_pieces, v.d_far_y, token)
        v.query_sum = PlaneSum(v.query_pieces, QUERY_BITS)
        return v.query_pieces

    def first_part(token):
        received = after(v.first_received, token)
        parts = [
            in_keep[k, :, :hidden].astype(F32) + v.in_swap[k, :, :hidden].astype(F32) + received[k].astype(F32)
            for k in range(2)
        ]
        v.gate_part, v.up_part = together(*[part.astype(BF16) for part in parts])
        return v.gate_part

    def down_send(token):
        v.down_y = swap(after(v.down_part, token), 0, 2)
        return token

    def up_send(token):
        v.up_y = swap(after(v.up_part, token), 0, 2)
        return token

    def gate_send(token):
        v.gate_y = swap(after(v.gate_part, token), 0, 2)
        return token

    def down_total(token):
        v.down_total = plus(v.down_part, after(v.down_y, token))
        v.down_core = swap(v.down_total, 0, 1)
        return v.down_total

    def gate_total(token):
        v.gate_total = plus(v.gate_part, after(v.gate_y, token))
        v.gate_core = swap(v.gate_total, 0, 1)
        return v.gate_total

    def layer(token):
        mixed = after(v.mixed, token).astype(F32)
        v.layer_out = (mid_state + done[0][1].astype(F32) + mixed).astype(BF16)
        return v.layer_out

    def down_part(token):
        own_part = v.down_keep[0].astype(F32) + v.down_swap[0].astype(F32)
        v.down_part = plus(own_part, after(v.down_received, token))
        return v.down_part

    def up_total(token):
        v.up_total = plus(v.up_part, after(v.up_y, token))
        v.up_core = swap(v.up_total, 0, 1)
        return v.up_total

    def down_place(token):
        v.down_sum = place_halves(where_core, v.down_total[None], after(v.down_core, token)[None], 0, False)[None]
        return v.down_sum

    def gate_place(token):
        v.gate_sum = place_halves(where_core, v.gate_total[None], after(v.gate_core, token)[None], 0, True)[None]
        return v.gate_sum

    def up_place(token):
        v.up_sum = place_halves(where_core, v.up_total[None], after(v.up_core, token)[None], 0, True)[None]
        return v.up_sum

    def key_value(token):
        d_key_value = v.d_rel[0].astype(F32) + v.from_core[0].astype(F32) + after(v.d_far_y, token).astype(F32)
        d_k_pre = rotate(d_key_value[:, :low], cosine, -sine, HEAD)
        v.d_kv_pre = jnp.concatenate([d_k_pre, d_key_value[:, low:]], 1).astype(BF16)
        return v.d_kv_pre

    def norms(token):
        d_kv_pre = after(v.d_kv_pre, token)
        d_normed = v.d_normed + jnp.concatenate([dot_nt(d_kv_pre, member) for member in key_value_w], 1)
        d_input_norm, gain_attn_grad = norm_backward(d_normed, unit_rel, factor_attn, gain_rel)
        d_input_norm = jnp.concatenate(
            xor_blocks([d_input_norm[:, j * block : (j + 1) * block] for j in range(4)], shard), 1
        )
        v.input_grad = v.d_mid + d_input_norm
        rest = jnp.concatenate([v.gain_moe_grad[None], v.router_grad, jnp.zeros((6, width), F32)], 0)
        rest = xor_blocks([rest[:, j * block : (j + 1) * block] for j in range(4)], shard)
        v.notes = []
        for j in range(4):
            piece = jnp.concatenate([gain_attn_grad[None, j * block : (j + 1) * block], rest[j]], 0)
            high = piece.astype(BF16)
            piece = jnp.concatenate([high, (piece - high.astype(F32)).astype(BF16)], 0)
            v.notes.append(jnp.concatenate([d_kv_pre, jnp.pad(piece, ((0, 0), (0, 2 * low - block)))], 0))
        v.notes_y = swap(jnp.concatenate([v.notes[2], v.notes[3]], 0), 0, 2)
        return v.notes[0]

    def notes(token):
        tall = v.notes[0].shape[0]
        v.notes_y, token = together(v.notes_y, token)
        v.notes_core = swap(jnp.concatenate([v.notes[1], v.notes_y[tall:]], 0), 0, 1)
        return token

    def last_grads(token):
        tall = v.notes[0].shape[0]
        core_part = after(v.notes_core, token)
        v.last = key_value_grad(
            mixer_rows, [v.notes[0], core_part[:tall], v.notes_y[:tall], core_part[tall:]], block
        )
        v.last_far = swap(v.last, LAST_BITS[0], 0)
        return v.last

    def last_1(token):
        v.last = plus(v.last, after(v.last_far, token))
        v.last_far = swap(v.last, LAST_BITS[1], 0)
        return v.last

    def last_2(token):
        v.last = plus(v.last, after(v.last_far, token))
        v.last_far = swap(v.last, LAST_BITS[2], 0)
        return v.last

    def last_3(token):
        v.last = v.last.astype(F32) + after(v.last_far, token).astype(F32)
        return v.last

    def query(token):
        return v.query_sum.receive(token)

    def out(token):
        return v.out_sum.receive(token)

    def query_place(token):
        even, odd = v.query_sum.done
        (v.query_grad,) = reorder(where_expert, after(even, token), odd, (width,), QUERY_BITS[0])
        return v.query_grad

    def out_place(token):
        even, odd = v.out_sum.done
        (v.out_w_grad,) = reorder(where_expert, after(even, token), odd, (width,), OUT_BITS[0])
        return v.out_w_grad

    steps = locals()
    token = third
    for name in EVENTS:
        token = steps[name](token)
    layer_out, input_grad, query_grad, out_w_grad = v.layer_out, v.input_grad, v.query_grad, v.out_w_grad
    gate_sum, up_sum, down_sum, last = v.gate_sum, v.up_sum, v.down_sum, v.last
    small_sums = last[block:, :block]
    return (
        layer_out,
        input_grad,
        small_sums[0],
        small_sums[1],
        query_grad,
        last[:block, :low],
        last[:block, low:],
        out_w_grad,
        small_sums[2 : 2 + experts].T,
        gate_sum,
        up_sum,
        down_sum,
    )


def on_device(hidden_in, segment_ids, routes, *rest):
    rows = hidden_in.shape[0]
    experts = rest[6].shape[1]
    capacity = rows * routes.shape[1] * 2 // experts
    shape = (lax.axis_size("expert"), lax.axis_size("shard"))
    if shape == (N_EXPERT, N_SHARD) and experts == N_EXPERT and capacity == rows:
        return on_device_rings(hidden_in, segment_ids, routes, *rest)
    return on_device_routed(hidden_in, segment_ids, routes, *rest)


def solution(mesh):
    placed = (
        P(("expert", "shard"), None),
        P("expert"),
        P(("expert", "shard"), None),
        P("shard"),
        P("shard"),
        P("shard", None),
        P("shard", None),
        P("shard", None),
        P("shard", None),
        P("shard", None),
        P("expert", None, None),
        P("expert", None, None),
        P("expert", None, None),
        P(("expert", "shard"), None),
    )
    return jax.shard_map(
        on_device,
        mesh=mesh,
        in_specs=placed,
        out_specs=(
            P(("expert", "shard"), None),
            P(("expert", "shard"), None),
            P("shard"),
            P("shard"),
            P("shard", None),
            P("shard", None),
            P("shard", None),
            P("shard", None),
            P("shard", None),
            P("expert", None, None),
            P("expert", None, None),
            P("expert", None, None),
        ),
        check_vma=False,
    )
```

```python
import functools
import types

import jax
import jax.numpy as jnp
from jax import lax
from jax.experimental import pallas as pl
from jax.experimental.pallas import tpu as pltpu
from jax.sharding import PartitionSpec as P

HQ = 12
KVH = 2
HEAD = 128


EPSILON = 1e-06
ROPE_BASE = 10000.0
MASKED_SCORE = -1e30
HIGHEST = lax.Precision.HIGHEST


def rope_tables(positions, head_size):
    half_size = head_size // 2
    frequency = ROPE_BASE ** (-(jnp.arange(half_size, dtype=jnp.float32) * 2.0 / head_size))
    angles = positions.astype(jnp.float32)[:, None] * frequency[None, :]
    return (jnp.cos(angles), jnp.sin(angles))


def rotate(values, cosine_table, sine_table, head_size):
    rows_count = values.shape[0]
    shaped = values.reshape(rows_count, -1, head_size)
    half_size = head_size // 2
    first_half = shaped[..., :half_size]
    second_half = shaped[..., half_size:]
    cosine_part = cosine_table[:, None, :]
    sine_part = sine_table[:, None, :]
    turned = jnp.concatenate(
        [
            first_half * cosine_part - second_half * sine_part,
            second_half * cosine_part + first_half * sine_part,
        ],
        -1,
    )
    return turned.reshape(rows_count, -1)


def norm_forward(values, gain):
    factor = lax.rsqrt(jnp.mean(values * values, -1, keepdims=True) + EPSILON)
    unit_rows = values * factor
    return (unit_rows, factor, (unit_rows * gain).astype(jnp.bfloat16))


def norm_backward(grad_rows, unit_rows, factor, gain):
    gain_grad = jnp.sum(grad_rows * unit_rows, 0)
    scaled_grad = grad_rows * gain
    return (
        factor * (scaled_grad - unit_rows * jnp.mean(scaled_grad * unit_rows, -1, keepdims=True)),
        gain_grad,
    )


def score_block(query_heads, key_heads, visible, score_scale):
    raw_scores = jnp.einsum(
        "tkgd,skd->kgts", query_heads, key_heads, preferred_element_type=jnp.float32
    )
    return jnp.where(visible, raw_scores * score_scale, MASKED_SCORE)


def on_device_routed(
    hidden_in,
    segment_ids,
    routes,
    attn_gain,
    moe_gain,
    w_query,
    w_key,
    w_value,
    w_out,
    w_router,
    expert_gate,
    expert_up,
    expert_down,
    out_grad,
):
    tok_rows = hidden_in.shape[0]
    top_count = routes.shape[1]
    experts = w_router.shape[1]
    capacity = tok_rows * top_count * 2 // experts
    groups = HQ // KVH
    score_scale = HEAD ** (-0.5)
    shard_index = lax.axis_index("shard")
    n_expert = lax.axis_size("expert")
    local_experts = expert_gate.shape[0]
    gain_attn, gain_moe, query_w, key_w, value_w, out_w, router_w = (
        lax.all_gather(attn_gain, "shard", axis=0, tiled=True),
        lax.all_gather(moe_gain, "shard", axis=0, tiled=True),
        lax.all_gather(w_query, "shard", axis=0, tiled=True),
        lax.all_gather(w_key, "shard", axis=0, tiled=True),
        lax.all_gather(w_value, "shard", axis=0, tiled=True),
        lax.all_gather(w_out, "shard", axis=0, tiled=True),
        lax.all_gather(w_router, "shard", axis=0, tiled=True),
    )
    gain_attn = gain_attn.astype(jnp.float32)
    gain_moe = gain_moe.astype(jnp.float32)
    inputs = hidden_in.astype(jnp.float32)
    unit_attn, factor_attn, normed = norm_forward(inputs, gain_attn)
    q_pre = jnp.dot(normed, query_w, preferred_element_type=jnp.float32)
    k_pre = jnp.dot(normed, key_w, preferred_element_type=jnp.float32)
    value_rows = jnp.dot(normed, value_w, preferred_element_type=jnp.float32).astype(jnp.bfloat16)
    positions = shard_index * tok_rows + jnp.arange(tok_rows, dtype=jnp.int32)
    cosine_table, sine_table = rope_tables(positions, HEAD)
    queries = rotate(q_pre, cosine_table, sine_table, HEAD).astype(jnp.bfloat16)
    key_local = rotate(k_pre, cosine_table, sine_table, HEAD).astype(jnp.bfloat16)
    key_rows, value_all = (
        lax.all_gather(key_local, "shard", axis=0, tiled=True),
        lax.all_gather(value_rows, "shard", axis=0, tiled=True),
    )
    seq_len = key_rows.shape[0]
    query_heads = queries.reshape(tok_rows, KVH, groups, HEAD)
    key_heads = key_rows.reshape(seq_len, KVH, HEAD)
    value_heads = value_all.reshape(seq_len, KVH, HEAD)
    seg_local = lax.dynamic_slice_in_dim(segment_ids, shard_index * tok_rows, tok_rows)
    visible = (positions[:, None] >= jnp.arange(seq_len, dtype=jnp.int32)[None, :]) & (
        seg_local[:, None] == segment_ids[None, :]
    )
    score_values = score_block(query_heads, key_heads, visible, score_scale)
    top_score = jnp.max(score_values, -1, keepdims=True)
    exponent = jnp.exp(score_values - top_score)
    denominators = jnp.sum(exponent, -1, keepdims=True)
    probabilities = exponent / denominators
    log_total = top_score + jnp.log(denominators)
    attended = (
        jnp.einsum(
            "kgts,skd->tkgd",
            probabilities.astype(jnp.bfloat16),
            value_heads,
            preferred_element_type=jnp.float32,
        )
        .reshape(tok_rows, -1)
        .astype(jnp.bfloat16)
    )
    mid_state = inputs + jnp.dot(attended, out_w, preferred_element_type=jnp.float32)
    unit_moe, factor_moe, normed_moe = norm_forward(mid_state, gain_moe)
    logits = jnp.dot(normed_moe, router_w, preferred_element_type=jnp.float32)
    onehot = (routes[:, :, None] == jnp.arange(experts, dtype=jnp.int32)[None, None, :]).astype(
        jnp.float32
    )
    chosen = jnp.sum(onehot * logits[:, None, :], -1)
    chosen = chosen - jnp.max(chosen, -1, keepdims=True)
    weights = jnp.exp(chosen)
    gate = weights / jnp.sum(weights, -1, keepdims=True)
    flat_routes = routes.reshape(-1)
    route_hot = (flat_routes[:, None] == jnp.arange(experts, dtype=jnp.int32)[None, :]).astype(
        jnp.int32
    )
    before = jnp.cumsum(route_hot, 0, dtype=jnp.int32) - route_hot
    slot_id = flat_routes * capacity + jnp.sum(before * route_hot, 1, dtype=jnp.int32)
    source = (
        jnp.zeros((experts * capacity,), jnp.int32)
        .at[slot_id]
        .set(jnp.arange(tok_rows * top_count, dtype=jnp.int32))
    )
    filled = jnp.zeros((experts * capacity,), jnp.bool_).at[slot_id].set(True)
    outgoing = jnp.where(filled[:, None], jnp.take(normed_moe, source // top_count, axis=0), 0)
    outgoing = outgoing.reshape(experts, capacity, -1)
    arrived = lax.all_to_all(outgoing, "expert", split_axis=0, concat_axis=0, tiled=True)
    item_count = arrived.shape[1]
    shaped = arrived.reshape(n_expert, local_experts, item_count, -1)
    gate_pre = jnp.einsum("nlcd,ldf->nlcf", shaped, expert_gate, preferred_element_type=jnp.float32)
    up_pre = jnp.einsum("nlcd,ldf->nlcf", shaped, expert_up, preferred_element_type=jnp.float32)
    hidden_rows = (gate_pre * jax.nn.sigmoid(gate_pre) * up_pre).astype(jnp.bfloat16)
    result = jnp.einsum(
        "nlcf,lfd->nlcd", hidden_rows, expert_down, preferred_element_type=jnp.float32
    )
    result = result.astype(jnp.bfloat16).reshape(arrived.shape)
    returned = lax.all_to_all(result, "expert", split_axis=0, concat_axis=0, tiled=True)
    outcome = (
        returned,
        arrived,
        gate_pre.reshape(n_expert * local_experts, item_count, -1),
        up_pre.reshape(n_expert * local_experts, item_count, -1),
        hidden_rows.reshape(n_expert * local_experts, item_count, -1),
    )
    returned_rows = jnp.take(outcome[0].reshape(experts * capacity, -1), slot_id, axis=0).reshape(
        tok_rows, top_count, -1
    )
    mixed = mid_state + jnp.sum(gate[:, :, None] * returned_rows, 1)
    layer_out = mixed.astype(jnp.bfloat16)
    grad_out = out_grad.astype(jnp.float32)
    gate_grad = jnp.sum(returned_rows * grad_out[:, None, :], -1)
    gate_slots = jnp.take(gate.reshape(-1), source, axis=0)
    d_send = jnp.where(
        filled[:, None], jnp.take(grad_out, source // top_count, axis=0) * gate_slots[:, None], 0.0
    )
    d_send = d_send.astype(jnp.bfloat16).reshape(experts, capacity, -1)
    d_arrived = lax.all_to_all(d_send, "expert", split_axis=0, concat_axis=0, tiled=True)
    d_shaped = d_arrived.reshape(n_expert, local_experts, capacity, -1)
    arrived_rows = outcome[1].reshape(n_expert, local_experts, capacity, -1)
    gate_pre = outcome[2].reshape(n_expert, local_experts, capacity, -1)
    up_pre = outcome[3].reshape(n_expert, local_experts, capacity, -1)
    hidden_rows = outcome[4].reshape(n_expert, local_experts, capacity, -1)
    sigmoid_gate = jax.nn.sigmoid(gate_pre)
    d_hidden = jnp.einsum(
        "nlcd,lfd->nlcf", d_shaped, expert_down, preferred_element_type=jnp.float32
    )
    down_grad = jnp.einsum(
        "nlcf,nlcd->lfd", hidden_rows, d_shaped, preferred_element_type=jnp.float32
    )
    d_gate = (d_hidden * up_pre * sigmoid_gate * (1.0 + gate_pre * (1.0 - sigmoid_gate))).astype(
        jnp.bfloat16
    )
    d_up = (d_hidden * gate_pre * sigmoid_gate).astype(jnp.bfloat16)
    gate_w_grad = jnp.einsum(
        "nlcd,nlcf->ldf", arrived_rows, d_gate, preferred_element_type=jnp.float32
    )
    up_w_grad = jnp.einsum("nlcd,nlcf->ldf", arrived_rows, d_up, preferred_element_type=jnp.float32)
    d_rows = jnp.einsum("nlcf,ldf->nlcd", d_gate, expert_gate, preferred_element_type=jnp.float32)
    d_rows = d_rows + jnp.einsum(
        "nlcf,ldf->nlcd", d_up, expert_up, preferred_element_type=jnp.float32
    )
    d_rows = d_rows.astype(jnp.bfloat16).reshape(experts, capacity, -1)
    d_returned = lax.all_to_all(d_rows, "expert", split_axis=0, concat_axis=0, tiled=True)
    expert_sums = (
        lax.psum(gate_w_grad.astype(jnp.bfloat16), "shard").astype(jnp.float32),
        lax.psum(up_w_grad.astype(jnp.bfloat16), "shard").astype(jnp.float32),
        lax.psum(down_grad.astype(jnp.bfloat16), "shard").astype(jnp.float32),
    )
    d_copies = jnp.take(d_returned.reshape(experts * capacity, -1), slot_id, axis=0).reshape(
        tok_rows, top_count, -1
    )
    d_normed_moe = jnp.sum(d_copies, 1, dtype=jnp.float32)
    d_chosen = gate * (gate_grad - jnp.sum(gate * gate_grad, -1, keepdims=True))
    d_logits = jnp.sum(onehot * d_chosen[:, :, None], 1)
    router_f32 = router_w.astype(jnp.float32)
    d_normed_moe = d_normed_moe + jnp.dot(d_logits, router_f32.T, precision=HIGHEST)
    router_grad = jnp.dot(normed_moe.astype(jnp.float32).T, d_logits, precision=HIGHEST)
    d_mid_norm, gain_moe_grad = norm_backward(d_normed_moe, unit_moe, factor_moe, gain_moe)
    d_mid = grad_out + d_mid_norm
    d_branch = d_mid.astype(jnp.bfloat16)
    out_w_grad = jnp.dot(attended.T, d_branch, preferred_element_type=jnp.float32)
    d_attended = jnp.dot(d_branch, out_w.T, preferred_element_type=jnp.float32).astype(jnp.bfloat16)
    d_attended = d_attended.reshape(tok_rows, KVH, groups, HEAD)
    score_again = score_block(query_heads, key_heads, visible, score_scale)
    prob_again = jnp.exp(score_again - log_total)
    d_probs = jnp.einsum(
        "tkgd,skd->kgts", d_attended, value_heads, preferred_element_type=jnp.float32
    )
    d_scores = (
        prob_again * (d_probs - jnp.sum(prob_again * d_probs, -1, keepdims=True)) * score_scale
    )
    d_scores = d_scores.astype(jnp.bfloat16)
    d_query = jnp.einsum(
        "kgts,skd->tkgd", d_scores, key_heads, preferred_element_type=jnp.float32
    ).reshape(tok_rows, -1)
    d_key_part = jnp.einsum(
        "kgts,tkgd->skd", d_scores, query_heads, preferred_element_type=jnp.float32
    ).reshape(seq_len, -1)
    d_value_part = jnp.einsum(
        "kgts,tkgd->skd",
        prob_again.astype(jnp.bfloat16),
        d_attended,
        preferred_element_type=jnp.float32,
    ).reshape(seq_len, -1)
    d_keys, d_values = (
        lax.psum_scatter(
            d_key_part.astype(jnp.bfloat16), "shard", scatter_dimension=0, tiled=True
        ).astype(jnp.float32),
        lax.psum_scatter(
            d_value_part.astype(jnp.bfloat16), "shard", scatter_dimension=0, tiled=True
        ).astype(jnp.float32),
    )
    d_q_pre = rotate(d_query, cosine_table, -sine_table, HEAD).astype(jnp.bfloat16)
    d_k_pre = rotate(d_keys, cosine_table, -sine_table, HEAD).astype(jnp.bfloat16)
    d_v_pre = d_values.astype(jnp.bfloat16)
    query_grad = jnp.dot(normed.T, d_q_pre, preferred_element_type=jnp.float32)
    key_grad = jnp.dot(normed.T, d_k_pre, preferred_element_type=jnp.float32)
    value_grad = jnp.dot(normed.T, d_v_pre, preferred_element_type=jnp.float32)
    d_normed = jnp.dot(d_q_pre, query_w.T, preferred_element_type=jnp.float32)
    d_normed = d_normed + jnp.dot(d_k_pre, key_w.T, preferred_element_type=jnp.float32)
    d_normed = d_normed + jnp.dot(d_v_pre, value_w.T, preferred_element_type=jnp.float32)
    d_input_norm, gain_attn_grad = norm_backward(d_normed, unit_attn, factor_attn, gain_attn)
    input_grad = d_mid + d_input_norm
    partial_sums = (
        gain_attn_grad,
        gain_moe_grad,
        query_grad,
        key_grad,
        value_grad,
        out_w_grad,
        router_grad,
    )
    summed = lax.psum(
        (
            partial_sums[0],
            partial_sums[1],
            partial_sums[2],
            partial_sums[3],
            partial_sums[4],
            partial_sums[5],
            partial_sums[6],
        ),
        ("expert", "shard"),
    )
    n_shard = lax.axis_size("shard")
    owned_grads = tuple(
        (
            lax.dynamic_slice_in_dim(
                member, shard_index * (member.shape[0] // n_shard), member.shape[0] // n_shard, 0
            )
            for member in summed
        )
    )
    return (
        layer_out,
        input_grad,
        owned_grads[0],
        owned_grads[1],
        owned_grads[2],
        owned_grads[3],
        owned_grads[4],
        owned_grads[5],
        owned_grads[6],
        expert_sums[0],
        expert_sums[1],
        expert_sums[2],
    )


AXES = ("expert", "shard")
N_EXPERT = 8
N_SHARD = 4
LANES = 128
MEBIBYTE = 1 << 20
BF16 = jnp.bfloat16
F32 = jnp.float32


COST_ATTENTION = 17
COST_IN = 1
COST_DOWN = 20
COST_PLACE = 3
COST_PRODUCTS = 5
OUT_BITS = (1, 2, 4)
QUERY_BITS = (1, 2, 4)
LAST_BITS = (2, 1, 4)
EVENTS = (
    "first_far", "mixed_0", "branch", "attention", "sync_1", "sync_2", "sync_3", "sync_4", "key_value", "norms",
    "out", "first_part", "gate_send", "query", "notes", "down_far", "down_cross", "layer", "out", "last_grads",
    "query", "out", "up_send", "query", "out", "last_1", "gate_total", "down_part", "down_send", "query", "out",
    "last_2", "query", "gate_place", "up_total", "out", "out_place", "query", "query_place", "down_total",
    "up_place", "last_3", "down_place",
)


def cost(microseconds):
    return pl.CostEstimate(flops=microseconds * 10**9, bytes_accessed=10**5, transcendentals=0)


def swap(values, expert_bits, shard_bits):
    pairs = [
        (e * N_SHARD + s, (e ^ expert_bits) * N_SHARD + (s ^ shard_bits))
        for e in range(N_EXPERT)
        for s in range(N_SHARD)
    ]
    return lax.ppermute(values, AXES, pairs)


def next_plane(values):
    pairs = [
        (e * N_SHARD + s, ((e + 2) % N_EXPERT) * N_SHARD + s)
        for e in range(N_EXPERT)
        for s in range(N_SHARD)
    ]
    return lax.ppermute(values, AXES, pairs)


def gather_shards(values):
    other_core = swap(values, 0, 1)
    other_y = swap(values, 0, 2)
    return [values, other_core, other_y, swap(other_y, 0, 1)]


def xor_blocks(blocks, index):
    odd = (index & 1) == 1
    high = (index & 2) == 2
    once = [jnp.where(odd, blocks[j ^ 1], blocks[j]) for j in range(4)]
    return [jnp.where(high, once[j ^ 2], once[j]) for j in range(4)]


def together(*values):
    return lax.optimization_barrier(values)


def after(value, *others):
    return lax.optimization_barrier((value,) + others)[0]


def rejoin(mine, partner, low_first):
    return jnp.where(
        low_first,
        jnp.concatenate([mine, partner], 0),
        jnp.concatenate([partner, mine], 0),
    )


def dot_nn(left, right):
    return lax.dot_general(left, right, (((1,), (0,)), ((), ())), preferred_element_type=F32)


def dot_nt(left, right):
    return lax.dot_general(left, right, (((1,), (1,)), ((), ())), preferred_element_type=F32)


def dot_tn(left, right):
    return lax.dot_general(left, right, (((0,), (0,)), ((), ())), preferred_element_type=F32)


def turn(values, cosine, sine):
    return values * cosine + pltpu.roll(values, HEAD // 2, 1) * sine


def attention_forward_body(
    where_ref, h1_ref, w0, w1, w2, w3, key_ref, value_ref, cos_ref, sin_ref, segq_ref, segk_ref,
    query_out, prob_out, attended_out, bias_ref,
):
    rows, seq_len = bias_ref.shape

    @pl.when(pl.program_id(0) == 0)
    def _():
        base = where_ref[0] * rows
        query_pos = base + lax.broadcasted_iota(jnp.int32, (rows, seq_len), 0)
        key_pos = lax.broadcasted_iota(jnp.int32, (rows, seq_len), 1)
        visible = (query_pos >= key_pos) & (segq_ref[...] == segk_ref[...])
        bias_ref[...] = jnp.where(visible, 0.0, MASKED_SCORE)

    depth = w0.shape[0]
    pre = dot_nn(h1_ref[:, :depth], w0[...])
    for j, weight in enumerate((w1, w2, w3)):
        pre = pre + dot_nn(h1_ref[:, (j + 1) * depth : (j + 2) * depth], weight[...])
    for h in range(pre.shape[1] // HEAD):
        cols = slice(h * HEAD, (h + 1) * HEAD)
        query = turn(pre[:, cols], cos_ref[...], sin_ref[...]).astype(BF16)
        query_out[:, cols] = query
        scores = dot_nt(query, key_ref[...]) * HEAD ** (-0.5) + bias_ref[...]
        exponent = jnp.exp(scores - jnp.max(scores, -1, keepdims=True))
        total = jnp.sum(exponent, -1, keepdims=True)
        probs = (exponent * (1.0 / total)).astype(BF16)
        prob_out[h] = probs
        attended_out[:, cols] = dot_nn(probs, value_ref[...]).astype(BF16)


def attention_forward(where, h1_rel, w_query, keys_values, cosine, sine, seg_query, seg_key):
    rows, width = h1_rel.shape
    seq_len = keys_values.shape[0]
    cols = width // N_SHARD
    heads = cols // HEAD

    def whole(shape):
        return pl.BlockSpec(shape, lambda j, w: (0,) * len(shape))

    weight = pl.BlockSpec((cols, cols), lambda j, w: (0, w[0] ^ j))
    part = pl.BlockSpec((rows, cols), lambda j, w: (0, j))
    return pl.pallas_call(
        attention_forward_body,
        grid_spec=pltpu.PrefetchScalarGridSpec(
            num_scalar_prefetch=1,
            grid=(N_SHARD,),
            in_specs=[
                whole((rows, width)), weight, weight, weight, weight,
                pl.BlockSpec((seq_len, HEAD), lambda j, w: (0, (w[0] ^ j) // 2)),
                pl.BlockSpec((seq_len, HEAD), lambda j, w: (0, KVH + (w[0] ^ j) // 2)),
                whole((rows, HEAD)), whole((rows, HEAD)), whole((rows, 1)), whole((1, seq_len)),
            ],
            out_specs=[part, pl.BlockSpec((heads, rows, seq_len), lambda j, w: (j, 0, 0)), part],
            scratch_shapes=[pltpu.VMEM((rows, seq_len), F32)],
        ),
        out_shape=[
            jax.ShapeDtypeStruct((rows, width), BF16),
            jax.ShapeDtypeStruct((HQ, rows, seq_len), BF16),
            jax.ShapeDtypeStruct((rows, width), BF16),
        ],
        compiler_params=pltpu.CompilerParams(vmem_limit_bytes=28 * MEBIBYTE),
        cost_estimate=cost(15),
        name="attention_forward",
    )(where, h1_rel, *w_query, keys_values, keys_values, cosine, sine, seg_query, seg_key)


def attention_backward_body(
    where_ref, branch_ref, out0, out1, out2, out3, attended_ref, query_ref, prob_ref, key_ref, value_ref,
    w0, w1, w2, w3, cos_ref, sin_ref,
    dq_out, dk_out, dv_out, dh_out, dh_acc, dk_acc, dv_acc, da_ref,
):
    step = pl.program_id(0)
    depth = w0.shape[0]
    rows = branch_ref.shape[0]

    for j, weight in enumerate((out0, out1, out2, out3)):

        @pl.when(step == j)
        def _(weight=weight):
            da_ref[...] = dot_nt(branch_ref[...], weight[...]).astype(BF16)

    @pl.when(step % 2 == 0)
    def _():
        dk_acc[...] = jnp.zeros_like(dk_acc)
        dv_acc[...] = jnp.zeros_like(dv_acc)

    @pl.when(step == 0)
    def _():
        dh_acc[...] = jnp.zeros_like(dh_acc)

    d_pre = []
    for h in range(depth // HEAD):
        cols = slice(h * HEAD, (h + 1) * HEAD)
        d_att = da_ref[:, cols]
        probs = prob_ref[h]
        delta = jnp.sum(d_att.astype(F32) * attended_ref[:, cols].astype(F32), -1, keepdims=True)
        d_probs = dot_nt(d_att, value_ref[...])
        d_scores = (probs.astype(F32) * ((d_probs - delta) * HEAD ** (-0.5))).astype(BF16)
        d_query = dot_nn(d_scores, key_ref[...])
        d_pre.append(turn(d_query, cos_ref[...], -sin_ref[...]).astype(BF16))
        dk_acc[...] += dot_tn(query_ref[:, cols], d_scores)
        dv_acc[...] += dot_tn(d_att, probs)
    d_pre = jnp.concatenate(d_pre, 1)
    dq_out[...] = d_pre
    for j, weight in enumerate((w0, w1, w2, w3)):
        dh_acc[:, j * depth : (j + 1) * depth] += dot_nt(d_pre, weight[...])

    @pl.when(step % 2 == 1)
    def _():
        dk_out[...] = dk_acc[...].T.astype(BF16)
        dv_out[...] = dv_acc[...].T.astype(BF16)

    @pl.when(step == N_SHARD - 1)
    def _():
        dh_out[...] = dh_acc[...]


def attention_backward(where, branch, w_out, attended, queries, probs, keys_values, w_query, cosine, sine):
    rows, width = branch.shape
    seq_len = keys_values.shape[0]
    cols = width // N_SHARD
    heads = cols // HEAD

    def whole(shape):
        return pl.BlockSpec(shape, lambda j, w: (0,) * len(shape))

    weight = pl.BlockSpec((cols, cols), lambda j, w: (0, w[0] ^ j))
    part = pl.BlockSpec((rows, cols), lambda j, w: (0, j))
    head_part = pl.BlockSpec((seq_len, HEAD), lambda j, w: (0, (w[0] ^ j) // 2))
    return pl.pallas_call(
        attention_backward_body,
        grid_spec=pltpu.PrefetchScalarGridSpec(
            num_scalar_prefetch=1,
            grid=(N_SHARD,),
            in_specs=[whole((rows, width))] + [whole((cols, width))] * 4 + [
                part, part, pl.BlockSpec((heads, rows, seq_len), lambda j, w: (j, 0, 0)),
                head_part,
                pl.BlockSpec((seq_len, HEAD), lambda j, w: (0, KVH + (w[0] ^ j) // 2)),
                weight, weight, weight, weight, whole((rows, HEAD)), whole((rows, HEAD)),
            ],
            out_specs=[
                pl.BlockSpec((rows, cols), lambda j, w: (0, w[0] ^ j)),
                head_part, head_part, whole((rows, width)),
            ],
            scratch_shapes=[
                pltpu.VMEM((rows, width), F32),
                pltpu.VMEM((HEAD, seq_len), F32),
                pltpu.VMEM((HEAD, seq_len), F32),
                pltpu.VMEM((rows, cols), BF16),
            ],
        ),
        out_shape=[
            jax.ShapeDtypeStruct((rows, width), BF16),
            jax.ShapeDtypeStruct((seq_len, KVH * HEAD), BF16),
            jax.ShapeDtypeStruct((seq_len, KVH * HEAD), BF16),
            jax.ShapeDtypeStruct((rows, width), F32),
        ],
        compiler_params=pltpu.CompilerParams(vmem_limit_bytes=30 * MEBIBYTE),
        cost_estimate=cost(COST_ATTENTION),
        name="attention_backward",
    )(where, branch, *w_out, attended, queries, probs, keys_values, keys_values, *w_query, cosine, sine)


def expert_body(
    where_ref, h2_ref, dy_ref, router_ref, *refs,
):
    own, far = refs[:6], refs[6:12]
    message_out, mixed_out, da_out, db_out, act_out, gates_ref, dh_acc, y_acc, gg_acc = refs[12:]
    e = pl.program_id(0)
    f = pl.program_id(1)
    rows, width = h2_ref.shape
    half = width // 2
    lane = lax.broadcasted_iota(jnp.int32, (rows, LANES), 1)
    places = [pl.ds(pl.multiple_of((where_ref[1] ^ i) * half, LANES), half) for i in range(2)]

    @pl.when((e == 0) & (f == 0))
    def _():
        named = dy_ref[:, width:].astype(F32) > 0.5
        logits = dot_nt(h2_ref[...], router_ref[...])
        logits = jnp.concatenate([logits, jnp.zeros((rows, LANES - logits.shape[1]), F32)], 1)
        logits = jnp.where(named, logits, MASKED_SCORE)
        top = jnp.max(logits, -1, keepdims=True)
        weights = jnp.where(named, jnp.exp(logits - top), 0.0)
        gates_ref[...] = weights / jnp.sum(weights, -1, keepdims=True)
        dh_acc[...] = jnp.zeros_like(dh_acc)
        y_acc[...] = jnp.zeros_like(y_acc)
        gg_acc[...] = jnp.zeros_like(gg_acc)

    here = lane == (where_ref[0] ^ e)

    def work(members):
        gates, ups, downs = [[members[2 * k + i] for i in range(2)] for k in range(3)]
        gate = jnp.sum(jnp.where(here, gates_ref[...], 0.0), -1, keepdims=True)
        h2 = [h2_ref[:, place] for place in places]
        dy = [dy_ref[:, place] for place in places]
        load = lambda ref: ref[...].reshape(ref.shape[-2:])
        a = dot_nn(h2[0], load(gates[0])) + dot_nn(h2[1], load(gates[1]))
        b = dot_nn(h2[0], load(ups[0])) + dot_nn(h2[1], load(ups[1]))
        d_plain = dot_nt(dy[0], load(downs[0])) + dot_nt(dy[1], load(downs[1]))
        sigmoid = 1.0 / (1.0 + jnp.exp(-a))
        silu = a * sigmoid
        act = silu * b
        gate_grad = jnp.sum(act * d_plain, -1, keepdims=True)
        gg_acc[...] += jnp.where(here, gate_grad, 0.0)
        d_act = d_plain * gate
        d_a = (d_act * b * (sigmoid + silu * (1.0 - sigmoid))).astype(BF16)
        d_b = (d_act * silu).astype(BF16)
        scaled = (act * gate).astype(BF16)
        da_out[...] = d_a
        db_out[...] = d_b
        act_out[...] = scaled
        for i in range(2):
            dh_acc[i] += dot_nt(d_a, load(gates[i])) + dot_nt(d_b, load(ups[i]))
            y_acc[i] += dot_nn(scaled, load(downs[i]))

    @pl.when(e == 0)
    def _():
        work(own)

    @pl.when(e == 1)
    def _():
        work(far)

    @pl.when((e == pl.num_programs(0) - 1) & (f == pl.num_programs(1) - 1))
    def _():
        for i in range(2):
            message_out[:, places[i]] = dh_acc[i].astype(BF16)
            mixed_out[:, places[i]] = y_acc[i].astype(BF16)
        high = gg_acc[...].astype(BF16).astype(F32)
        low = pltpu.roll(gg_acc[...] - high, N_EXPERT, 1)
        message_out[:, width:] = (high + low).astype(BF16)


def expert_block(where, h2, dy_routes, router, own, far):
    rows, width = h2.shape
    hidden = own[0].shape[1]
    half = width // 2
    chunk = 256
    chunks = hidden // chunk

    def whole(shape):
        return pl.BlockSpec(shape, lambda e, f, w: (0,) * len(shape))

    own_step = lambda e, f: jnp.where(e == 0, f, chunks - 1)
    far_step = lambda e, f: jnp.where(e == 0, 0, f)
    own_in = [pl.BlockSpec((half, chunk), lambda e, f, w, i=i: (w[1] ^ i, own_step(e, f))) for i in range(2)]
    own_down = [pl.BlockSpec((chunk, half), lambda e, f, w, i=i: (own_step(e, f), w[1] ^ i)) for i in range(2)]
    far_in = [pl.BlockSpec((1, half, chunk), lambda e, f, w, k=k: (k, 0, far_step(e, f))) for k in range(2)]
    far_down = pl.BlockSpec((1, chunk, half), lambda e, f, w: (2, far_step(e, f), 0))
    part = pl.BlockSpec((rows, chunk), lambda e, f, w: (0, e * chunks + f))
    return pl.pallas_call(
        expert_body,
        grid_spec=pltpu.PrefetchScalarGridSpec(
            num_scalar_prefetch=1,
            grid=(2, chunks),
            in_specs=[whole((rows, width)), whole(dy_routes.shape), whole(router.shape)]
            + own_in + own_in + own_down
            + [far_in[0], far_in[0], far_in[1], far_in[1], far_down, far_down],
            out_specs=[whole((rows, width + LANES)), whole((rows, width)), part, part, part],
            scratch_shapes=[
                pltpu.VMEM((rows, LANES), F32),
                pltpu.VMEM((2, rows, half), F32),
                pltpu.VMEM((2, rows, half), F32),
                pltpu.VMEM((rows, LANES), F32),
            ],
        ),
        out_shape=[
            jax.ShapeDtypeStruct((rows, width + LANES), BF16),
            jax.ShapeDtypeStruct((rows, width), BF16),
            jax.ShapeDtypeStruct((rows, 2 * hidden), BF16),
            jax.ShapeDtypeStruct((rows, 2 * hidden), BF16),
            jax.ShapeDtypeStruct((rows, 2 * hidden), BF16),
        ],
        compiler_params=pltpu.CompilerParams(vmem_limit_bytes=22 * MEBIBYTE),
        cost_estimate=cost(20),
        name="expert_block",
    )(
        where, h2, dy_routes, router, own[0], own[0], own[1], own[1], own[2], own[2],
        far[0], far[1], far[0], far[1], far[0], far[1],
    )


def summed_products_body(where_ref, *refs, parts, sets):
    lefts = refs[:parts]
    rights = refs[parts : parts * (1 + sets)]
    outs = refs[parts * (1 + sets) :]
    for k in range(sets):
        total = dot_tn(lefts[0][...], rights[k * parts][...])
        for j in range(1, parts):
            total = total + dot_tn(lefts[j][...], rights[k * parts + j][...])
        out = outs[k]
        if len(out.shape) == 3:
            pieces = out.shape[0]
            deep = out.shape[1]
            for piece in range(pieces):
                out[where_ref[0] ^ piece] = total[piece * deep : (piece + 1) * deep].astype(out.dtype)
        else:
            out[...] = total.astype(out.dtype)


def summed_products(where, lefts, right_sets, grid, left_spec, right_spec, out_spec, out_shape, name):
    parts = len(lefts)
    sets = len(right_sets)
    return pl.pallas_call(
        functools.partial(summed_products_body, parts=parts, sets=sets),
        grid_spec=pltpu.PrefetchScalarGridSpec(
            num_scalar_prefetch=1,
            grid=grid,
            in_specs=[left_spec] * parts + [right_spec] * (parts * sets),
            out_specs=[out_spec] * sets,
        ),
        out_shape=[jax.ShapeDtypeStruct(out_shape, BF16)] * sets,
        compiler_params=pltpu.CompilerParams(vmem_limit_bytes=24 * MEBIBYTE),
        cost_estimate=cost(COST_PRODUCTS),
        name=name,
    )(where, *lefts, *[member for members in right_sets for member in members])


def in_grads_body(where_ref, *refs):
    h2_refs, da_refs, db_refs = refs[:4], refs[4:8], refs[8:12]
    send_ref, keep_ref, turned_ref = refs[12:]
    rows = h2_refs[0].shape[0]
    half = turned_ref.shape[0] // 2

    @pl.when(pl.program_id(0) == 0)
    def _():
        for j in range(4):
            turned_ref[:, j * rows : (j + 1) * rows] = h2_refs[j][...].T

    for k, member in enumerate((da_refs, db_refs)):
        for out, place in ((send_ref, 1 - where_ref[0]), (keep_ref, where_ref[0])):
            here = pl.ds(pl.multiple_of(place * half, LANES), half)
            total = dot_nn(turned_ref[here, :rows], member[0][...])
            for j in range(1, 4):
                total = total + dot_nn(turned_ref[here, j * rows : (j + 1) * rows], member[j][...])
            out[k] = total.astype(BF16)


def expert_in_grads(where, h2, d_a, d_b):
    rows, width = h2[0].shape
    columns = d_a[0].shape[1]
    chunk = 256
    half = width // 2
    part = pl.BlockSpec((rows, chunk), lambda i, w: (0, i))
    out = pl.BlockSpec((2, half, chunk), lambda i, w: (0, 0, i))
    return pl.pallas_call(
        in_grads_body,
        grid_spec=pltpu.PrefetchScalarGridSpec(
            num_scalar_prefetch=1,
            grid=(columns // chunk,),
            in_specs=[pl.BlockSpec((rows, width), lambda i, w: (0, 0))] * 4 + [part] * 8,
            out_specs=[out] * 2,
            scratch_shapes=[pltpu.VMEM((width, 4 * rows), BF16)],
        ),
        out_shape=[jax.ShapeDtypeStruct((2, half, columns), BF16)] * 2,
        compiler_params=pltpu.CompilerParams(vmem_limit_bytes=24 * MEBIBYTE),
        cost_estimate=cost(COST_IN),
        name="expert_in_grads",
    )(where, *h2, *d_a, *d_b)


def down_grads_body(where_ref, *refs):
    act_refs, send_refs, keep_refs = refs[:4], refs[4:8], refs[8:12]
    turned = [act[...].T for act in act_refs]
    for rights, out in ((send_refs, refs[12]), (keep_refs, refs[13])):
        total = dot_nn(turned[0], rights[0][...])
        for j in range(1, 4):
            total = total + dot_nn(turned[j], rights[j][...])
        out[0] = total.astype(BF16)


def expert_down_grads(where, acts, dy_routes):
    rows, columns = acts[0].shape
    width = dy_routes[0].shape[1] - LANES
    half = width // 2
    hidden = columns // 2
    out = pl.BlockSpec((1, hidden, half), lambda e, w: (e, 0, 0))
    return pl.pallas_call(
        down_grads_body,
        grid_spec=pltpu.PrefetchScalarGridSpec(
            num_scalar_prefetch=1,
            grid=(2,),
            in_specs=[pl.BlockSpec((rows, hidden), lambda e, w: (0, e))] * 4
            + [pl.BlockSpec((rows, half), lambda e, w: (0, 1 - w[0]))] * 4
            + [pl.BlockSpec((rows, half), lambda e, w: (0, w[0]))] * 4,
            out_specs=[out, out],
        ),
        out_shape=[jax.ShapeDtypeStruct((2, hidden, half), BF16)] * 2,
        compiler_params=pltpu.CompilerParams(vmem_limit_bytes=22 * MEBIBYTE),
        cost_estimate=cost(COST_DOWN),
        name="expert_down_grads",
    )(where, *acts, *dy_routes, *dy_routes)


class PlaneSum:
    def __init__(self, pieces, order):
        self.shape = pieces.shape[1:]
        self.order = order
        self.axes = [4, 2, 1]
        self.kept = pieces.reshape((2, 2, 2) + self.shape)
        self.step = 0
        self.send()

    def send(self):
        if self.step < 3:
            at = self.axes.index(self.order[self.step])
            self.mine = lax.index_in_dim(self.kept, 0, at, keepdims=False)
            other = lax.index_in_dim(self.kept, 1, at, keepdims=False)
            self.received = swap(other, self.order[self.step], 0)
        else:
            self.received = swap(self.kept, self.order[5 - self.step], 0)

    def receive(self, token):
        received = after(self.received, token)
        if self.step < 3:
            self.kept = (self.mine.astype(F32) + received.astype(F32)).astype(BF16)
            self.axes.remove(self.order[self.step])
        else:
            bit = self.order[5 - self.step]
            if self.step == 5:
                self.done = (self.kept.reshape((4,) + self.shape), received.reshape((4,) + self.shape))
                return received
            at = sum(1 for b in self.axes if b > bit)
            self.kept = jnp.stack([self.kept, received], at)
            self.axes = sorted(self.axes + [bit], reverse=True)
        self.step += 1
        self.send()
        return self.kept


def reorder_body(where_ref, even_ref, odd_ref, out_ref, *, first):
    for b in range(N_EXPERT):
        place = where_ref[0] ^ b
        low = place % first
        index = (place // (2 * first)) * first + low
        odd = (place // first) % 2

        @pl.when(odd == 0)
        def _(b=b, index=index):
            out_ref[b] = even_ref[index].astype(F32)

        @pl.when(odd == 1)
        def _(b=b, index=index):
            out_ref[b] = odd_ref[index].astype(F32)


def reorder(where, even, odd, columns, first):
    deep, width = even.shape[1:]
    results = []
    begin = 0
    for count in columns:
        wide = min(count, 512)
        start = begin // wide
        spec = pl.BlockSpec((N_EXPERT // 2, deep, wide), lambda i, w, start=start: (0, 0, start + i))
        results.append(
            pl.pallas_call(
                functools.partial(reorder_body, first=first),
                grid_spec=pltpu.PrefetchScalarGridSpec(
                    num_scalar_prefetch=1,
                    grid=(count // wide,),
                    in_specs=[spec, spec],
                    out_specs=pl.BlockSpec((N_EXPERT, deep, wide), lambda i, w: (0, 0, i)),
                ),
                out_shape=jax.ShapeDtypeStruct((N_EXPERT, deep, count), F32),
                cost_estimate=cost(COST_PLACE),
                name="reorder",
            )(where, even, odd).reshape(N_EXPERT * deep, count)
        )
        begin += count
    return results


def key_value_grad_body(*refs):
    lefts, rights, out_ref = refs[:4], refs[4:8], refs[8]
    rows, block = lefts[0].shape
    total = dot_tn(lefts[0][...], rights[0][:rows])
    small = rights[0][rows:, :block].astype(F32)
    for j in range(1, 4):
        total = total + dot_tn(lefts[j][...], rights[j][:rows])
        small = small + rights[j][rows:, :block].astype(F32)
    few = small.shape[0] // 2
    out_ref[:block] = total.astype(BF16)
    out_ref[block:, :block] = (small[:few] + small[few:]).astype(BF16)
    out_ref[block:, block:] = jnp.zeros_like(out_ref[block:, block:])


def key_value_grad(lefts, rights, block):
    rows = lefts[0].shape[0]
    columns = rights[0].shape[1]
    few = (rights[0].shape[0] - rows) // 2
    whole = lambda shape: pl.BlockSpec(shape, lambda i: (0, 0))
    return pl.pallas_call(
        key_value_grad_body,
        grid=(1,),
        in_specs=[whole((rows, block))] * 4 + [whole(rights[0].shape)] * 4,
        out_specs=whole((block + few, columns)),
        out_shape=jax.ShapeDtypeStruct((block + few, columns), BF16),
        cost_estimate=cost(COST_PRODUCTS),
        name="key_value_grad",
    )(*lefts, *rights)


def place_body(where_ref, mine_ref, partner_ref, out_ref):
    @pl.when(pl.program_id(0) == 0)
    def _():
        out_ref[...] = mine_ref[0].astype(out_ref.dtype)

    @pl.when(pl.program_id(0) == 1)
    def _():
        out_ref[...] = partner_ref[0].astype(out_ref.dtype)


def place_halves(where, mine, partner, member, by_rows):
    tall, wide = mine.shape[1:]
    cuts = 1
    deep = tall // cuts

    def mine_map(h, i, w):
        return (member, jnp.where(h == 0, i, cuts - 1), 0)

    def partner_map(h, i, w):
        return (member, jnp.where(h == 0, 0, i), 0)

    def out_map(h, i, w):
        return ((w[0] ^ h) * cuts + i, 0) if by_rows else (i, w[0] ^ h)

    return pl.pallas_call(
        place_body,
        grid_spec=pltpu.PrefetchScalarGridSpec(
            num_scalar_prefetch=1,
            grid=(2, cuts),
            in_specs=[pl.BlockSpec((1, deep, wide), mine_map), pl.BlockSpec((1, deep, wide), partner_map)],
            out_specs=pl.BlockSpec((deep, wide), out_map),
        ),
        out_shape=jax.ShapeDtypeStruct((2 * tall, wide) if by_rows else (tall, 2 * wide), F32),
        compiler_params=pltpu.CompilerParams(vmem_limit_bytes=24 * MEBIBYTE),
        cost_estimate=cost(COST_PLACE),
        name="place_halves",
    )(where, mine, partner)


def far_halves_body(where_ref, *refs):
    out_ref = refs[-1]
    for k, ref in enumerate(refs[:-1]):

        @pl.when(pl.program_id(0) == k)
        def _(ref=ref):
            out_ref[0] = ref[...]


def far_halves(where, own):
    hidden = own[0].shape[1]
    half = own[0].shape[0] // 2
    cuts = 1
    tall = half // cuts

    def in_map(k):
        step = lambda i, r: jnp.where(i < k, 0, jnp.where(i == k, r, cuts - 1))
        if k == 2:
            return lambda i, r, w: (step(i, r), w[0])
        return lambda i, r, w: (w[0] * cuts + step(i, r), 0)

    return pl.pallas_call(
        far_halves_body,
        grid_spec=pltpu.PrefetchScalarGridSpec(
            num_scalar_prefetch=1,
            grid=(3, cuts),
            in_specs=[pl.BlockSpec((tall, hidden), in_map(k)) for k in range(3)],
            out_specs=pl.BlockSpec((1, tall, hidden), lambda i, r, w: (i, r, 0)),
        ),
        out_shape=jax.ShapeDtypeStruct((3, half, hidden), BF16),
        cost_estimate=cost(3),
        name="far_halves",
    )(where, *own)


def pack_body(key_ref, value_ref, small_ref, out_ref):
    rows, low = key_ref.shape
    out_ref[:rows, :low] = key_ref[...]
    out_ref[:rows, low:] = value_ref[...]
    out_ref[rows:, : small_ref.shape[1]] = small_ref[...]
    out_ref[rows:, small_ref.shape[1] :] = jnp.zeros_like(out_ref[rows:, small_ref.shape[1] :])


def pack(w_key, w_value, small):
    rows, low = w_key.shape
    return pl.pallas_call(
        pack_body,
        out_shape=jax.ShapeDtypeStruct((rows + small.shape[0], 2 * low), BF16),
        cost_estimate=cost(2),
        name="pack",
    )(w_key, w_value, small)


def plus(part, received):
    return (part.astype(F32) + received.astype(F32)).astype(BF16)


def on_device_rings(
    hidden_in, segment_ids, routes, attn_gain, moe_gain, w_query, w_key, w_value, w_out, w_router,
    expert_gate, expert_up, expert_down, out_grad,
):
    rows, width = hidden_in.shape
    experts = w_router.shape[1]
    shard = lax.axis_index("shard")
    expert = lax.axis_index("expert")
    core = shard % 2
    where_shard = shard.astype(jnp.int32)[None]
    where_expert = expert.astype(jnp.int32)[None]
    where_core = core.astype(jnp.int32)[None]
    where_far_core = 1 - where_core
    block = width // N_SHARD
    low = KVH * HEAD

    own = (expert_gate[0], expert_up[0], expert_down[0])
    far_send = far_halves(where_core, own)
    far_part = swap(far_send, 1, 0)
    small = jnp.concatenate(
        [w_router.T, attn_gain[None], moe_gain[None], jnp.zeros((6, block), BF16)], 0
    )
    packed_own = pack(after(w_key, far_send), w_value, small)
    packed_y = swap(packed_own, 0, 2)
    mask = (routes[:, :, None] == jnp.arange(LANES, dtype=jnp.int32)[None, None, :]).any(1)
    dy_routes = [jnp.concatenate([out_grad, mask.astype(BF16)], 1)]
    for _ in range(3):
        dy_routes.append(next_plane(dy_routes[-1]))
    query_w_core = swap(w_query, 0, 1)
    out_w_core = swap(w_out, 0, 1)
    query_w_y = swap(after(w_query, packed_y), 0, 2)
    packed_pair = swap(jnp.concatenate([packed_own, packed_y], 0), 0, 1)
    tall = packed_own.shape[0]
    packed = [packed_own, packed_pair[:tall], packed_y, packed_pair[tall:]]

    inputs = hidden_in.astype(F32)
    factor_attn = lax.rsqrt(jnp.mean(inputs * inputs, -1, keepdims=True) + EPSILON)
    unit_rel = jnp.concatenate(
        xor_blocks([inputs[:, j * block : (j + 1) * block] for j in range(4)], shard), 1
    ) * factor_attn
    gain_rel = jnp.concatenate([member[block + experts : block + experts + 1, :block] for member in packed], 1)
    gain_rel = gain_rel.astype(F32)
    h1_rel = after((unit_rel * gain_rel).astype(BF16), query_w_core, out_w_core)
    key_value_w = [member[:block] for member in packed]
    pre = sum(dot_nn(h1_rel[:, j * block : (j + 1) * block], key_value_w[j]) for j in range(4))
    positions = shard * rows + jnp.arange(rows, dtype=jnp.int32)
    cosine, sine = rope_tables(positions, HEAD)
    key_local = rotate(pre[:, :low], cosine, sine, HEAD)
    key_value = jnp.concatenate([key_local, pre[:, low:]], 1).astype(BF16)
    key_value = after(key_value, dy_routes[1])
    key_value_y = swap(key_value, 0, 2)
    query_w = [w_query, query_w_core, query_w_y, swap(query_w_y, 0, 1)]
    key_value_pair = swap(jnp.concatenate([key_value, key_value_y], 0), 0, 1)
    keys_values = jnp.concatenate(
        xor_blocks([key_value, key_value_pair[:rows], key_value_y, key_value_pair[rows:]], shard), 0
    )
    out_w_y = swap(after(w_out, query_w_y, key_value), 0, 2)
    cosine_row = jnp.concatenate([cosine, cosine], 1)
    sine_row = jnp.concatenate([-sine, sine], 1)
    seg_query = lax.dynamic_slice_in_dim(segment_ids, shard * rows, rows)[:, None]
    queries, probs, attended = attention_forward(
        where_shard, after(h1_rel, dy_routes[2]), query_w, keys_values, cosine_row, sine_row, seg_query, segment_ids[None, :]
    )
    attended_late = after(attended, dy_routes[3])
    out_w_y = after(out_w_y, attended)
    out_w = [w_out, out_w_core, out_w_y, swap(out_w_y, 0, 1)]
    mid_state = inputs + sum(
        dot_nn(attended_late[:, j * block : (j + 1) * block], out_w[j]) for j in range(4)
    )
    factor_moe = lax.rsqrt(jnp.mean(mid_state * mid_state, -1, keepdims=True) + EPSILON)
    unit_moe = mid_state * factor_moe
    small_true = jnp.concatenate(xor_blocks([member[block:, :block] for member in packed], shard), 1)
    gain_moe = small_true[experts + 1 : experts + 2].astype(F32)
    router = small_true[:experts].astype(F32)
    h2 = [(unit_moe * gain_moe).astype(BF16)]

    far_part = after(far_part, attended)
    far_other = swap(far_part, 0, 1)
    hidden = own[0].shape[1]
    deep = width // 2
    far = (far_part, far_other)
    where_pair = jnp.stack([expert, core]).astype(jnp.int32)

    mixer_rows = [
        jnp.concatenate([h1_rel[:, j * block : (j + 1) * block], attended[:, j * block : (j + 1) * block]], 1)
        for j in range(4)
    ]
    mixer_rows = [mixer_rows[0]] + [swap(mixer_rows[j], 0, j) for j in (1, 2, 3)]
    add = lambda a, b: (a.astype(F32) + b.astype(F32)).astype(BF16)
    block_of = lambda j, *ready: expert_block(
        where_pair, after(h2[j], *ready), dy_routes[j], small_true, own, far
    )
    h2.append(next_plane(h2[0]))
    done = [block_of(0)]
    h2.append(next_plane(after(h2[1], done[0][0])))
    done.append(block_of(1, done[0][0], *mixer_rows))
    h2[2] = after(h2[2], done[1][0])
    h2.append(next_plane(h2[2]))
    message = next_plane(after(done[1][0], h2[2]))
    done.append(block_of(2, done[1][0]))
    done.append(block_of(3, done[2][0]))
    second = add(done[2][0], after(message, done[3][0]))
    message = next_plane(second)

    acts = [done[j][4] for j in range(4)]
    in_send, in_keep = expert_in_grads(
        after(where_core, second), h2, [done[j][2] for j in range(4)], [done[j][3] for j in range(4)]
    )
    third = add(done[3][0], after(message, in_send))
    message = next_plane(third)
    v = types.SimpleNamespace(in_swap=swap(after(in_send, third), 0, 1))

    def mixer_grads(half, rights, name):
        n = rights[0].shape[1]
        (pieces,) = summed_products(
            where_expert, mixer_rows, [rights], (n // 512,),
            pl.BlockSpec((rows, block), lambda i, w: (0, half)),
            pl.BlockSpec((rows, 512), lambda i, w: (0, i)),
            pl.BlockSpec((N_EXPERT, block // N_EXPERT, 512), lambda i, w: (0, 0, i)),
            (N_EXPERT, block // N_EXPERT, n), name,
        )
        return pieces


    def first_far(token):
        v.in_swap, token = together(v.in_swap, token)
        far = jnp.stack([plus(in_keep[k, :, hidden:], v.in_swap[k, :, hidden:]) for k in range(2)])
        v.first_received = swap(far, 1, 0)
        return far

    def down_far(token):
        v.down_swap = after(v.down_swap, token)
        v.down_far = plus(v.down_keep[1], v.down_swap[1])
        return v.down_far

    def down_cross(token):
        v.down_received = swap(after(v.down_far, token), 1, 0)
        return token

    def branch(token):
        total = done[0][0].astype(F32) + after(message, token).astype(F32)
        named = mask[:, :experts]
        logits = jnp.where(named, dot_nt(h2[0], small_true[:experts]), MASKED_SCORE)
        weights = jnp.where(named, jnp.exp(logits - jnp.max(logits, -1, keepdims=True)), 0.0)
        gate = weights / jnp.sum(weights, -1, keepdims=True)
        gate_grad = total[:, width : width + experts] + total[:, width + experts : width + 2 * experts]
        d_logits = gate * (gate_grad - jnp.sum(gate * gate_grad, -1, keepdims=True))
        d_h2 = total[:, :width] + jnp.dot(d_logits, router, precision=HIGHEST)
        v.router_grad = jnp.dot(d_logits.T, h2[0].astype(F32), precision=HIGHEST)
        d_mid_norm, v.gain_moe_grad = norm_backward(d_h2, unit_moe, factor_moe, gain_moe)
        v.d_mid = out_grad.astype(F32) + d_mid_norm
        v.d_branch = v.d_mid.astype(BF16)
        v.branch_core = swap(v.d_branch, 0, 1)
        v.branch_y = swap(v.d_branch, 0, 2)
        return v.d_branch

    def mixed_0(token):
        v.mixed = next_plane(after(done[1][1], token))
        return token

    def attention(token):
        v.d_q_pre, v.d_key_part, v.d_value_part, v.d_normed = attention_backward(
            where_shard, after(v.d_branch, token), out_w, attended, queries, probs, keys_values, query_w,
            cosine_row, sine_row,
        )
        return v.d_q_pre

    def sync_1(token):
        v.d_q_pre, v.d_key_part, v.d_value_part, v.branch_y, v.branch_core, v.mixed = together(
            v.d_q_pre, v.d_key_part, v.d_value_part, v.branch_y, v.branch_core, v.mixed
        )
        v.d_q_y = swap(v.d_q_pre, 0, 2)
        v.d_q_core = swap(v.d_q_pre, 0, 1)
        v.branch_far = swap(v.branch_y, 0, 1)
        d_parts = jnp.concatenate([v.d_key_part, v.d_value_part], 1).reshape(N_SHARD, rows, 2 * low)
        v.d_rel = xor_blocks([d_parts[j] for j in range(4)], shard)
        v.from_core = swap(jnp.stack([v.d_rel[1], v.d_rel[3]]), 0, 1)
        v.mixed = add(done[2][1], v.mixed)
        return v.d_q_pre

    def sync_2(token):
        v.d_q_core, v.branch_far, v.from_core, v.mixed = together(
            v.d_q_core, v.branch_far, v.from_core, v.mixed
        )
        v.mixed = next_plane(v.mixed)
        d_far = add(v.d_rel[2], v.from_core[1])
        v.d_far_y = swap(d_far, 0, 2)
        rights = [v.d_branch, v.branch_core, v.branch_y, after(v.branch_far, d_far)]
        v.out_pieces = mixer_grads(1, rights, "w_out_grad")
        down_send, v.down_keep = expert_down_grads(after(where_core, v.out_pieces), acts, dy_routes)
        v.down_swap = swap(down_send, 0, 1)
        return down_send

    def sync_3(token):
        v.d_q_y, v.out_pieces, v.mixed, v.down_keep, token = together(
            v.d_q_y, v.out_pieces, v.mixed, v.down_keep, token
        )
        v.out_sum = PlaneSum(v.out_pieces, OUT_BITS)
        v.mixed = next_plane(add(done[3][1], v.mixed))
        rights = [v.d_q_pre, v.d_q_core, v.d_q_y, swap(v.d_q_y, 0, 1)]
        v.query_pieces = mixer_grads(0, rights, "w_query_grad")
        return v.query_pieces

    def sync_4(token):
        v.query_pieces, v.d_far_y, token = together(v.query_pieces, v.d_far_y, token)
        v.query_sum = PlaneSum(v.query_pieces, QUERY_BITS)
        return v.query_pieces

    def first_part(token):
        received = after(v.first_received, token)
        parts = [
            in_keep[k, :, :hidden].astype(F32) + v.in_swap[k, :, :hidden].astype(F32) + received[k].astype(F32)
            for k in range(2)
        ]
        v.gate_part, v.up_part = together(*[part.astype(BF16) for part in parts])
        return v.gate_part

    def down_send(token):
        v.down_y = swap(after(v.down_part, token), 0, 2)
        return token

    def up_send(token):
        v.up_y = swap(after(v.up_part, token), 0, 2)
        return token

    def gate_send(token):
        v.gate_y = swap(after(v.gate_part, token), 0, 2)
        return token

    def down_total(token):
        v.down_total = plus(v.down_part, after(v.down_y, token))
        v.down_core = swap(v.down_total, 0, 1)
        return v.down_total

    def gate_total(token):
        v.gate_total = plus(v.gate_part, after(v.gate_y, token))
        v.gate_core = swap(v.gate_total, 0, 1)
        return v.gate_total

    def layer(token):
        mixed = after(v.mixed, token).astype(F32)
        v.layer_out = (mid_state + done[0][1].astype(F32) + mixed).astype(BF16)
        return v.layer_out

    def down_part(token):
        own_part = v.down_keep[0].astype(F32) + v.down_swap[0].astype(F32)
        v.down_part = plus(own_part, after(v.down_received, token))
        return v.down_part

    def up_total(token):
        v.up_total = plus(v.up_part, after(v.up_y, token))
        v.up_core = swap(v.up_total, 0, 1)
        return v.up_total

    def down_place(token):
        v.down_sum = place_halves(where_core, v.down_total[None], after(v.down_core, token)[None], 0, False)[None]
        return v.down_sum

    def gate_place(token):
        v.gate_sum = place_halves(where_core, v.gate_total[None], after(v.gate_core, token)[None], 0, True)[None]
        return v.gate_sum

    def up_place(token):
        v.up_sum = place_halves(where_core, v.up_total[None], after(v.up_core, token)[None], 0, True)[None]
        return v.up_sum

    def key_value(token):
        d_key_value = v.d_rel[0].astype(F32) + v.from_core[0].astype(F32) + after(v.d_far_y, token).astype(F32)
        d_k_pre = rotate(d_key_value[:, :low], cosine, -sine, HEAD)
        v.d_kv_pre = jnp.concatenate([d_k_pre, d_key_value[:, low:]], 1).astype(BF16)
        return v.d_kv_pre

    def norms(token):
        d_kv_pre = after(v.d_kv_pre, token)
        d_normed = v.d_normed + jnp.concatenate([dot_nt(d_kv_pre, member) for member in key_value_w], 1)
        d_input_norm, gain_attn_grad = norm_backward(d_normed, unit_rel, factor_attn, gain_rel)
        d_input_norm = jnp.concatenate(
            xor_blocks([d_input_norm[:, j * block : (j + 1) * block] for j in range(4)], shard), 1
        )
        v.input_grad = v.d_mid + d_input_norm
        rest = jnp.concatenate([v.gain_moe_grad[None], v.router_grad, jnp.zeros((6, width), F32)], 0)
        rest = xor_blocks([rest[:, j * block : (j + 1) * block] for j in range(4)], shard)
        v.notes = []
        for j in range(4):
            piece = jnp.concatenate([gain_attn_grad[None, j * block : (j + 1) * block], rest[j]], 0)
            high = piece.astype(BF16)
            piece = jnp.concatenate([high, (piece - high.astype(F32)).astype(BF16)], 0)
            v.notes.append(jnp.concatenate([d_kv_pre, jnp.pad(piece, ((0, 0), (0, 2 * low - block)))], 0))
        v.notes_y = swap(jnp.concatenate([v.notes[2], v.notes[3]], 0), 0, 2)
        return v.notes[0]

    def notes(token):
        tall = v.notes[0].shape[0]
        v.notes_y, token = together(v.notes_y, token)
        v.notes_core = swap(jnp.concatenate([v.notes[1], v.notes_y[tall:]], 0), 0, 1)
        return token

    def last_grads(token):
        tall = v.notes[0].shape[0]
        core_part = after(v.notes_core, token)
        v.last = key_value_grad(
            mixer_rows, [v.notes[0], core_part[:tall], v.notes_y[:tall], core_part[tall:]], block
        )
        v.last_far = swap(v.last, LAST_BITS[0], 0)
        return v.last

    def last_1(token):
        v.last = plus(v.last, after(v.last_far, token))
        v.last_far = swap(v.last, LAST_BITS[1], 0)
        return v.last

    def last_2(token):
        v.last = plus(v.last, after(v.last_far, token))
        v.last_far = swap(v.last, LAST_BITS[2], 0)
        return v.last

    def last_3(token):
        v.last = v.last.astype(F32) + after(v.last_far, token).astype(F32)
        return v.last

    def query(token):
        return v.query_sum.receive(token)

    def out(token):
        return v.out_sum.receive(token)

    def query_place(token):
        even, odd = v.query_sum.done
        (v.query_grad,) = reorder(where_expert, after(even, token), odd, (width,), QUERY_BITS[0])
        return v.query_grad

    def out_place(token):
        even, odd = v.out_sum.done
        (v.out_w_grad,) = reorder(where_expert, after(even, token), odd, (width,), OUT_BITS[0])
        return v.out_w_grad

    steps = locals()
    token = third
    for name in EVENTS:
        token = steps[name](token)
    layer_out, input_grad, query_grad, out_w_grad = v.layer_out, v.input_grad, v.query_grad, v.out_w_grad
    gate_sum, up_sum, down_sum, last = v.gate_sum, v.up_sum, v.down_sum, v.last
    small_sums = last[block:, :block]
    return (
        layer_out,
        input_grad,
        small_sums[0],
        small_sums[1],
        query_grad,
        last[:block, :low],
        last[:block, low:],
        out_w_grad,
        small_sums[2 : 2 + experts].T,
        gate_sum,
        up_sum,
        down_sum,
    )


def on_device(hidden_in, segment_ids, routes, *rest):
    rows = hidden_in.shape[0]
    experts = rest[6].shape[1]
    capacity = rows * routes.shape[1] * 2 // experts
    shape = (lax.axis_size("expert"), lax.axis_size("shard"))
    if shape == (N_EXPERT, N_SHARD) and experts == N_EXPERT and capacity == rows:
        return on_device_rings(hidden_in, segment_ids, routes, *rest)
    return on_device_routed(hidden_in, segment_ids, routes, *rest)


def solution(mesh):
    placed = (
        P(("expert", "shard"), None),
        P("expert"),
        P(("expert", "shard"), None),
        P("shard"),
        P("shard"),
        P("shard", None),
        P("shard", None),
        P("shard", None),
        P("shard", None),
        P("shard", None),
        P("expert", None, None),
        P("expert", None, None),
        P("expert", None, None),
        P(("expert", "shard"), None),
    )
    return jax.shard_map(
        on_device,
        mesh=mesh,
        in_specs=placed,
        out_specs=(
            P(("expert", "shard"), None),
            P(("expert", "shard"), None),
            P("shard"),
            P("shard"),
            P("shard", None),
            P("shard", None),
            P("shard", None),
            P("shard", None),
            P("shard", None),
            P("expert", None, None),
            P("expert", None, None),
            P("expert", None, None),
        ),
        check_vma=False,
    )
```
